32 devices in a mesh: ha: 2 (over x), wa: 4 (over y, core), ba: 4 (over z).
Axes of the slice: x: 2, y: 2, z: 4, core: 2. Of those that a mesh axis runs over, the one named last changes fastest.
Arguments:
- images: bfloat16 [128, 8, 8, 512], P(('ha', 'wa', 'ba')), may hold values from -6 to 6
- valid_masks: int32 [128, 8, 8], P(('ha', 'wa', 'ba')), may hold values from 0 to 1, as said below
- cotangent: bfloat16 [128, 8, 8, 512], P(('ha', 'wa', 'ba')), may hold values from -6 to 6
- conv_weights: float32 [2, 9, 512, 512], P(None, None, ('ha', 'wa'), 'ba'), may hold values from -0.09375 to 0.09375
- conv_first: float32 [2, 9, 512, 512], P(None, None, ('ha', 'wa'), 'ba'), as said below
- conv_second: float32 [2, 9, 512, 512], P(None, None, ('ha', 'wa'), 'ba'), as said below
- norm_params: float32 [4, 512], replicated, may hold values from 0.3 to 1.3
- norm_first: float32 [4, 512], replicated, may hold values from -117.66257 to 117.66257
- norm_second: float32 [4, 512], replicated, may hold values from 819.2 to 3276.8
Outputs:
- block_output: bfloat16 [128, 8, 8, 512], P(('ha', 'wa', 'ba'))
- input_grad: bfloat16 [128, 8, 8, 512], P(('ha', 'wa', 'ba'))
- new_weights: float32 [2, 9, 512, 512], P(None, None, ('ha', 'wa'), 'ba')
- weight_copies: bfloat16 [2, 9, 512, 512], P(None, None, ('ha', 'wa'), 'ba')
- conv_first_new: float32 [2, 9, 512, 512], P(None, None, ('ha', 'wa'), 'ba')
- conv_second_new: float32 [2, 9, 512, 512], P(None, None, ('ha', 'wa'), 'ba')
- new_norm_params: float32 [4, 512], replicated
- norm_first_new: float32 [4, 512], replicated
- norm_second_new: float32 [4, 512], replicated
- trust_norms: float32 [2, 6], replicated
The draws below stay inside these ranges and needn't reach their ends.
Inputs may be any that keep to these rules, and one draw needn't show every extreme that they name: `valid_masks`: each image's valid pixels form a top-left rectangle of 1 to 8 rows and 1 to 8 columns; image 0 is whole. `conv_first`: of both signs, of the size of the kernels' gradients. `conv_second`: Positive, of the size of the squared kernels' gradients.
All inputs are finite; a program needn't handle non-finite values.
Results may differ from the reference program's by a relative error of at most 0.0039.
The reference program's roundings to bfloat16 on the way count: a program that leaves them out, or rounds other values in their place, can miss the bound.
Values may be sent and summed in bfloat16 or wider, within the bound.
No kernel may reach another device: no remote copies, remote signals or barrier semaphores. Data moves between devices by JAX's collectives and lax.ppermute only.
A program may use at most 128 MiB of HBM per device.

```python
import math
import jax
import jax.numpy as jnp
from jax import lax

C = 512
KK = 9
H = 8
W = 8
STEP = 3
IMAGES = 128


def draw_valid_masks(key, part):
    key_rows, key_cols = jax.random.split(key)
    heights = jax.random.randint(key_rows, (IMAGES,), 1, H + 1)
    widths = jax.random.randint(key_cols, (IMAGES,), 1, W + 1)
    leading = jnp.arange(IMAGES) == 0
    heights = jnp.where(leading, H, heights)
    widths = jnp.where(leading, W, widths)
    row_index = jnp.arange(H)
    col_index = jnp.arange(W)
    inside = (row_index[None, :, None] < heights[:, None, None]) & (col_index[None, None, :] < widths[:, None, None])
    return inside.astype(jnp.int32)


def kernel_scale():
    root_pixels = jnp.sqrt(jnp.float32(IMAGES * H * W))
    return jnp.array([0.24, 0.62], jnp.float32).reshape(2, 1, 1, 1) * root_pixels


def draw_conv_first(key, part):
    key = jax.random.fold_in(key, 12)
    values = jax.random.normal(key, (2, KK, C, C), jnp.float32)
    return jnp.clip(values, -4.0, 4.0) * kernel_scale()


def draw_conv_second(key, part):
    key = jax.random.fold_in(key, 11)
    exponent = jax.random.uniform(key, (2, KK, C, C), jnp.float32, 0.0, jnp.log(4.0))
    scale = kernel_scale()
    return jnp.exp(exponent) * scale * scale


def level_of(stream_key, extent, cuts, smallest, high):
    gain, own = 1.0, jax.random.fold_in(stream_key, 6)
    for axis_at, parts in cuts:
        steps = jnp.exp(jax.random.uniform(jax.random.fold_in(own, axis_at), (parts,), jnp.float32, smallest / len(cuts), high / len(cuts)))
        gain = gain * jnp.repeat(steps, extent[axis_at] // parts).reshape([-1 if axis == axis_at else 1 for axis in range(len(extent))])
    return gain


def noise(own_key, shape, deviation, limit, shards=(), held_as=jnp.bfloat16):
    gain = level_of(own_key, shape, shards, -0.22, 0.18) if shards else 1.0
    entries = jax.random.normal(own_key, shape, jnp.float32) * deviation * gain
    return jnp.minimum(jnp.maximum(entries, -limit), limit).astype(held_as)


def setup_inputs(seed: int = 0) -> dict:
    streams_of = jax.random.split(jax.random.key(seed), 10)
    images = noise(streams_of[0], (IMAGES, H, W, C), 1.0, 6.0, ((0, 32),))
    valid_masks = draw_valid_masks(jax.random.fold_in(streams_of[9], 71), 0)
    cotangent = noise(streams_of[2], (IMAGES, H, W, C), 1.0, 6.0, ((0, 32),))
    conv_weights = noise(streams_of[3], (2, KK, C, C), (KK * C) ** -0.5, 0.09375, ((2, 8), (3, 4)), jnp.float32)
    conv_first = draw_conv_first(jax.random.fold_in(streams_of[9], 71), 0)
    conv_second = draw_conv_second(jax.random.fold_in(streams_of[9], 71), 0)
    norm_params = jnp.clip(jax.random.uniform(streams_of[6], (4, C), jnp.float32, 0.3, 1.3), 0.3, 1.3)
    norm_first = noise(streams_of[7], (4, C), (0.33 * (IMAGES * H * W) ** 0.5), 117.66257, (), jnp.float32)
    norm_second = jnp.clip(jnp.exp(jax.random.uniform(streams_of[8], (4, C), jnp.float32, math.log(819.2), math.log(3276.8))), 819.2, 3276.8)
    return {"images": images, "valid_masks": valid_masks, "cotangent": cotangent, "conv_weights": conv_weights, "conv_first": conv_first, "conv_second": conv_second, "norm_params": norm_params, "norm_first": norm_first, "norm_second": norm_second}


@jax.custom_vjp
def low(v):
    return lax.optimization_barrier(v.astype(jnp.bfloat16)).astype(jnp.float32)

@jax.custom_vjp
def low_back(v):
    return v

def low_keep(v):
    return (low(v), None)

def low_pass(kept, grad):
    return (grad,)

def back_keep(v):
    return (v, None)

def back_low(kept, grad):
    return (low(grad),)
low.defvjp(low_keep, low_pass)
low_back.defvjp(back_keep, back_low)
learning_rate = 0.5
weight_decay = 0.01
beta_moment = 0.5

def convolve(feature, kernel):
    kernel_taps = kernel.reshape(3, 3, kernel.shape[1], kernel.shape[2])
    return lax.conv_general_dilated(feature, kernel_taps, (1, 1), 'SAME', dimension_numbers=('NHWC', 'HWIO', 'NHWC'), precision=lax.Precision.HIGHEST)

def masked_norm(conv_out, valid_map, valid_count, gain_row, shift_row):
    weight_mask = valid_map[..., None]
    mean_value = lax.optimization_barrier(jnp.sum(weight_mask * conv_out, axis=(0, 1, 2))) / valid_count
    centered = conv_out - mean_value
    variance = lax.optimization_barrier(jnp.sum(weight_mask * centered * centered, axis=(0, 1, 2))) / valid_count
    return weight_mask * (gain_row * (centered * lax.rsqrt(variance + 1e-05)) + shift_row)

def forward(feature, weights, params, valid_map, valid_count):
    kernels = low(weights)
    first_out = low_back(convolve(feature, kernels[0]))
    first_act = masked_norm(first_out, valid_map, valid_count, params[0], params[1])
    hidden = low(jax.nn.gelu(first_act))
    second_out = low_back(convolve(hidden, kernels[1]))
    second_act = masked_norm(second_out, valid_map, valid_count, params[2], params[3])
    summed = second_act + feature
    return jax.nn.gelu(summed)

def lamb_direction(gradient, first_moment, second_moment, param_value, decay_rate):
    new_first = beta_moment * first_moment + (1.0 - beta_moment) * gradient
    new_second = beta_moment * second_moment + (1.0 - beta_moment) * gradient * gradient
    bias_first = 1.0 - beta_moment ** STEP
    bias_second = 1.0 - beta_moment ** STEP
    direction = new_first / bias_first / (jnp.sqrt(new_second / bias_second) + 1e-06) + decay_rate * param_value
    return (new_first, new_second, direction)

def reference(images, valid_masks, cotangent, conv_weights, conv_first, conv_second, norm_params, norm_first, norm_second):
    inputs = images.astype(jnp.float32)
    valid_map = valid_masks.astype(jnp.float32)
    valid_count = jnp.sum(valid_map)

    def wrapped(feature, weights, params):
        return forward(feature, weights, params, valid_map, valid_count)
    summed_out, pullback = jax.vjp(wrapped, inputs, conv_weights, norm_params)
    input_grad, weight_grad, param_grad = pullback(cotangent.astype(jnp.float32))
    new_first, new_second, direction = lamb_direction(weight_grad, conv_first, conv_second, conv_weights, weight_decay)
    weight_norm = jnp.sqrt(lax.optimization_barrier(jnp.sum(conv_weights * conv_weights, axis=(1, 2, 3))))
    direction_norm = jnp.sqrt(lax.optimization_barrier(jnp.sum(direction * direction, axis=(1, 2, 3))))
    new_weights = conv_weights - learning_rate * (weight_norm / (direction_norm + 1e-06))[:, None, None, None] * direction
    param_first, param_second, param_direction = lamb_direction(param_grad, norm_first, norm_second, norm_params, 0.0)
    param_norm = jnp.sqrt(lax.optimization_barrier(jnp.sum(norm_params * norm_params, axis=1)))
    param_dir_norm = jnp.sqrt(lax.optimization_barrier(jnp.sum(param_direction * param_direction, axis=1)))
    new_params = norm_params - learning_rate * (param_norm / (param_dir_norm + 1e-06))[:, None] * param_direction
    trust_norms = jnp.stack([jnp.concatenate([weight_norm, param_norm]), jnp.concatenate([direction_norm, param_dir_norm])])
    return (summed_out.astype(jnp.bfloat16), input_grad.astype(jnp.bfloat16), new_weights, new_weights.astype(jnp.bfloat16), new_first, new_second, new_params, param_first, param_second, trust_norms)
```

```python
import functools

import jax
import jax.numpy as jnp
from jax import lax
from jax.experimental import pallas as pl
from jax.experimental.pallas import tpu as pltpu
from jax.sharding import Mesh
from jax.sharding import PartitionSpec as P

STEP = 3
RATE = 0.5
DECAY = 0.01
BETA = 0.5
BIAS = 1.0 - BETA**STEP
EPS = 1e-05
TINY = 1e-06
ROOT = 0.7978845608028654
CUBE = 0.044715
LANES = 128
VMEM_BYTES = 56 * 1024 * 1024
F32 = jnp.float32
BF16 = jnp.bfloat16


def gelu(v):
    return 0.5 * v * (1.0 + jnp.tanh(ROOT * (v + CUBE * (v * v * v))))


def gelu_both(v):
    t = jnp.tanh(ROOT * (v + CUBE * (v * v * v)))
    value = 0.5 * v * (1.0 + t)
    slope = 0.5 * (1.0 + t) + 0.5 * v * (1.0 - t * t) * (ROOT * (1.0 + (3.0 * CUBE) * (v * v)))
    return value, slope


class Sizes:
    def __init__(self, mesh, images, weights):
        self.Z = mesh.shape["ba"]
        self.R = mesh.shape["ha"] * mesh.shape["wa"]
        self.Q = self.Z
        self.S = self.R // self.Q
        n, self.H, self.W, self.C = images
        self.n_own = n // (self.R * self.Z)
        self.own = self.n_own * self.H * self.W
        self.n_group = self.n_own * self.Q
        self.G = self.own * self.Q
        self.L = self.C // self.Q
        self.LP = max(self.L, LANES)
        self.IB = self.C // self.R
        self.K = weights[1]


def call(body, out_shape, args, scratch=(), flops=0, nbytes=0):
    smem = [a.dtype == jnp.int32 and a.ndim == 1 for a in args]
    return pl.pallas_call(
        body,
        out_shape=out_shape,
        in_specs=[
            pl.BlockSpec(memory_space=pltpu.SMEM if m else pltpu.VMEM) for m in smem
        ],
        out_specs=jax.tree.map(lambda _: pl.BlockSpec(memory_space=pltpu.VMEM), out_shape),
        scratch_shapes=list(scratch),
        compiler_params=pltpu.CompilerParams(vmem_limit_bytes=VMEM_BYTES),
        cost_estimate=pl.CostEstimate(flops=flops, bytes_accessed=nbytes, transcendentals=0),
    )(*args)


def shape(dims, dtype=F32):
    return jax.ShapeDtypeStruct(tuple(dims), dtype)


def image_mask(z, hw):
    dims = (z.H, z.W, z.L)
    rows = lax.broadcasted_iota(jnp.int32, dims, 0).astype(F32)
    cols = lax.broadcasted_iota(jnp.int32, dims, 1).astype(F32)
    tall = hw[0:1, : z.L].reshape(1, 1, z.L)
    wide = hw[1:2, : z.L].reshape(1, 1, z.L)
    return jnp.where((rows < tall) & (cols < wide), 1.0, 0.0).reshape(z.H * z.W, z.L)


def shifted_sum(z, taps, sign):
    dims = (z.n_own, z.H, z.W, z.L)
    cols = lax.broadcasted_iota(jnp.int32, dims, 2)
    total = None
    for c in range(3):
        column = None
        for r in range(3):
            part = taps(3 * r + c).reshape(dims)
            move = (r - 1) * sign
            if move == 1:
                part = jnp.concatenate([part[:, 1:], jnp.zeros_like(part[:, :1])], axis=1)
            elif move == -1:
                part = jnp.concatenate([jnp.zeros_like(part[:, :1]), part[:, :-1]], axis=1)
            column = part if column is None else column + part
        move = (c - 1) * sign
        if move:
            flat = column.reshape(z.n_own * z.H, z.W, z.L)
            flat = pltpu.roll(flat, (-move) % z.W, 1)
            column = flat.reshape(dims)
            edge = z.W - 1 if move == 1 else 0
            column = jnp.where(cols == edge, 0.0, column)
        total = column if total is None else total + column
    return total.reshape(z.own, z.L)


def moved_taps(z, feature):
    dims = (z.n_own, z.H, z.W, z.L)
    cols = lax.broadcasted_iota(jnp.int32, dims, 2)
    out = [None] * 9
    for c in range(3):
        move = c - 1
        column = feature.reshape(dims)
        if move:
            flat = feature.reshape(z.n_own * z.H, z.W, z.L)
            column = pltpu.roll(flat, (-move) % z.W, 1).reshape(dims)
            edge = z.W - 1 if move == 1 else 0
            column = jnp.where(cols == edge, 0.0, column)
        for r in range(3):
            if r == 2:
                part = jnp.concatenate([column[:, 1:], jnp.zeros_like(column[:, :1])], axis=1)
            elif r == 0:
                part = jnp.concatenate([jnp.zeros_like(column[:, :1]), column[:, :-1]], axis=1)
            else:
                part = column
            out[3 * r + c] = part.reshape(z.own, z.L)
    return out


def spread(ref, rows):
    used = rows[0].shape[1]
    if len(rows) < 8:
        rows = rows + [jnp.zeros((8 - len(rows), used), F32)]
    stat = jnp.concatenate(rows, axis=0)
    if used < LANES:
        stat = jnp.concatenate([stat, jnp.zeros((8, LANES - used), F32)], axis=1)
    for k in range(ref.shape[0]):
        ref[k] = stat


def local_stats(z, z_ref, hw_ref, stats_ref):
    px = z.H * z.W

    def first(n, carry):
        count, total = carry
        mask = image_mask(z, hw_ref[n])
        block = z_ref[pl.ds(pl.multiple_of(n * px, px), px), :]
        return count + jnp.sum(mask, 0, keepdims=True), total + jnp.sum(mask * block, 0, keepdims=True)

    zero = jnp.zeros((1, z.L), F32)
    count, total = lax.fori_loop(0, z.n_group, first, (zero, zero), unroll=4)
    mean = total / count

    def second(n, spread_sum):
        mask = image_mask(z, hw_ref[n])
        centered = z_ref[pl.ds(pl.multiple_of(n * px, px), px), :] - mean
        return spread_sum + jnp.sum(mask * centered * centered, 0, keepdims=True)

    squares = lax.fori_loop(0, z.n_group, second, zero, unroll=4)
    spread(stats_ref, [count, mean, squares])


def conv_into(z, x_of, row_of, wcat, y_ref, z_ref, sign=1):
    for m in range(z.Q):
        y_ref[...] = x_of(m)
        z_ref[pl.ds(row_of(m), z.own), :] = shifted_sum(
            z, lambda k: y_ref[:, k * z.LP : k * z.LP + z.L], sign
        )


def fill_kernels(z, at, own, others, wcat):
    for t, blocks in enumerate([own] + others):
        s = at[1] ^ t
        for m, block in enumerate(blocks):
            row = pl.multiple_of((at[2] ^ m) * z.L + s * z.IB, z.IB)
            for k in range(z.K):
                wcat[pl.ds(row, z.IB), k * z.LP : k * z.LP + z.L] = block[k]


def first_conv(z, *refs):
    at = refs[0]
    xs, refs = refs[1 : 1 + z.Q], refs[1 + z.Q :]
    blocks = [refs[t * z.Z : (t + 1) * z.Z] for t in range(z.S)]
    z_ref, slice_ref, hw_ref, stats_ref, wcat, y_ref = refs[z.S * z.Z :]
    fill_kernels(z, at, blocks[0], list(blocks[1:]), wcat)
    for m in range(z.Q):
        j = at[0] ^ m
        for n in range(z.n_own):
            two = xs[m][z.own + 2 * n : z.own + 2 * n + 2, :LANES].astype(F32)
            hw_ref[j * z.n_own + n] = jnp.concatenate([two, jnp.zeros((6, LANES), F32)], axis=0)
        for slot in range(z.Q):

            @pl.when(at[0] == slot)
            def _(m=m, j=j, slot=slot):
                slice_ref[pl.ds(pl.multiple_of(j * z.own, z.own), z.own), :] = xs[m][
                    : z.own, slot * z.L : (slot + 1) * z.L
                ]

    conv_into(
        z,
        lambda m: jnp.dot(xs[m][: z.own, :], wcat[...], preferred_element_type=F32),
        lambda m: pl.multiple_of((at[0] ^ m) * z.own, z.own),
        wcat,
        y_ref,
        z_ref,
    )
    local_stats(z, z_ref, hw_ref, stats_ref)


def second_conv(z, *refs):
    at = refs[0]
    hs, refs = refs[1 : 1 + z.Q], refs[1 + z.Q :]
    blocks = [refs[t * z.Z : (t + 1) * z.Z] for t in range(z.S)]
    hw_ref, z_ref, stats_ref, wcat, h_ref, y_ref = refs[z.S * z.Z :]
    fill_kernels(z, at, blocks[0], list(blocks[1:]), wcat)
    for m in range(z.Q):
        h_ref[at[0] ^ m] = hs[m][...]

    def product(j):
        rows = slice(j * z.own, (j + 1) * z.own)
        if z.L % LANES == 0:
            whole = jnp.concatenate([h_ref[i, rows, :] for i in range(z.Q)], axis=1)
            return jnp.dot(whole, wcat[...], preferred_element_type=F32)
        return sum(
            jnp.dot(h_ref[i, rows, :], wcat[i * z.L : (i + 1) * z.L, :], preferred_element_type=F32)
            for i in range(z.Q)
        )

    conv_into(z, product, lambda j: j * z.own, wcat, y_ref, z_ref)
    local_stats(z, z_ref, hw_ref, stats_ref)


def merged(z, all_ref):
    counts = [all_ref[k, 0:1, : z.L] for k in range(z.S * z.Z)]
    means = [all_ref[k, 1:2, : z.L] for k in range(z.S * z.Z)]
    count = sum(counts)
    mean = sum(c * m for c, m in zip(counts, means)) / count
    squares = sum(
        all_ref[k, 2:3, : z.L] + counts[k] * (means[k] - mean) * (means[k] - mean)
        for k in range(z.S * z.Z)
    )
    return mean, lax.rsqrt(squares / count + EPS), count


def keep(ref, rows):
    used = rows[0].shape[1]
    ref[...] = jnp.concatenate(rows + [jnp.zeros((8 - len(rows), used), F32)], axis=0)


def over_images(z, step, init=0, unroll=2):
    px = z.H * z.W

    def one(n, carry):
        return step(n, pl.ds(pl.multiple_of(n * px, px), px), carry)

    return lax.fori_loop(0, z.n_group, one, init, unroll=unroll)


def hidden(z, z_ref, all_ref, hw_ref, par_ref, h_ref, sum_ref):
    mean, inv, count = merged(z, all_ref)
    keep(sum_ref, [mean, inv, count])
    gain, shift = par_ref[0:1, :], par_ref[1:2, :]

    def step(n, rows, carry):
        mask = image_mask(z, hw_ref[n])
        act = mask * (gain * ((z_ref[rows, :] - mean) * inv) + shift)
        h_ref[rows, :] = gelu(act).astype(BF16)
        return carry

    over_images(z, step)


def middle(z, at, z_ref, all_ref, hw_ref, par_ref, x_ref, *refs):
    cots, refs = refs[: z.Q], refs[z.Q :]
    outs, refs = refs[: z.Q], refs[z.Q :]
    d_ref, sum_ref, stats_ref = refs
    mean, inv, count = merged(z, all_ref)
    keep(sum_ref, [mean, inv, count])
    gain, shift = par_ref[2:3, :], par_ref[3:4, :]
    px = z.H * z.W
    carry = (jnp.zeros((1, z.L), F32), jnp.zeros((1, z.L), F32))
    for m in range(z.Q):
        j = at[0] ^ m

        def step(n, carry, m=m, j=j):
            near = pl.ds(pl.multiple_of(n * px, px), px)
            far = pl.ds(pl.multiple_of(j * z.own + n * px, px), px)
            mask = image_mask(z, hw_ref[j * z.n_own + n])
            normed = (z_ref[far, :] - mean) * inv
            summed = mask * (gain * normed + shift) + x_ref[far, :].astype(F32)
            value, slope = gelu_both(summed)
            outs[m][near, :] = value.astype(BF16)
            d = cots[m][near, :].astype(F32) * slope
            d_ref[far, :] = d
            masked = mask * d
            return (
                carry[0] + jnp.sum(masked, 0, keepdims=True),
                carry[1] + jnp.sum(masked * normed, 0, keepdims=True),
            )

        carry = lax.fori_loop(0, z.n_own, step, carry, unroll=2)
    spread(stats_ref, list(carry))


def norm_grad(z, row, z_ref, up_ref, sum_ref, all_ref, hw_ref, par_ref, out_ref, par_grad_ref):
    mean, inv, count = sum_ref[0:1, :], sum_ref[1:2, :], sum_ref[2:3, :]
    shift_grad = sum(all_ref[k, 0:1, : z.L] for k in range(z.S * z.Z))
    gain_grad = sum(all_ref[k, 1:2, : z.L] for k in range(z.S * z.Z))
    keep(par_grad_ref, [gain_grad, shift_grad])
    gain = par_ref[row : row + 1, :]

    def step(n, rows, carry):
        mask = image_mask(z, hw_ref[n])
        normed = (z_ref[rows, :] - mean) * inv
        grad = inv * mask * gain * (up_ref[rows, :] - (shift_grad + normed * gain_grad) / count)
        out_ref[rows, :] = grad.astype(BF16)
        return carry

    over_images(z, step)


def back_product(z, conv, at, dzs, w_ref, wcat, dz_ref):
    OB = z.C // z.Z
    for s in range(z.S):
        for b in range(z.Z):
            for k in range(z.K):
                block = w_ref[s * z.Z + b, conv, k]
                if z.L % LANES == 0:
                    wcat[0, k * z.LP + s * z.IB : k * z.LP + (s + 1) * z.IB, b * OB : (b + 1) * OB] = block
                else:
                    wcat[b, k * z.LP + s * z.IB : k * z.LP + (s + 1) * z.IB, :] = block
    for m in range(z.Q):
        dz_ref[at[0] ^ m] = dzs[m][...]
    contract = (((1,), (1,)), ((), ()))

    def product(j):
        rows = slice(j * z.own, (j + 1) * z.own)
        if z.L % LANES == 0:
            whole = jnp.concatenate([dz_ref[i, rows, :] for i in range(z.Q)], axis=1)
            return lax.dot_general(whole, wcat[0], contract, preferred_element_type=F32)
        return sum(
            lax.dot_general(dz_ref[i, rows, :], wcat[i], contract, preferred_element_type=F32)
            for i in range(z.Q)
        )

    return product


def back_scratch(z):
    if z.L % LANES == 0:
        wide = pltpu.VMEM((1, z.K * z.LP, z.C), BF16)
    else:
        wide = pltpu.VMEM((z.Z, z.K * z.LP, z.C // z.Z), BF16)
    return [wide, pltpu.VMEM((z.Q, z.G, z.L), BF16), pltpu.VMEM((z.own, z.K * z.LP), F32)]


def hidden_grad(z, *refs):
    at = refs[0]
    dzs, refs = refs[1 : 1 + z.Q], refs[1 + z.Q :]
    w_ref, z_ref, sum_ref, hw_ref, par_ref, da_ref, stats_ref, wcat, dz_ref, y_ref = refs
    product = back_product(z, 1, at, dzs, w_ref, wcat, dz_ref)
    conv_into(z, product, lambda j: j * z.own, wcat, y_ref, da_ref, -1)
    mean, inv = sum_ref[0:1, :], sum_ref[1:2, :]
    gain, shift = par_ref[0:1, :], par_ref[1:2, :]

    def step(n, rows, carry):
        mask = image_mask(z, hw_ref[n])
        normed = (z_ref[rows, :] - mean) * inv
        da = da_ref[rows, :] * gelu_both(mask * (gain * normed + shift))[1]
        da_ref[rows, :] = da
        masked = mask * da
        return (
            carry[0] + jnp.sum(masked, 0, keepdims=True),
            carry[1] + jnp.sum(masked * normed, 0, keepdims=True),
        )

    zero = jnp.zeros((1, z.L), F32)
    spread(stats_ref, list(over_images(z, step, (zero, zero))))


def input_grad(z, *refs):
    at = refs[0]
    dzs, refs = refs[1 : 1 + z.Q], refs[1 + z.Q :]
    w_ref, d_ref = refs[:2]
    outs, refs = refs[2 : 2 + z.Q], refs[2 + z.Q :]
    wcat, dz_ref, y_ref, dx_ref = refs
    product = back_product(z, 0, at, dzs, w_ref, wcat, dz_ref)
    conv_into(z, product, lambda j: j * z.own, wcat, y_ref, dx_ref, -1)
    for m in range(z.Q):
        rows = pl.ds(pl.multiple_of((at[0] ^ m) * z.own, z.own), z.own)
        outs[m][...] = (dx_ref[rows, :] + d_ref[rows, :]).astype(BF16)


def kernel_grad(z, *refs):
    at = refs[0]
    f_ref, refs = refs[1], refs[2:]
    dzs, refs = refs[: z.Q], refs[z.Q :]
    mine_ref, theirs_ref, moved_ref, full_ref = refs
    for j in range(z.Q):
        rows = slice(j * z.own, (j + 1) * z.own)
        for k, part in enumerate(moved_taps(z, f_ref[rows, :].astype(F32))):
            moved_ref[rows, k * z.LP : k * z.LP + z.L] = part.astype(BF16)
    contract = (((0,), (0,)), ((), ()))
    if z.L % LANES == 0:
        whole = jnp.concatenate([dz[...] for dz in dzs], axis=1)
        full_ref[...] = lax.dot_general(moved_ref[...], whole, contract, preferred_element_type=F32)
    else:
        for m in range(z.Q):
            full_ref[:, m * z.LP : m * z.LP + z.L] = lax.dot_general(
                moved_ref[...], dzs[m][...], contract, preferred_element_type=F32
            )
    for m in range(z.Q):
        to = at[2] ^ at[0] ^ m
        for t in range(z.S):
            s = at[1] ^ t
            for k in range(z.K):
                part = full_ref[
                    pl.ds(pl.multiple_of(k * z.LP + s * z.IB, z.IB), z.IB), m * z.LP : m * z.LP + z.L
                ]
                if t == 0:
                    mine_ref[to, k] = part
                else:
                    theirs_ref[t - 1, to, k] = part


def add_sharers(z, *refs):
    mine_ref, refs = refs[0], refs[1:]
    others, outs = refs[: z.S - 1], refs[z.S - 1 :]
    for m in range(z.Z):
        total = mine_ref[m]
        for other in others:
            total = total + other[m]
        outs[m][...] = total.astype(outs[m].dtype)


def direction_of(grad, first, second, param, decay):
    new_first = BETA * first + (1.0 - BETA) * grad
    new_second = BETA * second + (1.0 - BETA) * grad * grad
    move = new_first / BIAS / (jnp.sqrt(new_second / BIAS) + TINY) + decay * param
    return new_first, new_second, move


def moments(z, *refs):
    parts = [refs[j * z.Z : (j + 1) * z.Z] for j in range(2)]
    refs = refs[2 * z.Z :]
    w_ref, first_ref, second_ref, g1_ref, g2_ref, nf_ref, ns_ref, u_ref, stats_ref = refs
    rows = []
    weight_rows = []
    for j in range(2):
        total_u = jnp.zeros((1, z.L), F32)
        total_w = jnp.zeros((1, z.L), F32)
        for k in range(z.K):
            grad = sum(part[k].astype(F32) for part in parts[j])
            w = w_ref[j, k]
            nf, ns, u = direction_of(grad, first_ref[j, k], second_ref[j, k], w, DECAY)
            nf_ref[j, k] = nf
            ns_ref[j, k] = ns
            u_ref[j, k] = u
            total_u = total_u + jnp.sum(u * u, 0, keepdims=True)
            total_w = total_w + jnp.sum(w * w, 0, keepdims=True)
        rows.append(total_u)
        weight_rows.append(total_w)
    spread(
        stats_ref,
        rows + weight_rows + [g1_ref[0:1, :], g1_ref[1:2, :], g2_ref[0:1, :], g2_ref[1:2, :]],
    )


def finish(z, all_ref, w_ref, u_ref, np_ref, nf_ref, ns_ref, *outs):
    nw_ref, copy_ref, nnp_ref, nnf_ref, nns_ref, trust_ref = outs
    total = all_ref[0]
    for k in range(1, z.R * z.Z):
        total = total + all_ref[k]
    tops, bottoms = [], []
    for j in range(2):
        un = jnp.sqrt(jnp.sum(total[j : j + 1, : z.L], axis=1, keepdims=True))
        wn = jnp.sqrt(jnp.sum(total[2 + j : 3 + j, : z.L], axis=1, keepdims=True))
        tops.append(wn)
        bottoms.append(un)
        scale = RATE * (wn / (un + TINY))
        for k in range(z.K):
            new = w_ref[j, k] - scale * u_ref[j, k]
            nw_ref[j, k] = new
            copy_ref[j, k] = new.astype(BF16)
    for j in range(z.Q):
        nnp_ref[:, j * z.L : (j + 1) * z.L] = all_ref[j * z.Z, 4:8, : z.L]
    param = np_ref[...]
    nf, ns, move = direction_of(nnp_ref[...], nf_ref[...], ns_ref[...], param, 0.0)
    nnf_ref[...] = nf
    nns_ref[...] = ns
    pn = jnp.sqrt(jnp.sum(param * param, axis=1, keepdims=True))
    qn = jnp.sqrt(jnp.sum(move * move, axis=1, keepdims=True))
    nnp_ref[...] = param - RATE * (pn / (qn + TINY)) * move
    for r in range(4):
        tops.append(pn[r : r + 1])
        bottoms.append(qn[r : r + 1])
    at_row = lax.broadcasted_iota(jnp.int32, (2, 6), 0)
    at_col = lax.broadcasted_iota(jnp.int32, (2, 6), 1)
    trust = jnp.zeros((2, 6), F32)
    for c in range(6):
        trust = jnp.where(at_col == c, jnp.where(at_row == 0, tops[c], bottoms[c]), trust)
    trust_ref[...] = trust


def prepare(z, x_ref, valid_ref, cot_ref, at, ext_ref, *cots):
    ext_ref[: z.own, :] = x_ref[...]
    rows = []
    for n in range(z.n_own):
        valid = valid_ref[n].astype(F32)
        tall = jnp.sum(valid[:, 0:1], axis=0, keepdims=True)
        wide = jnp.sum(valid[0:1, :], axis=1, keepdims=True)
        rows += [tall, wide]
    rows = [jnp.broadcast_to(r, (1, z.C)) for r in rows]
    fill = ext_ref.shape[0] - z.own - len(rows)
    ext_ref[z.own :, :] = jnp.concatenate(rows + [jnp.zeros((fill, z.C), F32)], axis=0).astype(BF16)
    for m in range(z.Q):
        for slot in range(z.Q):

            @pl.when((at[0] ^ m) == slot)
            def _(m=m, slot=slot):
                cots[m][...] = cot_ref[:, slot * z.L : (slot + 1) * z.L]


def assemble(z, at, *refs):
    parts, out_ref, hold = refs[: z.Q], refs[z.Q], refs[z.Q + 1]
    for m in range(z.Q):
        hold[at[0] ^ m] = parts[m][...]
    for j in range(z.Q):
        out_ref[:, j * z.L : (j + 1) * z.L] = hold[j]


def shards(z, images, masks, cotangent, weights, first, second, params, p_first, p_second):
    q, s, b = lax.axis_index("q"), lax.axis_index("s"), lax.axis_index("z")
    at = jnp.stack([q, s, b]).astype(jnp.int32)
    everyone = ("q", "s", "z")

    def place(a, c, e):
        return (a * z.S + c) * z.Z + e

    def over_q(v, m):
        return lax.ppermute(v, "q", [(i, i ^ m) for i in range(z.Q)]) if m else v

    def over_z(v, m):
        return lax.ppermute(v, "z", [(i, i ^ m) for i in range(z.Z)]) if m else v

    def over_s(v, m):
        return lax.ppermute(v, "s", [(i, i ^ m) for i in range(z.S)]) if m else v

    def gather_q(v):
        return [over_q(v, m) for m in range(z.Q)]

    def sharers(v):
        return lax.all_to_all(v, ("s", "z"), 0, 0)

    def fetch(w):
        own = []
        for m in range(z.Z):
            pairs = [
                (place(a, c, e), place(e, c, a ^ m))
                for a in range(z.Q)
                for c in range(z.S)
                for e in range(z.Z)
            ]
            own.append(lax.ppermute(w, everyone, pairs))
        return own

    def share(own):
        return [[over_s(v, t) for v in own] for t in range(1, z.S)]

    rows = z.own
    GL = (z.G, z.L)
    conv_flops = 2 * z.G * z.C * z.K * z.L
    many = z.S * z.Z
    low = [weights[j].astype(BF16) for j in range(2)]
    extra = 16 * ((2 * z.n_own + 15) // 16)
    prepared = call(
        functools.partial(prepare, z),
        [shape((rows + extra, z.C), BF16)] + [shape((rows, z.L), BF16)] * z.Q,
        (images.reshape(rows, z.C), masks, cotangent.reshape(rows, z.C), at),
    )
    x_ext, cots = prepared[0], prepared[1:]
    own_one = fetch(low[0])
    xs = gather_q(x_ext)
    others_one = share(own_one)
    slice_params = lax.dynamic_slice(params, (0, q * z.L), (4, z.L))

    conv_scratch = [pltpu.VMEM((z.C, z.K * z.LP), BF16)]
    y_scratch = [pltpu.VMEM((rows, z.K * z.LP), F32)]
    z1, x_slice, hw, stats = call(
        functools.partial(first_conv, z),
        [shape(GL), shape(GL, BF16), shape((z.n_group, 8, LANES)), shape((many, 8, LANES))],
        (at, *xs, *own_one, *[v for o in others_one for v in o]),
        conv_scratch + y_scratch,
        flops=conv_flops,
    )
    own_two = fetch(low[1])
    others_two = share(own_two)
    cots = [over_q(cots[m], m) for m in range(z.Q)]
    h1, sum_one = call(
        functools.partial(hidden, z),
        [shape(GL, BF16), shape((8, z.L))],
        (z1, sharers(stats), hw, slice_params),
        flops=z.G * z.L * 20,
    )
    hs = gather_q(h1)
    z2, stats = call(
        functools.partial(second_conv, z),
        [shape(GL), shape((many, 8, LANES))],
        (at, *hs, *own_two, *[v for o in others_two for v in o], hw),
        conv_scratch + [pltpu.VMEM((z.Q, z.G, z.L), BF16)] + y_scratch,
        flops=conv_flops,
    )
    back = lax.all_gather(jnp.stack(low), ("s", "z"))
    mid = call(
        functools.partial(middle, z),
        [shape((rows, z.L), BF16)] * z.Q + [shape(GL), shape((8, z.L)), shape((many, 8, LANES))],
        (at, z2, sharers(stats), hw, slice_params, x_slice, *cots),
        flops=z.G * z.L * 40,
    )
    outs, (d, sum_two, stats) = mid[: z.Q], mid[z.Q :]
    dz2, grad_two = call(
        functools.partial(norm_grad, z, 2),
        [shape(GL, BF16), shape((8, z.L))],
        (z2, d, sum_two, sharers(stats), hw, slice_params),
        flops=z.G * z.L * 10,
    )
    dz2s = gather_q(dz2)
    da1, stats = call(
        functools.partial(hidden_grad, z),
        [shape(GL), shape((many, 8, LANES))],
        (at, *dz2s, back, z1, sum_one, hw, slice_params),
        back_scratch(z),
        flops=conv_flops,
    )
    grad_scratch = [pltpu.VMEM((z.G, z.K * z.LP), BF16), pltpu.VMEM((z.K * z.LP, z.Q * z.LP), F32)]
    piece = (z.K, z.IB, z.L)

    def reduce_kernels(feature, dzs):
        mine, theirs = call(
            functools.partial(kernel_grad, z),
            [shape((z.Z, *piece)), shape((z.S - 1, z.Z, *piece))],
            (at, feature, *dzs),
            grad_scratch,
            flops=conv_flops,
        )
        received = [over_s(theirs[t - 1], t) for t in range(1, z.S)]
        parts = call(
            functools.partial(add_sharers, z),
            [shape(piece)] + [shape(piece, BF16)] * (z.Z - 1),
            (mine, *received),
        )
        return [over_z(parts[m], m) for m in range(z.Z)]

    parts_two = reduce_kernels(h1, dz2s)
    dz1, grad_one = call(
        functools.partial(norm_grad, z, 0),
        [shape(GL, BF16), shape((8, z.L))],
        (z1, da1, sum_one, sharers(stats), hw, slice_params),
        flops=z.G * z.L * 10,
    )
    dz1s = gather_q(dz1)
    parts_one = reduce_kernels(x_slice, dz1s)
    dxs = call(
        functools.partial(input_grad, z),
        [shape((rows, z.L), BF16)] * z.Q,
        (at, *dz1s, back, d),
        back_scratch(z) + [pltpu.VMEM(GL, F32)],
        flops=conv_flops,
    )

    def give_back(parts):
        parts = [over_q(parts[m], m) for m in range(z.Q)]
        return call(
            functools.partial(assemble, z),
            shape((rows, z.C), BF16),
            (at, *parts),
            [pltpu.VMEM((z.Q, rows, z.L), BF16)],
        ).reshape(images.shape)

    block_output = give_back(outs)
    dx = give_back(dxs)
    new_first, new_second, move, stats = call(
        functools.partial(moments, z),
        [shape(weights.shape)] * 3 + [shape((z.R * z.Z, 8, LANES))],
        (*parts_one, *parts_two, weights, first, second, grad_one, grad_two),
    )
    stats = lax.all_to_all(stats, ("s", "q", "z"), 0, 0)
    new_weights, copies, new_params, new_p_first, new_p_second, trust = call(
        functools.partial(finish, z),
        [shape(weights.shape), shape(weights.shape, BF16)] + [shape(params.shape)] * 3 + [shape((2, 6))],
        (stats, weights, move, params, p_first, p_second),
    )
    return (
        block_output,
        dx,
        new_weights,
        copies,
        new_first,
        new_second,
        new_params,
        new_p_first,
        new_p_second,
        trust,
    )


def solution(mesh):
    def whole(images, masks, cotangent, weights, first, second, params, p_first, p_second):
        z = Sizes(mesh, images.shape, weights.shape)
        inner = Mesh(mesh.devices.reshape(z.Q, z.S, z.Z), ("q", "s", "z"))
        pixels = P(("q", "s", "z"), None, None, None)
        kernels = P(None, None, ("q", "s"), "z")
        return jax.shard_map(
            functools.partial(shards, z),
            mesh=inner,
            in_specs=(pixels, P(("q", "s", "z"), None, None), pixels, kernels, kernels, kernels, P(), P(), P()),
            out_specs=(pixels, pixels, kernels, kernels, kernels, kernels, P(), P(), P(), P()),
            check_vma=False,
        )(images, masks, cotangent, weights, first, second, params, p_first, p_second)

    return whole
```

```python
import functools

import jax
import jax.numpy as jnp
from jax import lax
from jax.experimental import pallas as pl
from jax.experimental.pallas import tpu as pltpu
from jax.sharding import Mesh
from jax.sharding import PartitionSpec as P

STEP = 3
RATE = 0.5
DECAY = 0.01
BETA = 0.5
BIAS = 1.0 - BETA**STEP
EPS = 1e-05
TINY = 1e-06
ROOT = 0.7978845608028654
CUBE = 0.044715
LANES = 128
COST_GRAD = 3 * 10**9
F32 = jnp.float32
BF16 = jnp.bfloat16


def gelu(v):
    return 0.5 * v * (1.0 + jnp.tanh(ROOT * (v + CUBE * (v * v * v))))


def gelu_both(v):
    t = jnp.tanh(ROOT * (v + CUBE * (v * v * v)))
    value = 0.5 * v * (1.0 + t)
    slope = 0.5 * (1.0 + t) + 0.5 * v * (1.0 - t * t) * (ROOT * (1.0 + (3.0 * CUBE) * (v * v)))
    return value, slope


class Sizes:
    def __init__(self, mesh, images, weights):
        self.Z = mesh.shape["ba"]
        self.R = mesh.shape["ha"] * mesh.shape["wa"]
        self.Q = self.Z
        self.S = self.R // self.Q
        n, self.H, self.W, self.C = images
        self.n_own = n // (self.R * self.Z)
        self.own = self.n_own * self.H * self.W
        self.n_group = self.n_own * self.Q
        self.G = self.own * self.Q
        self.L = self.C // self.Q
        self.LP = max(self.L, LANES)
        self.IB = self.C // self.R
        self.K = weights[1]
        self.extra = 16 * ((2 * self.n_own + 15) // 16)
        self.sent = self.own + self.extra + self.own // self.Q


def call(body, out_shape, args, scratch=(), limit=8, far=(), after=(), cost=1, raw=()):
    smem = [a.dtype == jnp.int32 and a.ndim == 1 for a in args]
    away = [any(a is f for f in far) for a in args]
    args = [
        a if m else pltpu.with_memory_space_constraint(a, pltpu.HBM if w else pltpu.VMEM)
        for a, m, w in zip(args, smem, away)
    ]
    n = len(args)

    def run(*refs):
        body(*refs[:n], *refs[n + len(after) :])

    return pl.pallas_call(
        run,
        out_shape=out_shape,
        in_specs=[pl.BlockSpec(memory_space=pltpu.SMEM if m else pltpu.VMEM) for m in smem]
        + [pl.BlockSpec(memory_space=pl.ANY)] * len(after),
        out_specs=jax.tree.map(
            lambda o: pl.BlockSpec(memory_space=pltpu.HBM if any(o is r for r in raw) else pltpu.VMEM),
            out_shape,
        ),
        scratch_shapes=list(scratch),
        compiler_params=pltpu.CompilerParams(vmem_limit_bytes=limit * 1024 * 1024),
        cost_estimate=pl.CostEstimate(flops=cost, bytes_accessed=1, transcendentals=0),
    )(*args, *after)


together = lax.optimization_barrier


def near(dims, dtype=F32):
    return pltpu.VMEM(tuple(dims), dtype)


def away(dims, dtype=F32):
    return pltpu.HBM(tuple(dims), dtype)


def shape(dims, dtype=F32):
    return jax.ShapeDtypeStruct(tuple(dims), dtype)


def image_mask(z, hw):
    dims = (z.H, z.W, z.L)
    rows = lax.broadcasted_iota(jnp.int32, dims, 0).astype(F32)
    cols = lax.broadcasted_iota(jnp.int32, dims, 1).astype(F32)
    tall = hw[0:1, : z.L].reshape(1, 1, z.L)
    wide = hw[1:2, : z.L].reshape(1, 1, z.L)
    return jnp.where((rows < tall) & (cols < wide), 1.0, 0.0).reshape(z.H * z.W, z.L)


def shifted_sum(z, taps, sign):
    dims = (z.n_own, z.H, z.W, z.L)
    cols = lax.broadcasted_iota(jnp.int32, dims, 2)
    total = None
    for c in range(3):
        column = None
        for r in range(3):
            part = taps(3 * r + c).reshape(dims)
            move = (r - 1) * sign
            if move == 1:
                part = jnp.concatenate([part[:, 1:], jnp.zeros_like(part[:, :1])], axis=1)
            elif move == -1:
                part = jnp.concatenate([jnp.zeros_like(part[:, :1]), part[:, :-1]], axis=1)
            column = part if column is None else column + part
        move = (c - 1) * sign
        if move:
            flat = column.reshape(z.n_own * z.H, z.W, z.L)
            flat = pltpu.roll(flat, (-move) % z.W, 1)
            column = flat.reshape(dims)
            edge = z.W - 1 if move == 1 else 0
            column = jnp.where(cols == edge, 0.0, column)
        total = column if total is None else total + column
    return total.reshape(z.own, z.L)


def moved_taps(z, feature):
    dims = (z.n_own, z.H, z.W, z.L)
    cols = lax.broadcasted_iota(jnp.int32, dims, 2)
    out = [None] * 9
    for c in range(3):
        move = 1 - c
        column = feature.reshape(dims)
        if move:
            flat = feature.reshape(z.n_own * z.H, z.W, z.L)
            column = pltpu.roll(flat, (-move) % z.W, 1).reshape(dims)
            edge = z.W - 1 if move == 1 else 0
            column = jnp.where(cols == edge, 0.0, column)
        for r in range(3):
            if r == 0:
                part = jnp.concatenate([column[:, 1:], jnp.zeros_like(column[:, :1])], axis=1)
            elif r == 2:
                part = jnp.concatenate([jnp.zeros_like(column[:, :1]), column[:, :-1]], axis=1)
            else:
                part = column
            out[3 * r + c] = part.reshape(z.own, z.L)
    return out


def fill_moved(z, a_ref, b_ref, moved_ref):
    half = z.Q // 2
    for j in range(z.Q):
        ref, at_row = (a_ref, j) if j < half else (b_ref, j - half)
        block = ref[at_row * z.own : (at_row + 1) * z.own, :].astype(F32)
        for k, part in enumerate(moved_taps(z, block)):
            moved_ref[j * z.own : (j + 1) * z.own, k * z.LP : k * z.LP + z.L] = part.astype(BF16)


def spread(ref, rows):
    used = rows[0].shape[1]
    if len(rows) < 8:
        rows = rows + [jnp.zeros((8 - len(rows), used), F32)]
    stat = jnp.concatenate(rows, axis=0)
    if used < LANES:
        stat = jnp.concatenate([stat, jnp.zeros((8, LANES - used), F32)], axis=1)
    for k in range(ref.shape[0]):
        ref[k] = stat


def local_stats(z, z_ref, hw_ref, stats_ref):
    px = z.H * z.W

    def first(n, carry):
        count, total = carry
        mask = image_mask(z, hw_ref[n])
        block = z_ref[pl.ds(pl.multiple_of(n * px, px), px), :]
        return count + jnp.sum(mask, 0, keepdims=True), total + jnp.sum(mask * block, 0, keepdims=True)

    zero = jnp.zeros((1, z.L), F32)
    count, total = lax.fori_loop(0, z.n_group, first, (zero, zero), unroll=4)
    mean = total / count

    def second(n, spread_sum):
        mask = image_mask(z, hw_ref[n])
        centered = z_ref[pl.ds(pl.multiple_of(n * px, px), px), :] - mean
        return spread_sum + jnp.sum(mask * centered * centered, 0, keepdims=True)

    squares = lax.fori_loop(0, z.n_group, second, zero, unroll=4)
    spread(stats_ref, [count, mean, squares])


def conv_into(z, product, y_ref, z_ref, sign=1):
    for j in range(z.Q):
        y_ref[...] = product(j)
        z_ref[j * z.own : (j + 1) * z.own, :] = shifted_sum(
            z, lambda k: y_ref[:, k * z.LP : k * z.LP + z.L], sign
        )


def fill_kernels(z, at, blocks, wcat):
    for t, block in enumerate(blocks):
        s = at[1] ^ t
        for a in range(z.Z):
            row = pl.multiple_of(a * z.L + s * z.IB, z.IB)
            for k in range(z.K):
                wcat[pl.ds(row, z.IB), k * z.LP : k * z.LP + z.L] = block[a, k]


def first_conv(z, at, np_ref, x_ref, *refs):
    blocks, refs = refs[: z.S], refs[z.S :]
    z_ref, slice_ref, cot_ref, par_ref, hw_ref, stats_ref, far_w, far_x, wcat, y_ref, sem = refs
    start, high = z.own + z.extra, z.own // z.Q
    fill_kernels(z, at, blocks, wcat)
    copies = [
        pltpu.make_async_copy(wcat, far_w, sem.at[0]),
        pltpu.make_async_copy(x_ref.at[:, : z.own, :], far_x, sem.at[1]),
    ]
    for copy in copies:
        copy.start()
    for j in range(z.Q):
        for n in range(z.n_own):
            row = z.own + 2 * n
            two = x_ref[j, row : row + 2, :LANES].astype(F32)
            hw_ref[j * z.n_own + n] = jnp.concatenate([two, jnp.zeros((6, LANES), F32)], axis=0)
        for i in range(z.Q):
            row = j * z.own + i * high
            cot_ref[row : row + high, :] = x_ref[j, start:, i * z.L : (i + 1) * z.L]
    for slot in range(z.Q):

        @pl.when(at[0] == slot)
        def _(slot=slot):
            par_ref[...] = np_ref[:, slot * z.L : (slot + 1) * z.L]
            for j in range(z.Q):
                slice_ref[j * z.own : (j + 1) * z.own, :] = x_ref[
                    j, : z.own, slot * z.L : (slot + 1) * z.L
                ]

    def product(j):
        return jnp.dot(x_ref[j, : z.own, :], wcat[...], preferred_element_type=F32)

    conv_into(z, product, y_ref, z_ref)
    local_stats(z, z_ref, hw_ref, stats_ref)
    for copy in copies:
        copy.wait()


def gathered(z, at, parts, hold):
    half = z.G // 2
    for m in range(z.Q):
        hold[at[0] ^ m, :half] = parts[m][...]
        hold[at[0] ^ m, half:] = parts[z.Q + m][...]


def second_conv(z, at, *refs):
    hs, refs = refs[: 2 * z.Q], refs[2 * z.Q :]
    blocks, refs = refs[: z.S], refs[z.S :]
    hw_ref, z_ref, stats_ref, far_ref, refs = *refs[:4], refs[4:]
    outs, (wcat, y_ref, h_ref, sem) = refs[: z.Q], refs[z.Q :]
    for m in range(z.Q):
        outs[m][...] = blocks[0][at[0] ^ m]
    gathered(z, at, hs, h_ref)
    copy = pltpu.make_async_copy(h_ref, far_ref, sem)
    copy.start()
    fill_kernels(z, at, blocks, wcat)

    def product(j):
        rows = slice(j * z.own, (j + 1) * z.own)
        if z.L % LANES == 0:
            whole = jnp.concatenate([h_ref[i, rows, :] for i in range(z.Q)], axis=1)
            return jnp.dot(whole, wcat[...], preferred_element_type=F32)
        return sum(
            jnp.dot(h_ref[i, rows, :], wcat[i * z.L : (i + 1) * z.L, :], preferred_element_type=F32)
            for i in range(z.Q)
        )

    conv_into(z, product, y_ref, z_ref)
    local_stats(z, z_ref, hw_ref, stats_ref)
    copy.wait()


def merged(z, all_ref):
    counts = [all_ref[k, 0:1, : z.L] for k in range(z.S * z.Z)]
    means = [all_ref[k, 1:2, : z.L] for k in range(z.S * z.Z)]
    count = sum(counts)
    mean = sum(c * m for c, m in zip(counts, means)) / count
    squares = sum(
        all_ref[k, 2:3, : z.L] + counts[k] * (means[k] - mean) * (means[k] - mean)
        for k in range(z.S * z.Z)
    )
    return mean, lax.rsqrt(squares / count + EPS), count


def keep(ref, rows):
    used = rows[0].shape[1]
    ref[...] = jnp.concatenate(rows + [jnp.zeros((8 - len(rows), used), F32)], axis=0)


def over_images(z, step, init=0, unroll=2):
    px = z.H * z.W

    def one(n, carry):
        return step(n, pl.ds(pl.multiple_of(n * px, px), px), carry)

    return lax.fori_loop(0, z.n_group, one, init, unroll=unroll)


def over_halves(z, step, refs):
    px, count = z.H * z.W, z.n_group // 2
    for i, ref in enumerate(refs):

        def one(n, carry, i=i, ref=ref):
            rows = pl.ds(pl.multiple_of((i * count + n) * px, px), px)
            ref[pl.ds(pl.multiple_of(n * px, px), px), :] = step(i * count + n, rows)
            return carry

        lax.fori_loop(0, count, one, 0, unroll=2)


def hidden(z, z_ref, all_ref, hw_ref, par_ref, a_ref, b_ref, sum_ref):
    mean, inv, count = merged(z, all_ref)
    keep(sum_ref, [mean, inv, count])
    gain, shift = par_ref[0:1, :], par_ref[1:2, :]

    def step(n, rows):
        mask = image_mask(z, hw_ref[n])
        return gelu(mask * (gain * ((z_ref[rows, :] - mean) * inv) + shift)).astype(BF16)

    over_halves(z, step, (a_ref, b_ref))


def middle(z, at, z_ref, all_ref, hw_ref, par_ref, x_ref, cot_ref, *refs):
    out_ref, d_ref, sum_ref, stats_ref = refs
    mean, inv, count = merged(z, all_ref)
    keep(sum_ref, [mean, inv, count])
    gain, shift = par_ref[2:3, :], par_ref[3:4, :]
    px = z.H * z.W
    carry = (jnp.zeros((1, z.L), F32), jnp.zeros((1, z.L), F32))
    for j in range(z.Q):

        def step(n, carry, j=j):
            local = pl.ds(pl.multiple_of(n * px, px), px)
            rows = pl.ds(pl.multiple_of(j * z.own + n * px, px), px)
            mask = image_mask(z, hw_ref[j * z.n_own + n])
            normed = (z_ref[rows, :] - mean) * inv
            summed = mask * (gain * normed + shift) + x_ref[rows, :].astype(F32)
            value, slope = gelu_both(summed)
            out_ref[j, local, :] = value.astype(BF16)
            d = cot_ref[rows, :].astype(F32) * slope
            d_ref[rows, :] = d
            masked = mask * d
            return (
                carry[0] + jnp.sum(masked, 0, keepdims=True),
                carry[1] + jnp.sum(masked * normed, 0, keepdims=True),
            )

        carry = lax.fori_loop(0, z.n_own, step, carry, unroll=2)
    spread(stats_ref, list(carry))


def norm_grad(z, row, z_ref, up_ref, sum_ref, all_ref, hw_ref, par_ref, a_ref, b_ref, par_grad_ref):
    mean, inv, count = sum_ref[0:1, :], sum_ref[1:2, :], sum_ref[2:3, :]
    shift_grad = sum(all_ref[k, 0:1, : z.L] for k in range(z.S * z.Z))
    gain_grad = sum(all_ref[k, 1:2, : z.L] for k in range(z.S * z.Z))
    keep(par_grad_ref, [gain_grad, shift_grad])
    gain = par_ref[row : row + 1, :]

    def step(n, rows):
        mask = image_mask(z, hw_ref[n])
        normed = (z_ref[rows, :] - mean) * inv
        grad = inv * mask * gain * (up_ref[rows, :] - (shift_grad + normed * gain_grad) / count)
        return grad.astype(BF16)

    over_halves(z, step, (a_ref, b_ref))


def back_product(z, at, dz_ref, blocks, wcat):
    for t, block in enumerate(blocks):
        s = at[1] ^ t
        for b in range(z.Z):
            for k in range(z.K):
                rows = pl.ds(pl.multiple_of(k * z.LP + s * z.IB, z.IB), z.IB)
                if z.L % LANES == 0:
                    wcat[0, rows, b * z.L : (b + 1) * z.L] = block[b, k]
                else:
                    wcat[b, rows, :] = block[b, k]
    contract = (((1,), (1,)), ((), ()))

    def product(j):
        rows = slice(j * z.own, (j + 1) * z.own)
        if z.L % LANES == 0:
            whole = jnp.concatenate([dz_ref[i, rows, :] for i in range(z.Q)], axis=1)
            return lax.dot_general(whole, wcat[0], contract, preferred_element_type=F32)
        return sum(
            lax.dot_general(dz_ref[i, rows, :], wcat[i], contract, preferred_element_type=F32)
            for i in range(z.Q)
        )

    return product


def back_scratch(z):
    if z.L % LANES == 0:
        wide = pltpu.VMEM((1, z.K * z.LP, z.C), BF16)
    else:
        wide = pltpu.VMEM((z.Z, z.K * z.LP, z.C // z.Z), BF16)
    return [wide, pltpu.VMEM((z.own, z.K * z.LP), F32), pltpu.VMEM((z.Q, z.G, z.L), BF16)]


def hidden_grad(z, at, *refs):
    dzs, refs = refs[: 2 * z.Q], refs[2 * z.Q :]
    blocks, refs = refs[: z.S], refs[z.S :]
    z_ref, sum_ref, hw_ref, par_ref, da_ref, stats_ref, wcat, y_ref, dz_ref = refs
    gathered(z, at, dzs, dz_ref)
    conv_into(z, back_product(z, at, dz_ref, blocks, wcat), y_ref, da_ref, -1)
    mean, inv = sum_ref[0:1, :], sum_ref[1:2, :]
    gain, shift = par_ref[0:1, :], par_ref[1:2, :]

    def step(n, rows, carry):
        mask = image_mask(z, hw_ref[n])
        normed = (z_ref[rows, :] - mean) * inv
        da = da_ref[rows, :] * gelu_both(mask * (gain * normed + shift))[1]
        da_ref[rows, :] = da
        masked = mask * da
        return (
            carry[0] + jnp.sum(masked, 0, keepdims=True),
            carry[1] + jnp.sum(masked * normed, 0, keepdims=True),
        )

    zero = jnp.zeros((1, z.L), F32)
    spread(stats_ref, list(over_images(z, step, (zero, zero))))


def input_part(z, at, a_ref, b_ref, w_ref, d_ref, *refs):
    outs, (moved_ref, dx_ref) = refs[: z.Q], refs[z.Q :]
    fill_moved(z, a_ref, b_ref, moved_ref)
    contract = (((1,), (1,)), ((), ()))
    for j in range(z.Q):
        rows = slice(j * z.own, (j + 1) * z.own)
        dx_ref[j] = lax.dot_general(moved_ref[rows, :], w_ref[...], contract, preferred_element_type=F32)
    for slot in range(z.Q):

        @pl.when(at[0] == slot)
        def _(slot=slot):
            for j in range(z.Q):
                lanes = slice(slot * z.L, (slot + 1) * z.L)
                dx_ref[j, :, lanes] = dx_ref[j, :, lanes] + d_ref[j * z.own : (j + 1) * z.own, :]

    for m in range(z.Q):
        outs[m][...] = dx_ref[at[0] ^ m].astype(outs[m].dtype)


def kernel_grad(z, at, f_ref, a_ref, b_ref, mine_ref, *refs):
    theirs, (moved_ref, full_ref) = refs[:-2], refs[-2:]
    fill_moved(z, a_ref, b_ref, moved_ref)
    contract = (((0,), (0,)), ((), ()))
    if f_ref.shape[2] == z.C:
        whole = f_ref[...].reshape(z.G, z.C)
        full_ref[...] = lax.dot_general(whole, moved_ref[...], contract, preferred_element_type=F32)
    elif z.L % LANES == 0:
        whole = jnp.concatenate([f_ref[i] for i in range(z.Q)], axis=1)
        full_ref[...] = lax.dot_general(whole, moved_ref[...], contract, preferred_element_type=F32)
    else:
        for i in range(z.Q):
            full_ref[i * z.L : (i + 1) * z.L, :] = lax.dot_general(
                f_ref[i], moved_ref[...], contract, preferred_element_type=F32
            )
    for r in range(z.Q):
        for t in range(z.S):
            row = pl.multiple_of((at[0] ^ r) * z.L + (at[1] ^ t) * z.IB, z.IB)
            for k in range(z.K):
                part = full_ref[pl.ds(row, z.IB), k * z.LP : k * z.LP + z.L]
                if t == 0:
                    mine_ref[r, k] = part
                else:
                    theirs[(t - 1) * z.Q + r][k] = part.astype(BF16)


def add_sharers(z, at, *refs):
    count = 1 + z.Q * (z.S - 1)
    mine_ref, others, refs = refs[0], refs[1:count], refs[count:]
    value_ref = None
    if len(refs) > z.Q:
        value_ref, refs = refs[0], refs[1:]
    for r in range(z.Q):
        for k in range(z.K):
            total = mine_ref[r, k]
            for other in others[r :: z.Q]:
                total = total + other[k].astype(F32)
            refs[r][k * z.IB : (k + 1) * z.IB, :] = total.astype(BF16)
        if value_ref is not None:
            refs[r][z.K * z.IB :, :] = value_ref[at[0] ^ r]


def route(z, at, *refs):
    parts, refs = refs[: z.Q], refs[z.Q :]
    outs, refs = refs[: z.Z], refs[z.Z :]
    hold = refs[-1]
    for r in range(z.Q):
        hold[at[2] ^ at[0] ^ r] = parts[r][: z.K * z.IB, :]
    for m in range(z.Z):
        outs[m][...] = hold[m]
    if len(refs) == 3:
        value_ref, slots, _ = refs
        for r in range(z.Q):
            slots[at[0] ^ r] = parts[r][z.K * z.IB :, :]
        for j in range(z.Q):
            value_ref[:, j * z.L : (j + 1) * z.L] = slots[j]


def total_of(z, *refs):
    refs[-1][...] = sum(ref[...].astype(F32) for ref in refs[:-1]).astype(refs[-1].dtype)


def direction_of(grad, first, second, param, decay):
    new_first = BETA * first + (1.0 - BETA) * grad
    new_second = BETA * second + (1.0 - BETA) * grad * grad
    move = new_first / BIAS / (jnp.sqrt(new_second / BIAS) + TINY) + decay * param
    return new_first, new_second, move


def moments(z, *refs):
    parts = [refs[: z.Z], refs[z.Z : z.Z + 1]]
    refs = refs[z.Z + 1 :]
    w_ref, first_ref, second_ref, g1_ref, g2_ref, nf_ref, ns_ref, u_ref, stats_ref = refs
    rows = []
    weight_rows = []
    for j in range(2):
        total_u = jnp.zeros((1, z.L), F32)
        total_w = jnp.zeros((1, z.L), F32)
        for k in range(z.K):
            grad = sum(part[k * z.IB : (k + 1) * z.IB, :].astype(F32) for part in parts[j])
            w = w_ref[j, k]
            nf, ns, u = direction_of(grad, first_ref[j, k], second_ref[j, k], w, DECAY)
            nf_ref[j, k] = nf
            ns_ref[j, k] = ns
            u_ref[j, k] = u
            total_u = total_u + jnp.sum(u * u, 0, keepdims=True)
            total_w = total_w + jnp.sum(w * w, 0, keepdims=True)
        rows.append(total_u)
        weight_rows.append(total_w)
    spread(
        stats_ref,
        rows + weight_rows + [g1_ref[0:1, :], g1_ref[1:2, :], g2_ref[0:1, :], g2_ref[1:2, :]],
    )


def finish(z, all_ref, w_ref, u_ref, np_ref, nf_ref, ns_ref, *outs):
    nw_ref, copy_ref, nnp_ref, nnf_ref, nns_ref, trust_ref = outs
    total = all_ref[0]
    for k in range(1, z.R * z.Z):
        total = total + all_ref[k]
    tops, bottoms = [], []
    for j in range(2):
        un = jnp.sqrt(jnp.sum(total[j : j + 1, : z.L], axis=1, keepdims=True))
        wn = jnp.sqrt(jnp.sum(total[2 + j : 3 + j, : z.L], axis=1, keepdims=True))
        tops.append(wn)
        bottoms.append(un)
        scale = RATE * (wn / (un + TINY))
        for k in range(z.K):
            new = w_ref[j, k] - scale * u_ref[j, k]
            nw_ref[j, k] = new
            copy_ref[j, k] = new.astype(BF16)
    for j in range(z.Q):
        nnp_ref[:, j * z.L : (j + 1) * z.L] = all_ref[j * z.Z, 4:8, : z.L]
    param = np_ref[...]
    nf, ns, move = direction_of(nnp_ref[...], nf_ref[...], ns_ref[...], param, 0.0)
    nnf_ref[...] = nf
    nns_ref[...] = ns
    pn = jnp.sqrt(jnp.sum(param * param, axis=1, keepdims=True))
    qn = jnp.sqrt(jnp.sum(move * move, axis=1, keepdims=True))
    nnp_ref[...] = param - RATE * (pn / (qn + TINY)) * move
    for r in range(4):
        tops.append(pn[r : r + 1])
        bottoms.append(qn[r : r + 1])
    at_row = lax.broadcasted_iota(jnp.int32, (2, 6), 0)
    at_col = lax.broadcasted_iota(jnp.int32, (2, 6), 1)
    trust = jnp.zeros((2, 6), F32)
    for c in range(6):
        trust = jnp.where(at_col == c, jnp.where(at_row == 0, tops[c], bottoms[c]), trust)
    trust_ref[...] = trust


def extend(z, x_ref, valid_ref, cot_ref, out_ref):
    rows = []
    for n in range(z.n_own):
        valid = valid_ref[n].astype(F32)
        tall = jnp.sum(valid[:, 0:1], axis=0, keepdims=True)
        wide = jnp.sum(valid[0:1, :], axis=1, keepdims=True)
        rows += [tall, wide]
    rows = [jnp.broadcast_to(r, (1, z.C)) for r in rows]
    fill = z.extra - len(rows)
    extra = jnp.concatenate(rows + [jnp.zeros((fill, z.C), F32)], axis=0).astype(BF16)
    start, high = z.own + z.extra, z.own // z.Q
    for j in range(z.Q):
        out_ref[j, : z.own, :] = x_ref[...]
        out_ref[j, z.own : start, :] = extra
        for i in range(z.Q):
            out_ref[j, start:, i * z.L : (i + 1) * z.L] = cot_ref[
                i * high : (i + 1) * high, j * z.L : (j + 1) * z.L
            ]


def unpick(z, at, *refs):
    for m in range(z.Q):
        refs[z.Q][at[0] ^ m] = refs[m][...]


def pack(z, at, *refs):
    for m in range(z.Z):
        refs[z.Z][at[2] ^ m] = refs[m][0]
        refs[z.Z + 1][at[2] ^ m] = refs[m][1]


def shards(z, images, masks, cotangent, weights, first, second, params, p_first, p_second):
    q, s, b = lax.axis_index("q"), lax.axis_index("s"), lax.axis_index("z")
    at = jnp.stack([q, s, b]).astype(jnp.int32)

    def over_z(v, m):
        return lax.ppermute(v, "z", [(i, i ^ m) for i in range(z.Z)]) if m else v

    def over_s(v, m):
        return lax.ppermute(v, "s", [(i, i ^ m) for i in range(z.S)]) if m else v

    def plane(v):
        return lax.all_to_all(v, "q", 0, 0)

    def sharers(v):
        return lax.all_to_all(v, ("s", "z"), 0, 0)

    def over_q(v, m):
        return lax.ppermute(v, "q", [(i, i ^ m) for i in range(z.Q)]) if m else v

    def gather_z(w):
        return [over_z(w, m) for m in range(z.Z)]

    def fetch(w):
        own = []
        for m in range(z.Z):
            pairs = [
                ((a * z.S + c) * z.Z + e, (e * z.S + c) * z.Z + (a ^ m))
                for a in range(z.Q)
                for c in range(z.S)
                for e in range(z.Z)
            ]
            own.append(lax.ppermute(w, ("q", "s", "z"), pairs))
        return own

    def gather(a, b):
        if z.Q != 4:
            return [over_q(v, m) for v in (a, b) for m in range(z.Q)]
        a1, a2, b1, b2 = over_q(a, 1), over_q(a, 2), over_q(b, 1), over_q(b, 2)
        return [a, a1, a2, over_q(a2, 1), b, b1, b2, over_q(b1, 2)]

    def share(packed):
        return [over_s(packed, t) for t in range(z.S)]

    rows = z.own
    GL = (z.G, z.L)
    HL = (z.G // 2, z.L)
    many = z.S * z.Z
    piece = (z.K, z.IB, z.L)
    blocks = near((z.Z, *piece), BF16)
    stat = near((many, 8, LANES))
    conv_scratch = [pltpu.VMEM((z.C, z.K * z.LP), BF16), pltpu.VMEM((rows, z.K * z.LP), F32)]
    grad_scratch = [pltpu.VMEM((z.G, z.K * z.LP), BF16), pltpu.VMEM((z.C, z.K * z.LP), F32)]
    cot_rows = cotangent.reshape(rows, z.C)
    image_rows = images.reshape(rows, z.C)

    low = weights.astype(BF16)
    both = fetch(low)
    x_all = plane(
        call(
            functools.partial(extend, z),
            near((z.Q, z.sent, z.C), BF16),
            (image_rows, masks, cot_rows),
            far=(image_rows, masks, cot_rows),
        )
    )
    both, x_all = together((both, x_all))
    front_one, front_two = call(functools.partial(pack, z), [blocks] * 2, (at, *both))
    w_far = away((z.C, z.K * z.LP), BF16)
    x_far = away((z.Q, rows, z.C), BF16)
    z1, x_slice, cots, slice_params, hw, stats, w_far, x_far = call(
        functools.partial(first_conv, z),
        [
            near(GL),
            near(GL, BF16),
            near(GL, BF16),
            near((4, z.L)),
            near((z.n_group, 8, LANES)),
            stat,
            w_far,
            x_far,
        ],
        (at, params, x_all, *share(front_one)),
        conv_scratch + [pltpu.SemaphoreType.DMA((2,))],
        limit=16,
        raw=(w_far, x_far),
    )
    stats = sharers(stats)
    ha, hb, sum_one = call(
        functools.partial(hidden, z),
        [near(HL, BF16), near(HL, BF16), near((8, z.L))],
        (z1, stats, hw, slice_params),
    )
    ha, hb, front_two = together((ha, hb, front_two))
    hs = gather(ha, hb)
    h_far = away((z.Q, *GL), BF16)
    z2, stats, h_far, *back = call(
        functools.partial(second_conv, z),
        [near(GL), stat, h_far] + [near(piece, BF16)] * z.Q,
        (at, *hs, *share(front_two), hw),
        conv_scratch + [pltpu.VMEM((z.Q, *GL), BF16), pltpu.SemaphoreType.DMA],
        limit=16,
        raw=(h_far,),
    )
    stats, back = together((stats, back))
    stats, back = together((sharers(stats), [over_q(back[m], m) for m in range(z.Q)]))
    out, d, sum_two, stats = call(
        functools.partial(middle, z),
        [near((z.Q, rows, z.L), BF16), near(GL), near((8, z.L)), stat],
        (at, z2, stats, hw, slice_params, x_slice, cots),
    )
    da, db, grad_two = call(
        functools.partial(norm_grad, z, 2),
        [near(HL, BF16), near(HL, BF16), near((8, z.L))],
        (z2, d, sum_two, sharers(stats), hw, slice_params),
    )
    da, db, back = together((da, db, back))
    keep_two = call(functools.partial(unpick, z), near((z.Q, *piece), BF16), (at, *back))
    dz2s = gather(da, db)

    def kernel_gradient(feature, halves, **more):
        mine, *theirs = call(
            functools.partial(kernel_grad, z),
            [near((z.Q, *piece))] + [near(piece, BF16)] * (z.Q * (z.S - 1)),
            (at, feature, *halves),
            grad_scratch,
            limit=14,
            cost=COST_GRAD,
            far=(feature,),
            **more,
        )
        return mine, [over_s(theirs[(t - 1) * z.Q + r], t) for t in range(1, z.S) for r in range(z.Q)]

    def add_up(mine, received, *value):
        more = rows if value else 0
        return call(
            functools.partial(add_sharers, z),
            [near((z.K * z.IB + more, z.L), BF16)] * z.Q,
            (at, mine, *received, *value),
        )

    def by_plane(parts):
        return [over_q(parts[r], r) for r in range(z.Q)]

    def along(parts):
        return [over_z(parts[m], m) for m in range(z.Z)]

    parts_two = add_up(*kernel_gradient(h_far, (da, db)), out)
    da1, stats = call(
        functools.partial(hidden_grad, z),
        [near(GL), stat],
        (at, *dz2s, *share(keep_two), z1, sum_one, hw, slice_params),
        back_scratch(z),
        limit=16,
    )
    stats, parts_two = together((stats, parts_two))
    stats, parts_two = together((sharers(stats), by_plane(parts_two)))
    da, db, grad_one = call(
        functools.partial(norm_grad, z, 0),
        [near(HL, BF16), near(HL, BF16), near((8, z.L))],
        (z1, da1, sum_one, stats, hw, slice_params),
    )
    flat = near((z.K * z.IB, z.L), BF16)
    hold = pltpu.VMEM((z.Z, z.K * z.IB, z.L), BF16)
    *parts_two, values = call(
        functools.partial(route, z),
        [flat] * z.Z + [near((rows, z.C), BF16)],
        (at, *parts_two),
        [pltpu.VMEM((z.Q, rows, z.L), BF16), hold],
        after=(da,),
    )
    mine, received = kernel_gradient(x_far, (da, db))
    parts_one = add_up(mine, received)
    parts_one, parts_two = by_plane(parts_one), along(parts_two)
    parts_one, parts_two = together((parts_one, parts_two))
    dxs = call(
        functools.partial(input_part, z),
        [near((rows, z.C))] + [near((rows, z.C), BF16)] * (z.Q - 1),
        (at, da, db, w_far, d),
        [grad_scratch[0], pltpu.VMEM((z.Q, rows, z.C), F32)],
        limit=16,
        cost=COST_GRAD,
        far=(w_far,),
        after=(received[0],),
    )
    parts_one = call(functools.partial(route, z), [flat] * z.Z, (at, *parts_one), [hold], after=(dxs[0],))
    parts_one, dxs, parts_two = together((parts_one, dxs, parts_two))
    parts_one = along(parts_one)
    total_two = call(functools.partial(total_of, z), shape((z.K * z.IB, z.L)), tuple(parts_two))
    dxs = [over_q(dxs[m], m) for m in range(z.Q)]
    parts_one, dxs = together((parts_one, dxs))
    new_first, new_second, move, stats = call(
        functools.partial(moments, z),
        [shape(weights.shape)] * 2 + [near(weights.shape), near((z.R * z.Z, 8, LANES))],
        (*parts_one, total_two, weights, first, second, grad_one, grad_two),
        far=(total_two,),
    )
    stats = lax.all_to_all(stats, ("s", "q", "z"), 0, 0)
    dx = call(functools.partial(total_of, z), shape((rows, z.C), BF16), tuple(dxs))
    new_weights, copies, new_params, new_p_first, new_p_second, trust = call(
        functools.partial(finish, z),
        [shape(weights.shape), shape(weights.shape, BF16)] + [shape(params.shape)] * 3 + [shape((2, 6))],
        (stats, weights, move, params, p_first, p_second),
    )
    return (
        values.reshape(images.shape),
        dx.reshape(images.shape),
        new_weights,
        copies,
        new_first,
        new_second,
        new_params,
        new_p_first,
        new_p_second,
        trust,
    )


def solution(mesh):
    def whole(images, masks, cotangent, weights, first, second, params, p_first, p_second):
        z = Sizes(mesh, images.shape, weights.shape)
        inner = Mesh(mesh.devices.reshape(z.Q, z.S, z.Z), ("q", "s", "z"))
        pixels = P(("q", "s", "z"), None, None, None)
        kernels = P(None, None, ("q", "s"), "z")
        return jax.shard_map(
            functools.partial(shards, z),
            mesh=inner,
            in_specs=(pixels, P(("q", "s", "z"), None, None), pixels, kernels, kernels, kernels, P(), P(), P()),
            out_specs=(pixels, pixels, kernels, kernels, kernels, kernels, P(), P(), P(), P()),
            check_vma=False,
        )(images, masks, cotangent, weights, first, second, params, p_first, p_second)

    return whole
```

```python
import functools

import jax
import jax.numpy as jnp
from jax import lax
from jax.experimental import pallas as pl
from jax.experimental.pallas import tpu as pltpu
from jax.sharding import Mesh
from jax.sharding import PartitionSpec as P

STEP = 3
RATE = 0.5
DECAY = 0.01
BETA = 0.5
BIAS = 1.0 - BETA**STEP
EPS = 1e-05
TINY = 1e-06
ROOT = 0.7978845608028654
CUBE = 0.044715
LANES = 128
COST_GRAD = 3 * 10**9
F32 = jnp.float32
BF16 = jnp.bfloat16


def gelu(v):
    return 0.5 * v * (1.0 + jnp.tanh(ROOT * (v + CUBE * (v * v * v))))


def gelu_both(v):
    t = jnp.tanh(ROOT * (v + CUBE * (v * v * v)))
    value = 0.5 * v * (1.0 + t)
    slope = 0.5 * (1.0 + t) + 0.5 * v * (1.0 - t * t) * (ROOT * (1.0 + (3.0 * CUBE) * (v * v)))
    return value, slope


class Sizes:
    def __init__(self, mesh, images, weights):
        self.Z = mesh.shape["ba"]
        self.R = mesh.shape["ha"] * mesh.shape["wa"]
        self.Q = self.Z
        self.S = self.R // self.Q
        n, self.H, self.W, self.C = images
        self.n_own = n // (self.R * self.Z)
        self.own = self.n_own * self.H * self.W
        self.n_group = self.n_own * self.Q
        self.G = self.own * self.Q
        self.L = self.C // self.Q
        self.LP = max(self.L, LANES)
        self.IB = self.C // self.R
        self.K = weights[1]
        self.extra = 16 * ((2 * self.n_own + 15) // 16)
        self.sent = self.own + self.extra


def call(body, out_shape, args, scratch=(), limit=8, far=(), after=(), cost=1, raw=()):
    smem = [a.dtype == jnp.int32 and a.ndim == 1 for a in args]
    away = [any(a is f for f in far) for a in args]
    args = [
        a if m else pltpu.with_memory_space_constraint(a, pltpu.HBM if w else pltpu.VMEM)
        for a, m, w in zip(args, smem, away)
    ]
    n = len(args)

    def run(*refs):
        body(*refs[:n], *refs[n + len(after) :])

    return pl.pallas_call(
        run,
        out_shape=out_shape,
        in_specs=[pl.BlockSpec(memory_space=pltpu.SMEM if m else pltpu.VMEM) for m in smem]
        + [pl.BlockSpec(memory_space=pl.ANY)] * len(after),
        out_specs=jax.tree.map(
            lambda o: pl.BlockSpec(memory_space=pltpu.HBM if any(o is r for r in raw) else pltpu.VMEM),
            out_shape,
        ),
        scratch_shapes=list(scratch),
        compiler_params=pltpu.CompilerParams(vmem_limit_bytes=limit * 1024 * 1024),
        cost_estimate=pl.CostEstimate(flops=cost, bytes_accessed=1, transcendentals=0),
    )(*args, *after)


together = lax.optimization_barrier


def near(dims, dtype=F32):
    return pltpu.VMEM(tuple(dims), dtype)


def away(dims, dtype=F32):
    return pltpu.HBM(tuple(dims), dtype)


def shape(dims, dtype=F32):
    return jax.ShapeDtypeStruct(tuple(dims), dtype)


def image_mask(z, hw):
    dims = (z.H, z.W, z.L)
    rows = lax.broadcasted_iota(jnp.int32, dims, 0).astype(F32)
    cols = lax.broadcasted_iota(jnp.int32, dims, 1).astype(F32)
    tall = hw[0:1, : z.L].reshape(1, 1, z.L)
    wide = hw[1:2, : z.L].reshape(1, 1, z.L)
    return jnp.where((rows < tall) & (cols < wide), 1.0, 0.0).reshape(z.H * z.W, z.L)


def shifted_sum(z, taps, sign):
    dims = (z.n_own, z.H, z.W, z.L)
    cols = lax.broadcasted_iota(jnp.int32, dims, 2)
    total = None
    for c in range(3):
        column = None
        for r in range(3):
            part = taps(3 * r + c).reshape(dims)
            move = (r - 1) * sign
            if move == 1:
                part = jnp.concatenate([part[:, 1:], jnp.zeros_like(part[:, :1])], axis=1)
            elif move == -1:
                part = jnp.concatenate([jnp.zeros_like(part[:, :1]), part[:, :-1]], axis=1)
            column = part if column is None else column + part
        move = (c - 1) * sign
        if move:
            flat = column.reshape(z.n_own * z.H, z.W, z.L)
            flat = pltpu.roll(flat, (-move) % z.W, 1)
            column = flat.reshape(dims)
            edge = z.W - 1 if move == 1 else 0
            column = jnp.where(cols == edge, 0.0, column)
        total = column if total is None else total + column
    return total.reshape(z.own, z.L)


def moved_taps(z, feature):
    dims = (z.n_own, z.H, z.W, z.L)
    cols = lax.broadcasted_iota(jnp.int32, dims, 2)
    out = [None] * 9
    for c in range(3):
        move = 1 - c
        column = feature.reshape(dims)
        if move:
            flat = feature.reshape(z.n_own * z.H, z.W, z.L)
            column = pltpu.roll(flat, (-move) % z.W, 1).reshape(dims)
            edge = z.W - 1 if move == 1 else 0
            column = jnp.where(cols == edge, 0.0, column)
        for r in range(3):
            if r == 0:
                part = jnp.concatenate([column[:, 1:], jnp.zeros_like(column[:, :1])], axis=1)
            elif r == 2:
                part = jnp.concatenate([jnp.zeros_like(column[:, :1]), column[:, :-1]], axis=1)
            else:
                part = column
            out[3 * r + c] = part.reshape(z.own, z.L)
    return out


def fill_moved(z, a_ref, b_ref, moved_ref):
    half = z.Q // 2
    for j in range(z.Q):
        ref, at_row = (a_ref, j) if j < half else (b_ref, j - half)
        block = ref[at_row * z.own : (at_row + 1) * z.own, :].astype(F32)
        for k, part in enumerate(moved_taps(z, block)):
            moved_ref[j * z.own : (j + 1) * z.own, k * z.LP : k * z.LP + z.L] = part.astype(BF16)


def spread(ref, rows):
    used = rows[0].shape[1]
    if len(rows) < 8:
        rows = rows + [jnp.zeros((8 - len(rows), used), F32)]
    stat = jnp.concatenate(rows, axis=0)
    if used < LANES:
        stat = jnp.concatenate([stat, jnp.zeros((8, LANES - used), F32)], axis=1)
    for k in range(ref.shape[0]):
        ref[k] = stat


def local_stats(z, z_ref, hw_ref, stats_ref):
    px = z.H * z.W

    def first(n, carry):
        count, total = carry
        mask = image_mask(z, hw_ref[n])
        block = z_ref[pl.ds(pl.multiple_of(n * px, px), px), :]
        return count + jnp.sum(mask, 0, keepdims=True), total + jnp.sum(mask * block, 0, keepdims=True)

    zero = jnp.zeros((1, z.L), F32)
    count, total = lax.fori_loop(0, z.n_group, first, (zero, zero), unroll=4)
    mean = total / count

    def second(n, spread_sum):
        mask = image_mask(z, hw_ref[n])
        centered = z_ref[pl.ds(pl.multiple_of(n * px, px), px), :] - mean
        return spread_sum + jnp.sum(mask * centered * centered, 0, keepdims=True)

    squares = lax.fori_loop(0, z.n_group, second, zero, unroll=4)
    spread(stats_ref, [count, mean, squares])


def conv_into(z, product, y_ref, z_ref, sign=1, at_q=0):
    for j in range(z.Q):
        y_ref[...] = product(j)
        z_ref[pl.ds(pl.multiple_of((at_q ^ j) * z.own, z.own), z.own), :] = shifted_sum(
            z, lambda k: y_ref[:, k * z.LP : k * z.LP + z.L], sign
        )


def fill_kernels(z, at, blocks, wcat):
    for t, block in enumerate(blocks):
        s = at[1] ^ t
        for a in range(z.Z):
            row = pl.multiple_of(a * z.L + s * z.IB, z.IB)
            for k in range(z.K):
                wcat[pl.ds(row, z.IB), k * z.LP : k * z.LP + z.L] = block[a, k]


def first_conv(z, at, np_ref, *refs):
    xs, refs = refs[: z.Q], refs[z.Q :]
    blocks, refs = refs[: z.S], refs[z.S :]
    z_ref, slice_ref, par_ref, hw_ref, stats_ref, far_w, far_x, wcat, y_ref, sem = refs
    fill_kernels(z, at, blocks, wcat)
    copies = [pltpu.make_async_copy(wcat, far_w, sem.at[0])]
    for m in range(z.Q):
        copies.append(
            pltpu.make_async_copy(xs[m].at[: z.own, :], far_x.at[at[0] ^ m], sem.at[1 + m])
        )
    for copy in copies:
        copy.start()
    for m in range(z.Q):
        j = at[0] ^ m
        for n in range(z.n_own):
            row = z.own + 2 * n
            two = xs[m][row : row + 2, :LANES].astype(F32)
            hw_ref[j * z.n_own + n] = jnp.concatenate([two, jnp.zeros((6, LANES), F32)], axis=0)
    for slot in range(z.Q):

        @pl.when(at[0] == slot)
        def _(slot=slot):
            par_ref[...] = np_ref[:, slot * z.L : (slot + 1) * z.L]
            for m in range(z.Q):
                j = slot ^ m
                slice_ref[j * z.own : (j + 1) * z.own, :] = xs[m][
                    : z.own, slot * z.L : (slot + 1) * z.L
                ]

    def product(m):
        return jnp.dot(xs[m][: z.own, :], wcat[...], preferred_element_type=F32)

    conv_into(z, product, y_ref, z_ref, 1, at[0])
    local_stats(z, z_ref, hw_ref, stats_ref)
    for copy in copies:
        copy.wait()


def gathered(z, at, parts, hold):
    half = z.G // 2
    for m in range(z.Q):
        hold[at[0] ^ m, :half] = parts[m][...]
        hold[at[0] ^ m, half:] = parts[z.Q + m][...]


def second_conv(z, at, *refs):
    hs, refs = refs[: 2 * z.Q], refs[2 * z.Q :]
    blocks, refs = refs[: z.S], refs[z.S :]
    hw_ref, z_ref, stats_ref, far_ref, wcat, y_ref, h_ref, sem = refs
    gathered(z, at, hs, h_ref)
    copy = pltpu.make_async_copy(h_ref, far_ref, sem)
    copy.start()
    fill_kernels(z, at, blocks, wcat)

    def product(j):
        rows = slice(j * z.own, (j + 1) * z.own)
        if z.L % LANES == 0:
            whole = jnp.concatenate([h_ref[i, rows, :] for i in range(z.Q)], axis=1)
            return jnp.dot(whole, wcat[...], preferred_element_type=F32)
        return sum(
            jnp.dot(h_ref[i, rows, :], wcat[i * z.L : (i + 1) * z.L, :], preferred_element_type=F32)
            for i in range(z.Q)
        )

    conv_into(z, product, y_ref, z_ref)
    local_stats(z, z_ref, hw_ref, stats_ref)
    copy.wait()


def merged(z, all_ref):
    counts = [all_ref[k, 0:1, : z.L] for k in range(z.S * z.Z)]
    means = [all_ref[k, 1:2, : z.L] for k in range(z.S * z.Z)]
    count = sum(counts)
    mean = sum(c * m for c, m in zip(counts, means)) / count
    squares = sum(
        all_ref[k, 2:3, : z.L] + counts[k] * (means[k] - mean) * (means[k] - mean)
        for k in range(z.S * z.Z)
    )
    return mean, lax.rsqrt(squares / count + EPS), count


def keep(ref, rows):
    used = rows[0].shape[1]
    ref[...] = jnp.concatenate(rows + [jnp.zeros((8 - len(rows), used), F32)], axis=0)


def over_images(z, step, init=0, unroll=2):
    px = z.H * z.W

    def one(n, carry):
        return step(n, pl.ds(pl.multiple_of(n * px, px), px), carry)

    return lax.fori_loop(0, z.n_group, one, init, unroll=unroll)


def over_halves(z, step, refs):
    px, count = z.H * z.W, z.n_group // 2
    for i, ref in enumerate(refs):

        def one(n, carry, i=i, ref=ref):
            rows = pl.ds(pl.multiple_of((i * count + n) * px, px), px)
            ref[pl.ds(pl.multiple_of(n * px, px), px), :] = step(i * count + n, rows)
            return carry

        lax.fori_loop(0, count, one, 0, unroll=2)


def hidden(z, z_ref, all_ref, hw_ref, par_ref, a_ref, b_ref, sum_ref):
    mean, inv, count = merged(z, all_ref)
    keep(sum_ref, [mean, inv, count])
    gain, shift = par_ref[0:1, :], par_ref[1:2, :]

    def step(n, rows):
        mask = image_mask(z, hw_ref[n])
        return gelu(mask * (gain * ((z_ref[rows, :] - mean) * inv) + shift)).astype(BF16)

    over_halves(z, step, (a_ref, b_ref))


def middle(z, at, z_ref, all_ref, hw_ref, par_ref, x_ref, *refs):
    cot_ref, out_ref, d_ref, sum_ref, stats_ref = refs
    mean, inv, count = merged(z, all_ref)
    keep(sum_ref, [mean, inv, count])
    gain, shift = par_ref[2:3, :], par_ref[3:4, :]
    px = z.H * z.W
    carry = (jnp.zeros((1, z.L), F32), jnp.zeros((1, z.L), F32))
    for j in range(z.Q):

        def step(n, carry, j=j):
            local = pl.ds(pl.multiple_of(n * px, px), px)
            rows = pl.ds(pl.multiple_of(j * z.own + n * px, px), px)
            mask = image_mask(z, hw_ref[j * z.n_own + n])
            normed = (z_ref[rows, :] - mean) * inv
            summed = mask * (gain * normed + shift) + x_ref[rows, :].astype(F32)
            value, slope = gelu_both(summed)
            out_ref[j, local, :] = value.astype(BF16)
            d = cot_ref[rows, :].astype(F32) * slope
            d_ref[rows, :] = d
            masked = mask * d
            return (
                carry[0] + jnp.sum(masked, 0, keepdims=True),
                carry[1] + jnp.sum(masked * normed, 0, keepdims=True),
            )

        carry = lax.fori_loop(0, z.n_own, step, carry, unroll=2)
    spread(stats_ref, list(carry))


def norm_grad(z, row, z_ref, up_ref, sum_ref, all_ref, hw_ref, par_ref, a_ref, b_ref, par_grad_ref):
    mean, inv, count = sum_ref[0:1, :], sum_ref[1:2, :], sum_ref[2:3, :]
    shift_grad = sum(all_ref[k, 0:1, : z.L] for k in range(z.S * z.Z))
    gain_grad = sum(all_ref[k, 1:2, : z.L] for k in range(z.S * z.Z))
    keep(par_grad_ref, [gain_grad, shift_grad])
    gain = par_ref[row : row + 1, :]

    def step(n, rows):
        mask = image_mask(z, hw_ref[n])
        normed = (z_ref[rows, :] - mean) * inv
        grad = inv * mask * gain * (up_ref[rows, :] - (shift_grad + normed * gain_grad) / count)
        return grad.astype(BF16)

    over_halves(z, step, (a_ref, b_ref))


def back_product(z, at, dz_ref, blocks, wcat):
    for t, block in enumerate(blocks):
        s = at[1] ^ t
        for b in range(z.Z):
            for k in range(z.K):
                rows = pl.ds(pl.multiple_of(k * z.LP + s * z.IB, z.IB), z.IB)
                if z.L % LANES == 0:
                    wcat[0, rows, b * z.L : (b + 1) * z.L] = block[b, k]
                else:
                    wcat[b, rows, :] = block[b, k]
    contract = (((1,), (1,)), ((), ()))

    def product(j):
        rows = slice(j * z.own, (j + 1) * z.own)
        if z.L % LANES == 0:
            whole = jnp.concatenate([dz_ref[i, rows, :] for i in range(z.Q)], axis=1)
            return lax.dot_general(whole, wcat[0], contract, preferred_element_type=F32)
        return sum(
            lax.dot_general(dz_ref[i, rows, :], wcat[i], contract, preferred_element_type=F32)
            for i in range(z.Q)
        )

    return product


def back_scratch(z):
    if z.L % LANES == 0:
        wide = pltpu.VMEM((1, z.K * z.LP, z.C), BF16)
    else:
        wide = pltpu.VMEM((z.Z, z.K * z.LP, z.C // z.Z), BF16)
    return [wide, pltpu.VMEM((z.own, z.K * z.LP), F32), pltpu.VMEM((z.Q, z.G, z.L), BF16)]


def hidden_grad(z, at, *refs):
    dzs, refs = refs[: 2 * z.Q], refs[2 * z.Q :]
    blocks, refs = refs[: z.S], refs[z.S :]
    z_ref, sum_ref, hw_ref, par_ref, da_ref, stats_ref, wcat, y_ref, dz_ref = refs
    gathered(z, at, dzs, dz_ref)
    conv_into(z, back_product(z, at, dz_ref, blocks, wcat), y_ref, da_ref, -1)
    mean, inv = sum_ref[0:1, :], sum_ref[1:2, :]
    gain, shift = par_ref[0:1, :], par_ref[1:2, :]

    def step(n, rows, carry):
        mask = image_mask(z, hw_ref[n])
        normed = (z_ref[rows, :] - mean) * inv
        da = da_ref[rows, :] * gelu_both(mask * (gain * normed + shift))[1]
        da_ref[rows, :] = da
        masked = mask * da
        return (
            carry[0] + jnp.sum(masked, 0, keepdims=True),
            carry[1] + jnp.sum(masked * normed, 0, keepdims=True),
        )

    zero = jnp.zeros((1, z.L), F32)
    spread(stats_ref, list(over_images(z, step, (zero, zero))))


def input_part(z, at, a_ref, b_ref, w_ref, d_ref, *refs):
    outs, (moved_ref, dx_ref) = refs[: z.Q], refs[z.Q :]
    fill_moved(z, a_ref, b_ref, moved_ref)
    contract = (((1,), (1,)), ((), ()))
    for j in range(z.Q):
        rows = slice(j * z.own, (j + 1) * z.own)
        dx_ref[j] = lax.dot_general(moved_ref[rows, :], w_ref[...], contract, preferred_element_type=F32)
    for slot in range(z.Q):

        @pl.when(at[0] == slot)
        def _(slot=slot):
            for j in range(z.Q):
                lanes = slice(slot * z.L, (slot + 1) * z.L)
                dx_ref[j, :, lanes] = dx_ref[j, :, lanes] + d_ref[j * z.own : (j + 1) * z.own, :]

    for m in range(z.Q):
        outs[m][...] = dx_ref[at[0] ^ m].astype(outs[m].dtype)


def kernel_grad(z, at, f_ref, a_ref, b_ref, mine_ref, *refs):
    theirs, (moved_ref, full_ref) = refs[:-2], refs[-2:]
    fill_moved(z, a_ref, b_ref, moved_ref)
    contract = (((0,), (0,)), ((), ()))
    if f_ref.shape[2] == z.C:
        whole = f_ref[...].reshape(z.G, z.C)
        full_ref[...] = lax.dot_general(whole, moved_ref[...], contract, preferred_element_type=F32)
    elif z.L % LANES == 0:
        whole = jnp.concatenate([f_ref[i] for i in range(z.Q)], axis=1)
        full_ref[...] = lax.dot_general(whole, moved_ref[...], contract, preferred_element_type=F32)
    else:
        for i in range(z.Q):
            full_ref[i * z.L : (i + 1) * z.L, :] = lax.dot_general(
                f_ref[i], moved_ref[...], contract, preferred_element_type=F32
            )
    for r in range(z.Q):
        for t in range(z.S):
            row = pl.multiple_of((at[0] ^ r) * z.L + (at[1] ^ t) * z.IB, z.IB)
            for k in range(z.K):
                part = full_ref[pl.ds(row, z.IB), k * z.LP : k * z.LP + z.L]
                if t == 0:
                    mine_ref[r, k] = part
                else:
                    theirs[(t - 1) * z.Q + r][k] = part.astype(BF16)


def add_sharers(z, at, *refs):
    count = 1 + z.Q * (z.S - 1)
    mine_ref, others, refs = refs[0], refs[1:count], refs[count:]
    value_ref = None
    if len(refs) > z.Q:
        value_ref, refs = refs[0], refs[1:]
    for r in range(z.Q):
        for k in range(z.K):
            total = mine_ref[r, k]
            for other in others[r :: z.Q]:
                total = total + other[k].astype(F32)
            refs[r][k * z.IB : (k + 1) * z.IB, :] = total.astype(BF16)
        if value_ref is not None:
            refs[r][z.K * z.IB :, :] = value_ref[at[0] ^ r]


def route(z, at, *refs):
    parts, refs = refs[: z.Q], refs[z.Q :]
    outs, refs = refs[: z.Z], refs[z.Z :]
    hold = refs[-1]
    for r in range(z.Q):
        hold[at[2] ^ at[0] ^ r] = parts[r][: z.K * z.IB, :]
    for m in range(z.Z):
        outs[m][...] = hold[m]
    if len(refs) == 3:
        value_ref, slots, _ = refs
        for r in range(z.Q):
            slots[at[0] ^ r] = parts[r][z.K * z.IB :, :]
        for j in range(z.Q):
            value_ref[:, j * z.L : (j + 1) * z.L] = slots[j]


def total_of(z, *refs):
    refs[-1][...] = sum(ref[...].astype(F32) for ref in refs[:-1]).astype(refs[-1].dtype)


def direction_of(grad, first, second, param, decay):
    new_first = BETA * first + (1.0 - BETA) * grad
    new_second = BETA * second + (1.0 - BETA) * grad * grad
    move = new_first / BIAS / (jnp.sqrt(new_second / BIAS) + TINY) + decay * param
    return new_first, new_second, move


def moments(z, *refs):
    parts = [refs[: z.Z], refs[z.Z : z.Z + 1]]
    refs = refs[z.Z + 1 :]
    w_ref, first_ref, second_ref, g1_ref, g2_ref, nf_ref, ns_ref, u_ref, stats_ref = refs
    rows = []
    weight_rows = []
    for j in range(2):
        total_u = jnp.zeros((1, z.L), F32)
        total_w = jnp.zeros((1, z.L), F32)
        for k in range(z.K):
            grad = sum(part[k * z.IB : (k + 1) * z.IB, :].astype(F32) for part in parts[j])
            w = w_ref[j, k]
            nf, ns, u = direction_of(grad, first_ref[j, k], second_ref[j, k], w, DECAY)
            nf_ref[j, k] = nf
            ns_ref[j, k] = ns
            u_ref[j, k] = u
            total_u = total_u + jnp.sum(u * u, 0, keepdims=True)
            total_w = total_w + jnp.sum(w * w, 0, keepdims=True)
        rows.append(total_u)
        weight_rows.append(total_w)
    spread(
        stats_ref,
        rows + weight_rows + [g1_ref[0:1, :], g1_ref[1:2, :], g2_ref[0:1, :], g2_ref[1:2, :]],
    )


def finish(z, all_ref, w_ref, u_ref, np_ref, nf_ref, ns_ref, *outs):
    nw_ref, copy_ref, nnp_ref, nnf_ref, nns_ref, trust_ref = outs
    total = all_ref[0]
    for k in range(1, z.R * z.Z):
        total = total + all_ref[k]
    tops, bottoms = [], []
    for j in range(2):
        un = jnp.sqrt(jnp.sum(total[j : j + 1, : z.L], axis=1, keepdims=True))
        wn = jnp.sqrt(jnp.sum(total[2 + j : 3 + j, : z.L], axis=1, keepdims=True))
        tops.append(wn)
        bottoms.append(un)
        scale = RATE * (wn / (un + TINY))
        for k in range(z.K):
            new = w_ref[j, k] - scale * u_ref[j, k]
            nw_ref[j, k] = new
            copy_ref[j, k] = new.astype(BF16)
    for j in range(z.Q):
        nnp_ref[:, j * z.L : (j + 1) * z.L] = all_ref[j * z.Z, 4:8, : z.L]
    param = np_ref[...]
    nf, ns, move = direction_of(nnp_ref[...], nf_ref[...], ns_ref[...], param, 0.0)
    nnf_ref[...] = nf
    nns_ref[...] = ns
    pn = jnp.sqrt(jnp.sum(param * param, axis=1, keepdims=True))
    qn = jnp.sqrt(jnp.sum(move * move, axis=1, keepdims=True))
    nnp_ref[...] = param - RATE * (pn / (qn + TINY)) * move
    for r in range(4):
        tops.append(pn[r : r + 1])
        bottoms.append(qn[r : r + 1])
    at_row = lax.broadcasted_iota(jnp.int32, (2, 6), 0)
    at_col = lax.broadcasted_iota(jnp.int32, (2, 6), 1)
    trust = jnp.zeros((2, 6), F32)
    for c in range(6):
        trust = jnp.where(at_col == c, jnp.where(at_row == 0, tops[c], bottoms[c]), trust)
    trust_ref[...] = trust


def extend(z, x_ref, valid_ref, out_ref):
    rows = []
    for n in range(z.n_own):
        valid = valid_ref[n].astype(F32)
        tall = jnp.sum(valid[:, 0:1], axis=0, keepdims=True)
        wide = jnp.sum(valid[0:1, :], axis=1, keepdims=True)
        rows += [tall, wide]
    rows = [jnp.broadcast_to(r, (1, z.C)) for r in rows]
    fill = z.extra - len(rows)
    extra = jnp.concatenate(rows + [jnp.zeros((fill, z.C), F32)], axis=0).astype(BF16)
    out_ref[: z.own, :] = x_ref[...]
    out_ref[z.own :, :] = extra


def pick(z, more, at, *refs):
    parts, refs = refs[: z.Z], refs[z.Z :]
    map_ref = None
    if more == "map":
        map_ref, refs = refs[0], refs[1:]
    if more == "keep":
        far_ref, outs, (hold, sem) = refs[0], refs[1:-2], refs[-2:]
    else:
        outs, hold = refs[:-1], refs[-1]
    for m in range(z.Z):
        hold[at[2] ^ m] = parts[m][...]
    if more == "keep":
        copy = pltpu.make_async_copy(hold, far_ref, sem)
        copy.start()
    for m in range(z.Q):
        for k in range(z.K):
            outs[m][k * z.IB : (k + 1) * z.IB, :] = hold[at[0] ^ m, k]
        if map_ref is not None:
            for slot in range(z.Q):

                @pl.when((at[0] ^ m) == slot)
                def _(m=m, slot=slot):
                    outs[m][z.K * z.IB :, :] = map_ref[:, slot * z.L : (slot + 1) * z.L]

    if more == "keep":
        copy.wait()


def unpick(z, at, *refs):
    parts, refs = refs[: z.Q], refs[z.Q :]
    for m in range(z.Q):
        q = at[0] ^ m
        for k in range(z.K):
            refs[0][q, k] = parts[m][k * z.IB : (k + 1) * z.IB, :]
        if len(refs) > 1:
            refs[1][pl.ds(pl.multiple_of(q * z.own, z.own), z.own), :] = parts[m][z.K * z.IB :, :]


def shards(z, images, masks, cotangent, weights, first, second, params, p_first, p_second):
    q, s, b = lax.axis_index("q"), lax.axis_index("s"), lax.axis_index("z")
    at = jnp.stack([q, s, b]).astype(jnp.int32)

    def over_z(v, m):
        return lax.ppermute(v, "z", [(i, i ^ m) for i in range(z.Z)]) if m else v

    def over_s(v, m):
        return lax.ppermute(v, "s", [(i, i ^ m) for i in range(z.S)]) if m else v

    def sharers(v):
        return lax.all_to_all(v, ("s", "z"), 0, 0)

    def over_q(v, m):
        return lax.ppermute(v, "q", [(i, i ^ m) for i in range(z.Q)]) if m else v

    def gather_z(w):
        return [over_z(w, m) for m in range(z.Z)]

    def gather(a, b):
        if z.Q != 4:
            return [over_q(v, m) for v in (a, b) for m in range(z.Q)]
        a1, a2, b1, b2 = over_q(a, 1), over_q(a, 2), over_q(b, 1), over_q(b, 2)
        return [a, a1, a2, over_q(a2, 1), b, b1, b2, over_q(b1, 2)]

    def share(packed):
        return [over_s(packed, t) for t in range(z.S)]

    rows = z.own
    GL = (z.G, z.L)
    HL = (z.G // 2, z.L)
    many = z.S * z.Z
    piece = (z.K, z.IB, z.L)
    blocks = near((z.Z, *piece), BF16)
    stat = near((many, 8, LANES))
    conv_scratch = [pltpu.VMEM((z.C, z.K * z.LP), BF16), pltpu.VMEM((rows, z.K * z.LP), F32)]
    grad_scratch = [pltpu.VMEM((z.G, z.K * z.LP), BF16), pltpu.VMEM((z.C, z.K * z.LP), F32)]
    cot_rows = cotangent.reshape(rows, z.C)
    image_rows = images.reshape(rows, z.C)

    low_one, low_two = (weights[j].astype(BF16) for j in range(2))
    one = [over_z(low_one, m) for m in range(z.Z)]
    x_sent = call(
        functools.partial(extend, z),
        near((z.sent, z.C), BF16),
        (image_rows, masks),
        far=(image_rows, masks),
    )
    xs = [over_q(x_sent, m) for m in range(z.Q)]
    one, xs, low_two = together((one, xs, low_two))
    hold = pltpu.VMEM((z.Z, *piece), BF16)
    picked = call(
        functools.partial(pick, z, "map"),
        [near((z.K * z.IB + rows, z.L), BF16)] * z.Q,
        (at, *one, cot_rows),
        [hold],
        far=(cot_rows,),
    )
    two = [over_z(low_two, m) for m in range(z.Z)]
    picked, two = together(([over_q(picked[m], m) for m in range(z.Q)], two))
    front_one, cots = call(functools.partial(unpick, z), [blocks, near(GL, BF16)], (at, *picked))
    keep = away((z.Z, *piece), BF16)
    keep_two, *picked = call(
        functools.partial(pick, z, "keep"),
        [keep] + [near((z.K * z.IB, z.L), BF16)] * z.Q,
        (at, *two),
        [hold, pltpu.SemaphoreType.DMA],
        raw=(keep,),
    )
    w_far = away((z.C, z.K * z.LP), BF16)
    x_far = away((z.Q, rows, z.C), BF16)
    z1, x_slice, slice_params, hw, stats, w_far, x_far = call(
        functools.partial(first_conv, z),
        [
            near(GL),
            near(GL, BF16),
            near((4, z.L)),
            near((z.n_group, 8, LANES)),
            stat,
            w_far,
            x_far,
        ],
        (at, params, *xs, *share(front_one)),
        conv_scratch + [pltpu.SemaphoreType.DMA((1 + z.Q,))],
        limit=16,
        raw=(w_far, x_far),
    )
    stats, picked = together((stats, picked))
    stats, picked = together((sharers(stats), [over_q(picked[m], m) for m in range(z.Q)]))
    ha, hb, sum_one = call(
        functools.partial(hidden, z),
        [near(HL, BF16), near(HL, BF16), near((8, z.L))],
        (z1, stats, hw, slice_params),
    )
    ha, hb, picked = together((ha, hb, picked))
    hs = gather(ha, hb)
    front_two = call(functools.partial(unpick, z), [blocks], (at, *picked))[0]
    h_far = away((z.Q, *GL), BF16)
    z2, stats, h_far = call(
        functools.partial(second_conv, z),
        [near(GL), stat, h_far],
        (at, *hs, *share(front_two), hw),
        conv_scratch + [pltpu.VMEM((z.Q, *GL), BF16), pltpu.SemaphoreType.DMA],
        limit=16,
        raw=(h_far,),
    )
    out, d, sum_two, stats = call(
        functools.partial(middle, z),
        [near((z.Q, rows, z.L), BF16), near(GL), near((8, z.L)), stat],
        (at, z2, sharers(stats), hw, slice_params, x_slice, cots),
    )
    da, db, grad_two = call(
        functools.partial(norm_grad, z, 2),
        [near(HL, BF16), near(HL, BF16), near((8, z.L))],
        (z2, d, sum_two, sharers(stats), hw, slice_params),
    )
    da, db, keep_two = together((da, db, keep_two))
    dz2s = gather(da, db)

    def kernel_gradient(feature, halves, **more):
        mine, *theirs = call(
            functools.partial(kernel_grad, z),
            [near((z.Q, *piece))] + [near(piece, BF16)] * (z.Q * (z.S - 1)),
            (at, feature, *halves),
            grad_scratch,
            limit=14,
            cost=COST_GRAD,
            far=(feature,),
            **more,
        )
        return mine, [over_s(theirs[(t - 1) * z.Q + r], t) for t in range(1, z.S) for r in range(z.Q)]

    def add_up(mine, received, *value):
        more = rows if value else 0
        return call(
            functools.partial(add_sharers, z),
            [near((z.K * z.IB + more, z.L), BF16)] * z.Q,
            (at, mine, *received, *value),
        )

    def by_plane(parts):
        return [over_q(parts[r], r) for r in range(z.Q)]

    def along(parts):
        return [over_z(parts[m], m) for m in range(z.Z)]

    parts_two = add_up(*kernel_gradient(h_far, (da, db)), out)
    da1, stats = call(
        functools.partial(hidden_grad, z),
        [near(GL), stat],
        (at, *dz2s, *share(keep_two), z1, sum_one, hw, slice_params),
        back_scratch(z),
        limit=16,
    )
    stats, parts_two = together((stats, parts_two))
    stats, parts_two = together((sharers(stats), by_plane(parts_two)))
    da, db, grad_one = call(
        functools.partial(norm_grad, z, 0),
        [near(HL, BF16), near(HL, BF16), near((8, z.L))],
        (z1, da1, sum_one, stats, hw, slice_params),
    )
    flat = near((z.K * z.IB, z.L), BF16)
    hold = pltpu.VMEM((z.Z, z.K * z.IB, z.L), BF16)
    *parts_two, values = call(
        functools.partial(route, z),
        [flat] * z.Z + [near((rows, z.C), BF16)],
        (at, *parts_two),
        [pltpu.VMEM((z.Q, rows, z.L), BF16), hold],
        after=(da,),
    )
    mine, received = kernel_gradient(x_far, (da, db))
    parts_one = add_up(mine, received)
    parts_one, parts_two = by_plane(parts_one), along(parts_two)
    parts_one, parts_two = together((parts_one, parts_two))
    dxs = call(
        functools.partial(input_part, z),
        [near((rows, z.C))] + [near((rows, z.C), BF16)] * (z.Q - 1),
        (at, da, db, w_far, d),
        [grad_scratch[0], pltpu.VMEM((z.Q, rows, z.C), F32)],
        limit=16,
        cost=COST_GRAD,
        far=(w_far,),
        after=(received[0],),
    )
    parts_one = call(functools.partial(route, z), [flat] * z.Z, (at, *parts_one), [hold], after=(dxs[0],))
    parts_one, dxs, parts_two = together((parts_one, dxs, parts_two))
    parts_one = along(parts_one)
    total_two = call(functools.partial(total_of, z), shape((z.K * z.IB, z.L)), tuple(parts_two))
    dxs = [over_q(dxs[m], m) for m in range(z.Q)]
    parts_one, dxs = together((parts_one, dxs))
    new_first, new_second, move, stats = call(
        functools.partial(moments, z),
        [shape(weights.shape)] * 2 + [near(weights.shape), near((z.R * z.Z, 8, LANES))],
        (*parts_one, total_two, weights, first, second, grad_one, grad_two),
        far=(total_two,),
    )
    stats = lax.all_to_all(stats, ("s", "q", "z"), 0, 0)
    dx = call(functools.partial(total_of, z), shape((rows, z.C), BF16), tuple(dxs))
    new_weights, copies, new_params, new_p_first, new_p_second, trust = call(
        functools.partial(finish, z),
        [shape(weights.shape), shape(weights.shape, BF16)] + [shape(params.shape)] * 3 + [shape((2, 6))],
        (stats, weights, move, params, p_first, p_second),
    )
    return (
        values.reshape(images.shape),
        dx.reshape(images.shape),
        new_weights,
        copies,
        new_first,
        new_second,
        new_params,
        new_p_first,
        new_p_second,
        trust,
    )


def solution(mesh):
    def whole(images, masks, cotangent, weights, first, second, params, p_first, p_second):
        z = Sizes(mesh, images.shape, weights.shape)
        inner = Mesh(mesh.devices.reshape(z.Q, z.S, z.Z), ("q", "s", "z"))
        pixels = P(("q", "s", "z"), None, None, None)
        kernels = P(None, None, ("q", "s"), "z")
        return jax.shard_map(
            functools.partial(shards, z),
            mesh=inner,
            in_specs=(pixels, P(("q", "s", "z"), None, None), pixels, kernels, kernels, kernels, P(), P(), P()),
            out_specs=(pixels, pixels, kernels, kernels, kernels, kernels, P(), P(), P(), P()),
            check_vma=False,
        )(images, masks, cotangent, weights, first, second, params, p_first, p_second)

    return whole
```

```python
import functools

import jax
import jax.numpy as jnp
from jax import lax
from jax.experimental import pallas as pl
from jax.experimental.pallas import tpu as pltpu
from jax.sharding import Mesh
from jax.sharding import PartitionSpec as P

STEP = 3
RATE = 0.5
DECAY = 0.01
BETA = 0.5
BIAS = 1.0 - BETA**STEP
EPS = 1e-05
TINY = 1e-06
ROOT = 0.7978845608028654
CUBE = 0.044715
LANES = 128
COST_GRAD = 3 * 10**9
F32 = jnp.float32
BF16 = jnp.bfloat16


def gelu(v):
    return 0.5 * v * (1.0 + jnp.tanh(ROOT * (v + CUBE * (v * v * v))))


def gelu_both(v):
    t = jnp.tanh(ROOT * (v + CUBE * (v * v * v)))
    value = 0.5 * v * (1.0 + t)
    slope = 0.5 * (1.0 + t) + 0.5 * v * (1.0 - t * t) * (ROOT * (1.0 + (3.0 * CUBE) * (v * v)))
    return value, slope


class Sizes:
    def __init__(self, mesh, images, weights):
        self.Z = mesh.shape["ba"]
        self.R = mesh.shape["ha"] * mesh.shape["wa"]
        self.Q = self.Z
        self.S = self.R // self.Q
        n, self.H, self.W, self.C = images
        self.n_own = n // (self.R * self.Z)
        self.own = self.n_own * self.H * self.W
        self.n_group = self.n_own * self.Q
        self.G = self.own * self.Q
        self.L = self.C // self.Q
        self.LP = max(self.L, LANES)
        self.IB = self.C // self.R
        self.K = weights[1]
        self.extra = 16 * ((2 * self.n_own + 15) // 16)
        self.sent = self.K * self.IB + self.own + self.extra


def call(body, out_shape, args, scratch=(), limit=8, far=(), after=(), cost=1, raw=()):
    smem = [a.dtype == jnp.int32 and a.ndim == 1 for a in args]
    away = [any(a is f for f in far) for a in args]
    args = [
        a if m else pltpu.with_memory_space_constraint(a, pltpu.HBM if w else pltpu.VMEM)
        for a, m, w in zip(args, smem, away)
    ]
    n = len(args)

    def run(*refs):
        body(*refs[:n], *refs[n + len(after) :])

    return pl.pallas_call(
        run,
        out_shape=out_shape,
        in_specs=[pl.BlockSpec(memory_space=pltpu.SMEM if m else pltpu.VMEM) for m in smem]
        + [pl.BlockSpec(memory_space=pl.ANY)] * len(after),
        out_specs=jax.tree.map(
            lambda o: pl.BlockSpec(memory_space=pltpu.HBM if any(o is r for r in raw) else pltpu.VMEM),
            out_shape,
        ),
        scratch_shapes=list(scratch),
        compiler_params=pltpu.CompilerParams(vmem_limit_bytes=limit * 1024 * 1024),
        cost_estimate=pl.CostEstimate(flops=cost, bytes_accessed=1, transcendentals=0),
    )(*args, *after)


together = lax.optimization_barrier


def near(dims, dtype=F32):
    return pltpu.VMEM(tuple(dims), dtype)


def away(dims, dtype=F32):
    return pltpu.HBM(tuple(dims), dtype)


def shape(dims, dtype=F32):
    return jax.ShapeDtypeStruct(tuple(dims), dtype)


def image_mask(z, hw):
    dims = (z.H, z.W, z.L)
    rows = lax.broadcasted_iota(jnp.int32, dims, 0).astype(F32)
    cols = lax.broadcasted_iota(jnp.int32, dims, 1).astype(F32)
    tall = hw[0:1, : z.L].reshape(1, 1, z.L)
    wide = hw[1:2, : z.L].reshape(1, 1, z.L)
    return jnp.where((rows < tall) & (cols < wide), 1.0, 0.0).reshape(z.H * z.W, z.L)


def shifted_sum(z, taps, sign):
    dims = (z.n_own, z.H, z.W, z.L)
    cols = lax.broadcasted_iota(jnp.int32, dims, 2)
    total = None
    for c in range(3):
        column = None
        for r in range(3):
            part = taps(3 * r + c).reshape(dims)
            move = (r - 1) * sign
            if move == 1:
                part = jnp.concatenate([part[:, 1:], jnp.zeros_like(part[:, :1])], axis=1)
            elif move == -1:
                part = jnp.concatenate([jnp.zeros_like(part[:, :1]), part[:, :-1]], axis=1)
            column = part if column is None else column + part
        move = (c - 1) * sign
        if move:
            flat = column.reshape(z.n_own * z.H, z.W, z.L)
            flat = pltpu.roll(flat, (-move) % z.W, 1)
            column = flat.reshape(dims)
            edge = z.W - 1 if move == 1 else 0
            column = jnp.where(cols == edge, 0.0, column)
        total = column if total is None else total + column
    return total.reshape(z.own, z.L)


def moved_taps(z, feature):
    dims = (z.n_own, z.H, z.W, z.L)
    cols = lax.broadcasted_iota(jnp.int32, dims, 2)
    out = [None] * 9
    for c in range(3):
        move = 1 - c
        column = feature.reshape(dims)
        if move:
            flat = feature.reshape(z.n_own * z.H, z.W, z.L)
            column = pltpu.roll(flat, (-move) % z.W, 1).reshape(dims)
            edge = z.W - 1 if move == 1 else 0
            column = jnp.where(cols == edge, 0.0, column)
        for r in range(3):
            if r == 0:
                part = jnp.concatenate([column[:, 1:], jnp.zeros_like(column[:, :1])], axis=1)
            elif r == 2:
                part = jnp.concatenate([jnp.zeros_like(column[:, :1]), column[:, :-1]], axis=1)
            else:
                part = column
            out[3 * r + c] = part.reshape(z.own, z.L)
    return out


def fill_moved(z, a_ref, b_ref, moved_ref):
    half = z.Q // 2
    for j in range(z.Q):
        ref, at_row = (a_ref, j) if j < half else (b_ref, j - half)
        block = ref[at_row * z.own : (at_row + 1) * z.own, :].astype(F32)
        for k, part in enumerate(moved_taps(z, block)):
            moved_ref[j * z.own : (j + 1) * z.own, k * z.LP : k * z.LP + z.L] = part.astype(BF16)


def spread(ref, rows):
    used = rows[0].shape[1]
    if len(rows) < 8:
        rows = rows + [jnp.zeros((8 - len(rows), used), F32)]
    stat = jnp.concatenate(rows, axis=0)
    if used < LANES:
        stat = jnp.concatenate([stat, jnp.zeros((8, LANES - used), F32)], axis=1)
    for k in range(ref.shape[0]):
        ref[k] = stat


def local_stats(z, z_ref, hw_ref, stats_ref):
    px = z.H * z.W
    pivot = z_ref[0:1, :]

    def step(n, carry):
        mask = image_mask(z, hw_ref[n])
        centered = mask * (z_ref[pl.ds(pl.multiple_of(n * px, px), px), :] - pivot)
        return (
            carry[0] + jnp.sum(mask, 0, keepdims=True),
            carry[1] + jnp.sum(centered, 0, keepdims=True),
            carry[2] + jnp.sum(centered * centered, 0, keepdims=True),
        )

    zero = jnp.zeros((1, z.L), F32)
    count, total, squares = lax.fori_loop(0, z.n_group, step, (zero, zero, zero), unroll=4)
    offset = total / count
    spread(stats_ref, [count, pivot + offset, jnp.maximum(squares - total * offset, 0.0)])


def conv_into(z, product, y_ref, z_ref, sign=1, at_q=0):
    for j in range(z.Q):
        y_ref[...] = product(j)
        z_ref[pl.ds(pl.multiple_of((at_q ^ j) * z.own, z.own), z.own), :] = shifted_sum(
            z, lambda k: y_ref[:, k * z.LP : k * z.LP + z.L], sign
        )


def fill_kernels(z, at, blocks, wcat):
    for t, block in enumerate(blocks):
        s = at[1] ^ t
        for a in range(z.Z):
            row = pl.multiple_of(a * z.L + s * z.IB, z.IB)
            for k in range(z.K):
                wcat[pl.ds(row, z.IB), k * z.LP : k * z.LP + z.L] = block[a, k]


def first_conv(z, at, np_ref, *refs):
    xs, refs = refs[: z.Q], refs[z.Q :]
    blocks, refs = refs[: z.S], refs[z.S :]
    hw_ref, refs = refs[0], refs[1:]
    z_ref, slice_ref, par_ref, stats_ref, far_w, far_x, wcat, y_ref, sem = refs
    fill_kernels(z, at, blocks, wcat)
    copies = [pltpu.make_async_copy(wcat, far_w, sem.at[0])]
    for m in range(z.Q):
        copies.append(
            pltpu.make_async_copy(xs[m], far_x.at[at[0] ^ m], sem.at[1 + m])
        )
    for copy in copies:
        copy.start()
    for slot in range(z.Q):

        @pl.when(at[0] == slot)
        def _(slot=slot):
            par_ref[...] = np_ref[:, slot * z.L : (slot + 1) * z.L]
            for m in range(z.Q):
                j = slot ^ m
                slice_ref[j * z.own : (j + 1) * z.own, :] = xs[m][
                    :, slot * z.L : (slot + 1) * z.L
                ]

    def product(m):
        return jnp.dot(xs[m][...], wcat[...], preferred_element_type=F32)

    conv_into(z, product, y_ref, z_ref, 1, at[0])
    local_stats(z, z_ref, hw_ref, stats_ref)
    for copy in copies:
        copy.wait()


def gathered(z, at, parts, hold):
    half = z.G // 2
    for m in range(z.Q):
        hold[at[0] ^ m, :half] = parts[m][...]
        hold[at[0] ^ m, half:] = parts[z.Q + m][...]


def second_conv(z, at, *refs):
    hs, refs = refs[: 2 * z.Q], refs[2 * z.Q :]
    blocks, refs = refs[: z.S], refs[z.S :]
    hw_ref, z_ref, stats_ref, far_ref, wcat, y_ref, h_ref, sem = refs
    gathered(z, at, hs, h_ref)
    copy = pltpu.make_async_copy(h_ref, far_ref, sem)
    copy.start()
    fill_kernels(z, at, blocks, wcat)

    def product(j):
        rows = slice(j * z.own, (j + 1) * z.own)
        if z.L % LANES == 0:
            whole = jnp.concatenate([h_ref[i, rows, :] for i in range(z.Q)], axis=1)
            return jnp.dot(whole, wcat[...], preferred_element_type=F32)
        return sum(
            jnp.dot(h_ref[i, rows, :], wcat[i * z.L : (i + 1) * z.L, :], preferred_element_type=F32)
            for i in range(z.Q)
        )

    conv_into(z, product, y_ref, z_ref)
    local_stats(z, z_ref, hw_ref, stats_ref)
    copy.wait()


def merged(z, all_ref):
    counts = [all_ref[k, 0:1, : z.L] for k in range(z.S * z.Z)]
    means = [all_ref[k, 1:2, : z.L] for k in range(z.S * z.Z)]
    count = sum(counts)
    mean = sum(c * m for c, m in zip(counts, means)) / count
    squares = sum(
        all_ref[k, 2:3, : z.L] + counts[k] * (means[k] - mean) * (means[k] - mean)
        for k in range(z.S * z.Z)
    )
    return mean, lax.rsqrt(squares / count + EPS), count


def keep(ref, rows):
    used = rows[0].shape[1]
    ref[...] = jnp.concatenate(rows + [jnp.zeros((8 - len(rows), used), F32)], axis=0)


def over_images(z, step, init=0, unroll=2):
    px = z.H * z.W

    def one(n, carry):
        return step(n, pl.ds(pl.multiple_of(n * px, px), px), carry)

    return lax.fori_loop(0, z.n_group, one, init, unroll=unroll)


def over_halves(z, step, refs):
    px, count = z.H * z.W, z.n_group // 2
    for i, ref in enumerate(refs):

        def one(n, carry, i=i, ref=ref):
            rows = pl.ds(pl.multiple_of((i * count + n) * px, px), px)
            ref[pl.ds(pl.multiple_of(n * px, px), px), :] = step(i * count + n, rows)
            return carry

        lax.fori_loop(0, count, one, 0, unroll=2)


def hidden(z, at, z_ref, all_ref, hw_ref, par_ref, *refs):
    parts, (a_ref, b_ref, sum_ref, kernel_ref) = refs[: z.Q], refs[z.Q :]
    unpick(z, at, *parts, kernel_ref)
    mean, inv, count = merged(z, all_ref)
    keep(sum_ref, [mean, inv, count])
    gain, shift = par_ref[0:1, :], par_ref[1:2, :]

    def step(n, rows):
        mask = image_mask(z, hw_ref[n])
        return gelu(mask * (gain * ((z_ref[rows, :] - mean) * inv) + shift)).astype(BF16)

    over_halves(z, step, (a_ref, b_ref))


def middle(z, at, z_ref, all_ref, hw_ref, par_ref, x_ref, *refs):
    cot_ref, out_ref, d_ref, sum_ref, stats_ref = refs
    mean, inv, count = merged(z, all_ref)
    keep(sum_ref, [mean, inv, count])
    gain, shift = par_ref[2:3, :], par_ref[3:4, :]
    px = z.H * z.W
    carry = (jnp.zeros((1, z.L), F32), jnp.zeros((1, z.L), F32))
    for j in range(z.Q):

        def step(n, carry, j=j):
            local = pl.ds(pl.multiple_of(n * px, px), px)
            rows = pl.ds(pl.multiple_of(j * z.own + n * px, px), px)
            mask = image_mask(z, hw_ref[j * z.n_own + n])
            normed = (z_ref[rows, :] - mean) * inv
            summed = mask * (gain * normed + shift) + x_ref[rows, :].astype(F32)
            value, slope = gelu_both(summed)
            out_ref[j, local, :] = value.astype(BF16)
            d = cot_ref[rows, :].astype(F32) * slope
            d_ref[rows, :] = d
            masked = mask * d
            return (
                carry[0] + jnp.sum(masked, 0, keepdims=True),
                carry[1] + jnp.sum(masked * normed, 0, keepdims=True),
            )

        carry = lax.fori_loop(0, z.n_own, step, carry, unroll=2)
    spread(stats_ref, list(carry))


def norm_grad(z, row, z_ref, up_ref, sum_ref, all_ref, hw_ref, par_ref, a_ref, b_ref, par_grad_ref):
    mean, inv, count = sum_ref[0:1, :], sum_ref[1:2, :], sum_ref[2:3, :]
    shift_grad = sum(all_ref[k, 0:1, : z.L] for k in range(z.S * z.Z))
    gain_grad = sum(all_ref[k, 1:2, : z.L] for k in range(z.S * z.Z))
    keep(par_grad_ref, [gain_grad, shift_grad])
    gain = par_ref[row : row + 1, :]

    def step(n, rows):
        mask = image_mask(z, hw_ref[n])
        normed = (z_ref[rows, :] - mean) * inv
        grad = inv * mask * gain * (up_ref[rows, :] - (shift_grad + normed * gain_grad) / count)
        return grad.astype(BF16)

    over_halves(z, step, (a_ref, b_ref))


def back_product(z, at, dz_ref, blocks, wcat):
    for t, block in enumerate(blocks):
        s = at[1] ^ t
        for b in range(z.Z):
            for k in range(z.K):
                rows = pl.ds(pl.multiple_of(k * z.LP + s * z.IB, z.IB), z.IB)
                if z.L % LANES == 0:
                    wcat[0, rows, b * z.L : (b + 1) * z.L] = block[b, k]
                else:
                    wcat[b, rows, :] = block[b, k]
    contract = (((1,), (1,)), ((), ()))

    def product(j):
        rows = slice(j * z.own, (j + 1) * z.own)
        if z.L % LANES == 0:
            whole = jnp.concatenate([dz_ref[i, rows, :] for i in range(z.Q)], axis=1)
            return lax.dot_general(whole, wcat[0], contract, preferred_element_type=F32)
        return sum(
            lax.dot_general(dz_ref[i, rows, :], wcat[i], contract, preferred_element_type=F32)
            for i in range(z.Q)
        )

    return product


def back_scratch(z):
    if z.L % LANES == 0:
        wide = pltpu.VMEM((1, z.K * z.LP, z.C), BF16)
    else:
        wide = pltpu.VMEM((z.Z, z.K * z.LP, z.C // z.Z), BF16)
    return [wide, pltpu.VMEM((z.own, z.K * z.LP), F32), pltpu.VMEM((z.Q, z.G, z.L), BF16)]


def hidden_grad(z, at, *refs):
    dzs, refs = refs[: 2 * z.Q], refs[2 * z.Q :]
    blocks, refs = refs[: z.S], refs[z.S :]
    z_ref, sum_ref, hw_ref, par_ref, da_ref, stats_ref, wcat, y_ref, dz_ref = refs
    gathered(z, at, dzs, dz_ref)
    conv_into(z, back_product(z, at, dz_ref, blocks, wcat), y_ref, da_ref, -1)
    mean, inv = sum_ref[0:1, :], sum_ref[1:2, :]
    gain, shift = par_ref[0:1, :], par_ref[1:2, :]

    def step(n, rows, carry):
        mask = image_mask(z, hw_ref[n])
        normed = (z_ref[rows, :] - mean) * inv
        da = da_ref[rows, :] * gelu_both(mask * (gain * normed + shift))[1]
        da_ref[rows, :] = da
        masked = mask * da
        return (
            carry[0] + jnp.sum(masked, 0, keepdims=True),
            carry[1] + jnp.sum(masked * normed, 0, keepdims=True),
        )

    zero = jnp.zeros((1, z.L), F32)
    spread(stats_ref, list(over_images(z, step, (zero, zero))))


def input_part(z, at, a_ref, b_ref, w_ref, d_ref, *refs):
    outs, (moved_ref, dx_ref) = refs[: z.Q], refs[z.Q :]
    fill_moved(z, a_ref, b_ref, moved_ref)
    contract = (((1,), (1,)), ((), ()))
    for j in range(z.Q):
        rows = slice(j * z.own, (j + 1) * z.own)
        dx_ref[j] = lax.dot_general(moved_ref[rows, :], w_ref[...], contract, preferred_element_type=F32)
    for slot in range(z.Q):

        @pl.when(at[0] == slot)
        def _(slot=slot):
            for j in range(z.Q):
                lanes = slice(slot * z.L, (slot + 1) * z.L)
                dx_ref[j, :, lanes] = dx_ref[j, :, lanes] + d_ref[j * z.own : (j + 1) * z.own, :]

    for m in range(z.Q):
        outs[m][...] = dx_ref[at[0] ^ m].astype(outs[m].dtype)


def kernel_grad(z, at, f_ref, a_ref, b_ref, mine_ref, *refs):
    theirs, (moved_ref, full_ref) = refs[:-2], refs[-2:]
    fill_moved(z, a_ref, b_ref, moved_ref)
    contract = (((0,), (0,)), ((), ()))
    if f_ref.shape[2] == z.C:
        whole = f_ref[...].reshape(z.G, z.C)
        full_ref[...] = lax.dot_general(whole, moved_ref[...], contract, preferred_element_type=F32)
    elif z.L % LANES == 0:
        whole = jnp.concatenate([f_ref[i] for i in range(z.Q)], axis=1)
        full_ref[...] = lax.dot_general(whole, moved_ref[...], contract, preferred_element_type=F32)
    else:
        for i in range(z.Q):
            full_ref[i * z.L : (i + 1) * z.L, :] = lax.dot_general(
                f_ref[i], moved_ref[...], contract, preferred_element_type=F32
            )
    for r in range(z.Q):
        for t in range(z.S):
            row = pl.multiple_of((at[0] ^ r) * z.L + (at[1] ^ t) * z.IB, z.IB)
            for k in range(z.K):
                part = full_ref[pl.ds(row, z.IB), k * z.LP : k * z.LP + z.L]
                if t == 0:
                    mine_ref[r, k] = part
                else:
                    theirs[(t - 1) * z.Q + r][k] = part.astype(BF16)


def first_back(z, at, z_ref, up_ref, sum_ref, all_ref, hw_ref, par_ref, f_ref, *refs):
    (a_ref, b_ref, par_grad_ref), refs = refs[:3], refs[3:]
    norm_grad(z, 0, z_ref, up_ref, sum_ref, all_ref, hw_ref, par_ref, a_ref, b_ref, par_grad_ref)
    kernel_grad(z, at, f_ref, a_ref, b_ref, *refs)


def add_sharers(z, at, *refs):
    count = 1 + z.Q * (z.S - 1)
    mine_ref, others, refs = refs[0], refs[1:count], refs[count:]
    value_ref = None
    if len(refs) > z.Q:
        value_ref, refs = refs[0], refs[1:]
    for r in range(z.Q):
        for k in range(z.K):
            total = mine_ref[r, k]
            for other in others[r :: z.Q]:
                total = total + other[k].astype(F32)
            refs[r][k * z.IB : (k + 1) * z.IB, :] = total.astype(BF16)
        if value_ref is not None:
            refs[r][z.K * z.IB :, :] = value_ref[at[0] ^ r]


def route(z, at, *refs):
    parts, refs = refs[: z.Q], refs[z.Q :]
    outs, refs = refs[: z.Z], refs[z.Z :]
    hold = refs[-1]
    for r in range(z.Q):
        hold[at[2] ^ at[0] ^ r] = parts[r][: z.K * z.IB, :]
    for m in range(z.Z):
        outs[m][...] = hold[m]
    if len(refs) == 3:
        value_ref, slots, _ = refs
        for r in range(z.Q):
            slots[at[0] ^ r] = parts[r][z.K * z.IB :, :]
        for j in range(z.Q):
            value_ref[:, j * z.L : (j + 1) * z.L] = slots[j]


def total_of(z, *refs):
    refs[-1][...] = sum(ref[...].astype(F32) for ref in refs[:-1]).astype(refs[-1].dtype)


def direction_of(grad, first, second, param, decay):
    new_first = BETA * first + (1.0 - BETA) * grad
    new_second = BETA * second + (1.0 - BETA) * grad * grad
    move = new_first / BIAS / (jnp.sqrt(new_second / BIAS) + TINY) + decay * param
    return new_first, new_second, move


def moments(z, j, *refs):
    count = len(refs) - (7 if j else 12)
    parts, refs = refs[:count], refs[count:]
    w_ref, first_ref, second_ref, refs = *refs[:3], refs[3:]
    if j == 0:
        other_ref, g1_ref, g2_ref, refs = refs[0], refs[1], refs[2], refs[5:]
    nf_ref, ns_ref, u_ref, stats_ref = refs
    total_u = jnp.zeros((1, z.L), F32)
    total_w = jnp.zeros((1, z.L), F32)
    for k in range(z.K):
        grad = sum(part[k * z.IB : (k + 1) * z.IB, :].astype(F32) for part in parts)
        w = w_ref[0, k]
        nf, ns, u = direction_of(grad, first_ref[0, k], second_ref[0, k], w, DECAY)
        nf_ref[0, k] = nf
        ns_ref[0, k] = ns
        u_ref[k] = u
        total_u = total_u + jnp.sum(u * u, 0, keepdims=True)
        total_w = total_w + jnp.sum(w * w, 0, keepdims=True)
    if j:
        keep(stats_ref, [total_u, total_w])
    else:
        grads = [g1_ref[0:1, :], g1_ref[1:2, :], g2_ref[0:1, :], g2_ref[1:2, :]]
        spread(stats_ref, [total_u, other_ref[0:1, :], total_w, other_ref[1:2, :]] + grads)


def finish(z, all_ref, w_ref, u0_ref, u1_ref, np_ref, nf_ref, ns_ref, *outs):
    nw_ref, copy_ref, nnp_ref, nnf_ref, nns_ref, trust_ref = outs
    total = all_ref[0]
    for k in range(1, z.R * z.Z):
        total = total + all_ref[k]
    tops, bottoms = [], []
    for j in range(2):
        un = jnp.sqrt(jnp.sum(total[j : j + 1, : z.L], axis=1, keepdims=True))
        wn = jnp.sqrt(jnp.sum(total[2 + j : 3 + j, : z.L], axis=1, keepdims=True))
        tops.append(wn)
        bottoms.append(un)
        scale = RATE * (wn / (un + TINY))
        for k in range(z.K):
            new = w_ref[j, k] - scale * (u0_ref, u1_ref)[j][k]
            nw_ref[j, k] = new
            copy_ref[j, k] = new.astype(BF16)
    for j in range(z.Q):
        nnp_ref[:, j * z.L : (j + 1) * z.L] = all_ref[j * z.Z, 4:8, : z.L]
    param = np_ref[...]
    nf, ns, move = direction_of(nnp_ref[...], nf_ref[...], ns_ref[...], param, 0.0)
    nnf_ref[...] = nf
    nns_ref[...] = ns
    pn = jnp.sqrt(jnp.sum(param * param, axis=1, keepdims=True))
    qn = jnp.sqrt(jnp.sum(move * move, axis=1, keepdims=True))
    nnp_ref[...] = param - RATE * (pn / (qn + TINY)) * move
    for r in range(4):
        tops.append(pn[r : r + 1])
        bottoms.append(qn[r : r + 1])
    at_row = lax.broadcasted_iota(jnp.int32, (2, 6), 0)
    at_col = lax.broadcasted_iota(jnp.int32, (2, 6), 1)
    trust = jnp.zeros((2, 6), F32)
    for c in range(6):
        trust = jnp.where(at_col == c, jnp.where(at_row == 0, tops[c], bottoms[c]), trust)
    trust_ref[...] = trust


def pick(z, more, at, *refs):
    parts, refs = refs[: z.Z], refs[z.Z :]
    map_ref = None
    if more == "map":
        map_ref, valid_ref, refs = refs[0], refs[1], refs[2:]
        rows = []
        for n in range(z.n_own):
            valid = valid_ref[n].astype(F32)
            tall = jnp.sum(valid[:, 0:1], axis=0, keepdims=True)
            wide = jnp.sum(valid[0:1, :], axis=1, keepdims=True)
            rows += [jnp.broadcast_to(tall, (1, z.L)), jnp.broadcast_to(wide, (1, z.L))]
        rows.append(jnp.zeros((z.extra - len(rows), z.L), F32))
        sizes = jnp.concatenate(rows, axis=0).astype(BF16)
    if more == "keep":
        far_ref, outs, (hold, sem) = refs[0], refs[1:-2], refs[-2:]
    else:
        outs, hold = refs[:-1], refs[-1]
    for m in range(z.Z):
        hold[at[2] ^ m] = parts[m][...]
    if more == "keep":
        copy = pltpu.make_async_copy(hold, far_ref, sem)
        copy.start()
    for m in range(z.Q):
        for k in range(z.K):
            outs[m][k * z.IB : (k + 1) * z.IB, :] = hold[at[0] ^ m, k]
        if map_ref is not None:
            for slot in range(z.Q):

                @pl.when((at[0] ^ m) == slot)
                def _(m=m, slot=slot):
                    outs[m][z.K * z.IB : z.K * z.IB + z.own, :] = map_ref[:, slot * z.L : (slot + 1) * z.L]

            outs[m][z.K * z.IB + z.own :, :] = sizes

    if more == "keep":
        copy.wait()


def unpick(z, at, *refs):
    parts, refs = refs[: z.Q], refs[z.Q :]
    for m in range(z.Q):
        q = at[0] ^ m
        for k in range(z.K):
            refs[0][q, k] = parts[m][k * z.IB : (k + 1) * z.IB, :]
        if len(refs) > 1:
            start = z.K * z.IB
            refs[1][pl.ds(pl.multiple_of(q * z.own, z.own), z.own), :] = parts[m][start : start + z.own, :]
            for n in range(z.n_own):
                row = start + z.own + 2 * n
                two = jnp.broadcast_to(parts[m][row : row + 2, 0:1].astype(F32), (2, LANES))
                refs[2][q * z.n_own + n] = jnp.concatenate([two, jnp.zeros((6, LANES), F32)], axis=0)


def shards(z, images, masks, cotangent, weights, first, second, params, p_first, p_second):
    q, s, b = lax.axis_index("q"), lax.axis_index("s"), lax.axis_index("z")
    at = jnp.stack([q, s, b]).astype(jnp.int32)

    def over_z(v, m):
        return lax.ppermute(v, "z", [(i, i ^ m) for i in range(z.Z)]) if m else v

    def over_s(v, m):
        return lax.ppermute(v, "s", [(i, i ^ m) for i in range(z.S)]) if m else v

    def sharers(v):
        return lax.all_to_all(v, ("s", "z"), 0, 0)

    def over_q(v, m):
        return lax.ppermute(v, "q", [(i, i ^ m) for i in range(z.Q)]) if m else v

    def gather_z(w):
        return [over_z(w, m) for m in range(z.Z)]

    def gather(a, b):
        if z.Q != 4:
            return [over_q(v, m) for v in (a, b) for m in range(z.Q)]
        a1, a2, b1, b2 = over_q(a, 1), over_q(a, 2), over_q(b, 1), over_q(b, 2)
        return [a, a1, a2, over_q(a2, 1), b, b1, b2, over_q(b1, 2)]

    def share(packed):
        return [over_s(packed, t) for t in range(z.S)]

    rows = z.own
    GL = (z.G, z.L)
    HL = (z.G // 2, z.L)
    many = z.S * z.Z
    piece = (z.K, z.IB, z.L)
    blocks = near((z.Z, *piece), BF16)
    stat = near((many, 8, LANES))
    conv_scratch = [pltpu.VMEM((z.C, z.K * z.LP), BF16), pltpu.VMEM((rows, z.K * z.LP), F32)]
    grad_scratch = [pltpu.VMEM((z.G, z.K * z.LP), BF16), pltpu.VMEM((z.C, z.K * z.LP), F32)]
    cot_rows = cotangent.reshape(rows, z.C)
    image_rows = images.reshape(rows, z.C)

    low_one, low_two = (weights[j].astype(BF16) for j in range(2))
    one = [over_z(low_one, m) for m in range(z.Z)]
    xs = [over_q(image_rows, m) for m in range(z.Q)]
    one, low_two = together((one, low_two))
    hold = pltpu.VMEM((z.Z, *piece), BF16)
    picked = call(
        functools.partial(pick, z, "map"),
        [near((z.sent, z.L), BF16)] * z.Q,
        (at, *one, cot_rows, masks),
        [hold],
    )
    picked, xs = together((picked, xs))
    two = [over_z(low_two, m) for m in range(z.Z)]
    picked, two = together(([over_q(picked[m], m) for m in range(z.Q)], two))
    front_one, cots, hw = call(
        functools.partial(unpick, z),
        [blocks, near(GL, BF16), near((z.n_group, 8, LANES))],
        (at, *picked),
    )
    keep = away((z.Z, *piece), BF16)
    keep_two, *picked = call(
        functools.partial(pick, z, "keep"),
        [keep] + [near((z.K * z.IB, z.L), BF16)] * z.Q,
        (at, *two),
        [hold, pltpu.SemaphoreType.DMA],
        raw=(keep,),
    )
    w_far = away((z.C, z.K * z.LP), BF16)
    x_far = away((z.Q, rows, z.C), BF16)
    z1, x_slice, slice_params, stats, w_far, x_far = call(
        functools.partial(first_conv, z),
        [
            near(GL),
            near(GL, BF16),
            near((4, z.L)),
            stat,
            w_far,
            x_far,
        ],
        (at, params, *xs, *share(front_one), hw),
        conv_scratch + [pltpu.SemaphoreType.DMA((1 + z.Q,))],
        limit=16,
        raw=(w_far, x_far),
    )
    stats, picked = together((stats, picked))
    stats, picked = together((sharers(stats), [over_q(picked[m], m) for m in range(z.Q)]))
    ha, hb, sum_one, front_two = call(
        functools.partial(hidden, z),
        [near(HL, BF16), near(HL, BF16), near((8, z.L)), blocks],
        (at, z1, stats, hw, slice_params, *picked),
    )
    hs = gather(ha, hb)
    h_far = away((z.Q, *GL), BF16)
    z2, stats, h_far = call(
        functools.partial(second_conv, z),
        [near(GL), stat, h_far],
        (at, *hs, *share(front_two), hw),
        conv_scratch + [pltpu.VMEM((z.Q, *GL), BF16), pltpu.SemaphoreType.DMA],
        limit=16,
        raw=(h_far,),
    )
    out, d, sum_two, stats = call(
        functools.partial(middle, z),
        [near((z.Q, rows, z.L), BF16), near(GL), near((8, z.L)), stat],
        (at, z2, sharers(stats), hw, slice_params, x_slice, cots),
    )
    da, db, grad_two = call(
        functools.partial(norm_grad, z, 2),
        [near(HL, BF16), near(HL, BF16), near((8, z.L))],
        (z2, d, sum_two, sharers(stats), hw, slice_params),
    )
    da, db, keep_two = together((da, db, keep_two))
    dz2s = gather(da, db)

    gradient_shapes = [near((z.Q, *piece))] + [near(piece, BF16)] * (z.Q * (z.S - 1))

    def to_sharers(theirs):
        return [over_s(theirs[(t - 1) * z.Q + r], t) for t in range(1, z.S) for r in range(z.Q)]

    def add_up(mine, received, *value):
        more = rows if value else 0
        return call(
            functools.partial(add_sharers, z),
            [near((z.K * z.IB + more, z.L), BF16)] * z.Q,
            (at, mine, *received, *value),
        )

    def by_plane(parts):
        return [over_q(parts[r], r) for r in range(z.Q)]

    def along(parts):
        return [over_z(parts[m], m) for m in range(z.Z)]

    def update(j, parts, *more):
        whole = pl.BlockSpec(memory_space=pltpu.VMEM)
        block = pl.BlockSpec((1, *piece), lambda i: (j, 0, 0, 0))
        held = pl.BlockSpec(memory_space=pl.ANY)
        args = [pltpu.with_memory_space_constraint(v, pltpu.VMEM) for v in (*parts,)]
        args += [weights, first, second]
        specs = [whole] * len(parts) + [block] * 3
        if more:
            args += [pltpu.with_memory_space_constraint(v, pltpu.VMEM) for v in more[:3]] + list(more[3:])
            specs += [whole] * 3 + [held] * 2
        n = len(args)
        return pl.pallas_call(
            functools.partial(moments, z, j),
            grid=(1,),
            out_shape=[shape(weights.shape)] * 2
            + [near(piece), near((8, z.L)) if j else near((z.R * z.Z, 8, LANES))],
            in_specs=specs,
            out_specs=[block, block, whole, whole],
            input_output_aliases={} if j else {n - 2: 0, n - 1: 1},
            compiler_params=pltpu.CompilerParams(vmem_limit_bytes=8 * 1024 * 1024),
            cost_estimate=pl.CostEstimate(flops=1 if j else COST_GRAD, bytes_accessed=1, transcendentals=0),
        )(*args)

    mine, *theirs = call(
        functools.partial(kernel_grad, z),
        gradient_shapes,
        (at, h_far, da, db),
        grad_scratch,
        limit=14,
        cost=COST_GRAD,
    )
    parts_two = add_up(mine, to_sharers(theirs), out)
    da1, stats = call(
        functools.partial(hidden_grad, z),
        [near(GL), stat],
        (at, *dz2s, *share(keep_two), z1, sum_one, hw, slice_params),
        back_scratch(z),
        limit=16,
    )
    stats, parts_two = together((stats, parts_two))
    stats, parts_two = together((sharers(stats), by_plane(parts_two)))
    da, db, grad_one, mine, *theirs = call(
        functools.partial(first_back, z),
        [near(HL, BF16), near(HL, BF16), near((8, z.L))] + gradient_shapes,
        (at, z1, da1, sum_one, stats, hw, slice_params, x_far),
        grad_scratch,
        limit=14,
        cost=COST_GRAD,
    )
    flat = near((z.K * z.IB, z.L), BF16)
    hold = pltpu.VMEM((z.Z, z.K * z.IB, z.L), BF16)
    *parts_two, values = call(
        functools.partial(route, z),
        [flat] * z.Z + [near((rows, z.C), BF16)],
        (at, *parts_two),
        [pltpu.VMEM((z.Q, rows, z.L), BF16), hold],
        after=(da,),
    )
    received = to_sharers(theirs)
    parts_one = add_up(mine, received)
    parts_one, parts_two = by_plane(parts_one), along(parts_two)
    parts_one, parts_two = together((parts_one, parts_two))
    dxs = call(
        functools.partial(input_part, z),
        [near((rows, z.C))] + [near((rows, z.C), BF16)] * (z.Q - 1),
        (at, da, db, w_far, d),
        [grad_scratch[0], pltpu.VMEM((z.Q, rows, z.C), F32)],
        limit=16,
        cost=COST_GRAD,
        far=(w_far,),
        after=(received[0],),
    )
    parts_one = call(functools.partial(route, z), [flat] * z.Z, (at, *parts_one), [hold], after=(dxs[0],))
    parts_one, dxs, parts_two = together((parts_one, dxs, parts_two))
    parts_one = along(parts_one)
    new_first, new_second, move_two, other = update(1, parts_two)
    dxs = [over_q(dxs[m], m) for m in range(z.Q)]
    new_first, new_second, move_one, stats = update(
        0, parts_one, other, grad_one, grad_two, new_first, new_second
    )
    stats = lax.all_to_all(stats, ("s", "q", "z"), 0, 0)
    dx = call(functools.partial(total_of, z), shape((rows, z.C), BF16), tuple(dxs))
    new_weights, copies, new_params, new_p_first, new_p_second, trust = call(
        functools.partial(finish, z),
        [shape(weights.shape), shape(weights.shape, BF16)] + [shape(params.shape)] * 3 + [shape((2, 6))],
        (stats, weights, move_one, move_two, params, p_first, p_second),
    )
    return (
        values.reshape(images.shape),
        dx.reshape(images.shape),
        new_weights,
        copies,
        new_first,
        new_second,
        new_params,
        new_p_first,
        new_p_second,
        trust,
    )


def solution(mesh):
    def whole(images, masks, cotangent, weights, first, second, params, p_first, p_second):
        z = Sizes(mesh, images.shape, weights.shape)
        inner = Mesh(mesh.devices.reshape(z.Q, z.S, z.Z), ("q", "s", "z"))
        pixels = P(("q", "s", "z"), None, None, None)
        kernels = P(None, None, ("q", "s"), "z")
        return jax.shard_map(
            functools.partial(shards, z),
            mesh=inner,
            in_specs=(pixels, P(("q", "s", "z"), None, None), pixels, kernels, kernels, kernels, P(), P(), P()),
            out_specs=(pixels, pixels, kernels, kernels, kernels, kernels, P(), P(), P(), P()),
            check_vma=False,
        )(images, masks, cotangent, weights, first, second, params, p_first, p_second)

    return whole
```

```python
import functools

import jax
import jax.numpy as jnp
from jax import lax
from jax.experimental import pallas as pl
from jax.experimental.pallas import tpu as pltpu
from jax.sharding import Mesh
from jax.sharding import PartitionSpec as P

STEP = 3
RATE = 0.5
DECAY = 0.01
BETA = 0.5
BIAS = 1.0 - BETA**STEP
EPS = 1e-05
TINY = 1e-06
ROOT = 0.7978845608028654
CUBE = 0.044715
LANES = 128
COST_GRAD = 3 * 10**9
F32 = jnp.float32
BF16 = jnp.bfloat16


def gelu(v):
    return 0.5 * v * (1.0 + jnp.tanh(ROOT * (v + CUBE * (v * v * v))))


def gelu_both(v):
    t = jnp.tanh(ROOT * (v + CUBE * (v * v * v)))
    value = 0.5 * v * (1.0 + t)
    slope = 0.5 * (1.0 + t) + 0.5 * v * (1.0 - t * t) * (ROOT * (1.0 + (3.0 * CUBE) * (v * v)))
    return value, slope


class Sizes:
    def __init__(self, mesh, images, weights):
        self.Z = mesh.shape["ba"]
        self.R = mesh.shape["ha"] * mesh.shape["wa"]
        self.Q = self.Z
        self.S = self.R // self.Q
        n, self.H, self.W, self.C = images
        self.n_own = n // (self.R * self.Z)
        self.own = self.n_own * self.H * self.W
        self.n_group = self.n_own * self.Q
        self.G = self.own * self.Q
        self.L = self.C // self.Q
        self.LP = max(self.L, LANES)
        self.IB = self.C // self.R
        self.K = weights[1]
        self.extra = 16 * ((2 * self.n_own + 15) // 16)
        self.sent = self.K * self.IB + self.own + self.extra


def call(body, out_shape, args, scratch=(), limit=8, far=(), after=(), cost=1, raw=()):
    smem = [a.dtype == jnp.int32 and a.ndim == 1 for a in args]
    away = [any(a is f for f in far) for a in args]
    args = [
        a if m else pltpu.with_memory_space_constraint(a, pltpu.HBM if w else pltpu.VMEM)
        for a, m, w in zip(args, smem, away)
    ]
    n = len(args)

    def run(*refs):
        body(*refs[:n], *refs[n + len(after) :])

    return pl.pallas_call(
        run,
        out_shape=out_shape,
        in_specs=[pl.BlockSpec(memory_space=pltpu.SMEM if m else pltpu.VMEM) for m in smem]
        + [pl.BlockSpec(memory_space=pl.ANY)] * len(after),
        out_specs=jax.tree.map(
            lambda o: pl.BlockSpec(memory_space=pltpu.HBM if any(o is r for r in raw) else pltpu.VMEM),
            out_shape,
        ),
        scratch_shapes=list(scratch),
        compiler_params=pltpu.CompilerParams(vmem_limit_bytes=limit * 1024 * 1024),
        cost_estimate=pl.CostEstimate(flops=cost, bytes_accessed=1, transcendentals=0),
    )(*args, *after)


together = lax.optimization_barrier


def near(dims, dtype=F32):
    return pltpu.VMEM(tuple(dims), dtype)


def away(dims, dtype=F32):
    return pltpu.HBM(tuple(dims), dtype)


def shape(dims, dtype=F32):
    return jax.ShapeDtypeStruct(tuple(dims), dtype)


def image_mask(z, hw):
    dims = (z.H, z.W, z.L)
    rows = lax.broadcasted_iota(jnp.int32, dims, 0).astype(F32)
    cols = lax.broadcasted_iota(jnp.int32, dims, 1).astype(F32)
    tall = hw[0:1, : z.L].reshape(1, 1, z.L)
    wide = hw[1:2, : z.L].reshape(1, 1, z.L)
    return jnp.where((rows < tall) & (cols < wide), 1.0, 0.0).reshape(z.H * z.W, z.L)


def shifted_sum(z, taps, sign):
    dims = (z.n_own, z.H, z.W, z.L)
    cols = lax.broadcasted_iota(jnp.int32, dims, 2)
    total = None
    for c in range(3):
        column = None
        for r in range(3):
            part = taps(3 * r + c).reshape(dims)
            move = (r - 1) * sign
            if move == 1:
                part = jnp.concatenate([part[:, 1:], jnp.zeros_like(part[:, :1])], axis=1)
            elif move == -1:
                part = jnp.concatenate([jnp.zeros_like(part[:, :1]), part[:, :-1]], axis=1)
            column = part if column is None else column + part
        move = (c - 1) * sign
        if move:
            flat = column.reshape(z.n_own * z.H, z.W, z.L)
            flat = pltpu.roll(flat, (-move) % z.W, 1)
            column = flat.reshape(dims)
            edge = z.W - 1 if move == 1 else 0
            column = jnp.where(cols == edge, 0.0, column)
        total = column if total is None else total + column
    return total.reshape(z.own, z.L)


def moved_taps(z, feature):
    dims = (z.n_own, z.H, z.W, z.L)
    cols = lax.broadcasted_iota(jnp.int32, dims, 2)
    out = [None] * 9
    for c in range(3):
        move = 1 - c
        column = feature.reshape(dims)
        if move:
            flat = feature.reshape(z.n_own * z.H, z.W, z.L)
            column = pltpu.roll(flat, (-move) % z.W, 1).reshape(dims)
            edge = z.W - 1 if move == 1 else 0
            column = jnp.where(cols == edge, 0.0, column)
        for r in range(3):
            if r == 0:
                part = jnp.concatenate([column[:, 1:], jnp.zeros_like(column[:, :1])], axis=1)
            elif r == 2:
                part = jnp.concatenate([jnp.zeros_like(column[:, :1]), column[:, :-1]], axis=1)
            else:
                part = column
            out[3 * r + c] = part.reshape(z.own, z.L)
    return out


def fill_moved(z, a_ref, b_ref, moved_ref):
    half = z.Q // 2
    for j in range(z.Q):
        ref, at_row = (a_ref, j) if j < half else (b_ref, j - half)
        block = ref[at_row * z.own : (at_row + 1) * z.own, :].astype(F32)
        for k, part in enumerate(moved_taps(z, block)):
            moved_ref[j * z.own : (j + 1) * z.own, k * z.LP : k * z.LP + z.L] = part.astype(BF16)


def spread(ref, rows):
    used = rows[0].shape[1]
    if len(rows) < 8:
        rows = rows + [jnp.zeros((8 - len(rows), used), F32)]
    stat = jnp.concatenate(rows, axis=0)
    if used < LANES:
        stat = jnp.concatenate([stat, jnp.zeros((8, LANES - used), F32)], axis=1)
    for k in range(ref.shape[0]):
        ref[k] = stat


def local_stats(z, z_ref, hw_ref, stats_ref):
    px = z.H * z.W
    pivot = z_ref[0:1, :]

    def step(n, carry):
        mask = image_mask(z, hw_ref[n])
        centered = mask * (z_ref[pl.ds(pl.multiple_of(n * px, px), px), :] - pivot)
        return (
            carry[0] + jnp.sum(mask, 0, keepdims=True),
            carry[1] + jnp.sum(centered, 0, keepdims=True),
            carry[2] + jnp.sum(centered * centered, 0, keepdims=True),
        )

    zero = jnp.zeros((1, z.L), F32)
    count, total, squares = lax.fori_loop(0, z.n_group, step, (zero, zero, zero), unroll=4)
    offset = total / count
    spread(stats_ref, [count, pivot + offset, jnp.maximum(squares - total * offset, 0.0)])


def conv_into(z, product, y_ref, z_ref, sign=1, at_q=0):
    for j in range(z.Q):
        y_ref[...] = product(j)
        z_ref[pl.ds(pl.multiple_of((at_q ^ j) * z.own, z.own), z.own), :] = shifted_sum(
            z, lambda k: y_ref[:, k * z.LP : k * z.LP + z.L], sign
        )


def fill_kernels(z, at, blocks, wcat):
    for t, block in enumerate(blocks):
        s = at[1] ^ t
        for a in range(z.Z):
            row = pl.multiple_of(a * z.L + s * z.IB, z.IB)
            for k in range(z.K):
                wcat[pl.ds(row, z.IB), k * z.LP : k * z.LP + z.L] = block[a, k]


def split_channels(z, at, slices, outs, rows):
    for s in range(z.S):

        @pl.when(at[1] == s)
        def _(s=s):
            for t in range(z.S):
                low = (s ^ t) * z.IB
                outs[t][rows, :] = jnp.concatenate([v[:, low : low + z.IB] for v in slices], axis=1)


def first_conv(z, at, np_ref, *refs):
    xs, refs = refs[: z.Q], refs[z.Q :]
    blocks, refs = refs[: z.S], refs[z.S :]
    hw_ref, refs = refs[0], refs[1:]
    outs, refs = refs[: z.S], refs[z.S :]
    z_ref, slice_ref, par_ref, stats_ref, far_w, wcat, y_ref, sem = refs
    fill_kernels(z, at, blocks, wcat)
    copy = pltpu.make_async_copy(wcat, far_w, sem)
    copy.start()
    for m in range(z.Q):
        rows = pl.ds(pl.multiple_of((at[0] ^ m) * z.own, z.own), z.own)
        split_channels(z, at, [xs[m][:, a * z.L : (a + 1) * z.L] for a in range(z.Q)], outs, rows)
    for slot in range(z.Q):

        @pl.when(at[0] == slot)
        def _(slot=slot):
            par_ref[...] = np_ref[:, slot * z.L : (slot + 1) * z.L]
            for m in range(z.Q):
                j = slot ^ m
                slice_ref[j * z.own : (j + 1) * z.own, :] = xs[m][
                    :, slot * z.L : (slot + 1) * z.L
                ]

    def product(m):
        return jnp.dot(xs[m][...], wcat[...], preferred_element_type=F32)

    conv_into(z, product, y_ref, z_ref, 1, at[0])
    local_stats(z, z_ref, hw_ref, stats_ref)
    copy.wait()


def gathered(z, at, parts, hold):
    half = z.G // 2
    for m in range(z.Q):
        hold[at[0] ^ m, :half] = parts[m][...]
        hold[at[0] ^ m, half:] = parts[z.Q + m][...]


def second_conv(z, at, *refs):
    hs, refs = refs[: 2 * z.Q], refs[2 * z.Q :]
    blocks, refs = refs[: z.S], refs[z.S :]
    hw_ref, outs, (z_ref, stats_ref, wcat, y_ref, h_ref) = refs[0], refs[1 : 1 + z.S], refs[1 + z.S :]
    gathered(z, at, hs, h_ref)
    fill_kernels(z, at, blocks, wcat)
    for j in range(z.Q):
        rows = slice(j * z.own, (j + 1) * z.own)
        split_channels(z, at, [h_ref[a, rows, :] for a in range(z.Q)], outs, rows)

    def product(j):
        rows = slice(j * z.own, (j + 1) * z.own)
        if z.L % LANES == 0:
            whole = jnp.concatenate([h_ref[i, rows, :] for i in range(z.Q)], axis=1)
            return jnp.dot(whole, wcat[...], preferred_element_type=F32)
        return sum(
            jnp.dot(h_ref[i, rows, :], wcat[i * z.L : (i + 1) * z.L, :], preferred_element_type=F32)
            for i in range(z.Q)
        )

    conv_into(z, product, y_ref, z_ref)
    local_stats(z, z_ref, hw_ref, stats_ref)


def merged(z, all_ref):
    counts = [all_ref[k, 0:1, : z.L] for k in range(z.S * z.Z)]
    means = [all_ref[k, 1:2, : z.L] for k in range(z.S * z.Z)]
    count = sum(counts)
    mean = sum(c * m for c, m in zip(counts, means)) / count
    squares = sum(
        all_ref[k, 2:3, : z.L] + counts[k] * (means[k] - mean) * (means[k] - mean)
        for k in range(z.S * z.Z)
    )
    return mean, lax.rsqrt(squares / count + EPS), count


def keep(ref, rows):
    used = rows[0].shape[1]
    ref[...] = jnp.concatenate(rows + [jnp.zeros((8 - len(rows), used), F32)], axis=0)


def over_images(z, step, init=0, unroll=2):
    px = z.H * z.W

    def one(n, carry):
        return step(n, pl.ds(pl.multiple_of(n * px, px), px), carry)

    return lax.fori_loop(0, z.n_group, one, init, unroll=unroll)


def over_halves(z, step, refs):
    px, count = z.H * z.W, z.n_group // 2
    for i, ref in enumerate(refs):

        def one(n, carry, i=i, ref=ref):
            rows = pl.ds(pl.multiple_of((i * count + n) * px, px), px)
            ref[pl.ds(pl.multiple_of(n * px, px), px), :] = step(i * count + n, rows)
            return carry

        lax.fori_loop(0, count, one, 0, unroll=2)


def hidden(z, at, z_ref, all_ref, hw_ref, par_ref, *refs):
    parts, (a_ref, b_ref, sum_ref, kernel_ref) = refs[: z.Q], refs[z.Q :]
    unpick(z, at, *parts, kernel_ref)
    mean, inv, count = merged(z, all_ref)
    keep(sum_ref, [mean, inv, count])
    gain, shift = par_ref[0:1, :], par_ref[1:2, :]

    def step(n, rows):
        mask = image_mask(z, hw_ref[n])
        return gelu(mask * (gain * ((z_ref[rows, :] - mean) * inv) + shift)).astype(BF16)

    over_halves(z, step, (a_ref, b_ref))


def middle(z, at, z_ref, all_ref, hw_ref, par_ref, x_ref, *refs):
    cot_ref, out_ref, d_ref, sum_ref, stats_ref = refs
    mean, inv, count = merged(z, all_ref)
    keep(sum_ref, [mean, inv, count])
    gain, shift = par_ref[2:3, :], par_ref[3:4, :]
    px = z.H * z.W
    carry = (jnp.zeros((1, z.L), F32), jnp.zeros((1, z.L), F32))
    for j in range(z.Q):

        def step(n, carry, j=j):
            local = pl.ds(pl.multiple_of(n * px, px), px)
            rows = pl.ds(pl.multiple_of(j * z.own + n * px, px), px)
            mask = image_mask(z, hw_ref[j * z.n_own + n])
            normed = (z_ref[rows, :] - mean) * inv
            summed = mask * (gain * normed + shift) + x_ref[rows, :].astype(F32)
            value, slope = gelu_both(summed)
            out_ref[j, local, :] = value.astype(BF16)
            d = cot_ref[rows, :].astype(F32) * slope
            d_ref[rows, :] = d
            masked = mask * d
            return (
                carry[0] + jnp.sum(masked, 0, keepdims=True),
                carry[1] + jnp.sum(masked * normed, 0, keepdims=True),
            )

        carry = lax.fori_loop(0, z.n_own, step, carry, unroll=2)
    spread(stats_ref, list(carry))


def norm_grad(z, row, z_ref, up_ref, sum_ref, all_ref, hw_ref, par_ref, a_ref, b_ref, whole_ref, par_grad_ref):
    mean, inv, count = sum_ref[0:1, :], sum_ref[1:2, :], sum_ref[2:3, :]
    shift_grad = sum(all_ref[k, 0:1, : z.L] for k in range(z.S * z.Z))
    gain_grad = sum(all_ref[k, 1:2, : z.L] for k in range(z.S * z.Z))
    keep(par_grad_ref, [gain_grad, shift_grad])
    gain = par_ref[row : row + 1, :]

    def step(n, rows):
        mask = image_mask(z, hw_ref[n])
        normed = (z_ref[rows, :] - mean) * inv
        grad = inv * mask * gain * (up_ref[rows, :] - (shift_grad + normed * gain_grad) / count)
        low = grad.astype(BF16)
        whole_ref[rows, :] = low
        return low

    over_halves(z, step, (a_ref, b_ref))


def back_product(z, at, dz_ref, blocks, wcat):
    for t, block in enumerate(blocks):
        s = at[1] ^ t
        for b in range(z.Z):
            for k in range(z.K):
                rows = pl.ds(pl.multiple_of(k * z.LP + s * z.IB, z.IB), z.IB)
                if z.L % LANES == 0:
                    wcat[0, rows, b * z.L : (b + 1) * z.L] = block[b, k]
                else:
                    wcat[b, rows, :] = block[b, k]
    contract = (((1,), (1,)), ((), ()))

    def product(j):
        rows = slice(j * z.own, (j + 1) * z.own)
        if z.L % LANES == 0:
            whole = jnp.concatenate([dz_ref[i, rows, :] for i in range(z.Q)], axis=1)
            return lax.dot_general(whole, wcat[0], contract, preferred_element_type=F32)
        return sum(
            lax.dot_general(dz_ref[i, rows, :], wcat[i], contract, preferred_element_type=F32)
            for i in range(z.Q)
        )

    return product


def back_scratch(z):
    if z.L % LANES == 0:
        wide = pltpu.VMEM((1, z.K * z.LP, z.C), BF16)
    else:
        wide = pltpu.VMEM((z.Z, z.K * z.LP, z.C // z.Z), BF16)
    return [wide, pltpu.VMEM((z.own, z.K * z.LP), F32), pltpu.VMEM((z.Q, z.G, z.L), BF16)]


def hidden_grad(z, at, *refs):
    dzs, refs = refs[: 2 * z.Q], refs[2 * z.Q :]
    blocks, refs = refs[: z.S], refs[z.S :]
    z_ref, sum_ref, hw_ref, par_ref, da_ref, stats_ref, wcat, y_ref, dz_ref = refs
    gathered(z, at, dzs, dz_ref)
    conv_into(z, back_product(z, at, dz_ref, blocks, wcat), y_ref, da_ref, -1)
    mean, inv = sum_ref[0:1, :], sum_ref[1:2, :]
    gain, shift = par_ref[0:1, :], par_ref[1:2, :]

    def step(n, rows, carry):
        mask = image_mask(z, hw_ref[n])
        normed = (z_ref[rows, :] - mean) * inv
        da = da_ref[rows, :] * gelu_both(mask * (gain * normed + shift))[1]
        da_ref[rows, :] = da
        masked = mask * da
        return (
            carry[0] + jnp.sum(masked, 0, keepdims=True),
            carry[1] + jnp.sum(masked * normed, 0, keepdims=True),
        )

    zero = jnp.zeros((1, z.L), F32)
    spread(stats_ref, list(over_images(z, step, (zero, zero))))


def input_part(z, at, a_ref, b_ref, w_ref, d_ref, *refs):
    outs, (moved_ref, dx_ref) = refs[: z.Q], refs[z.Q :]
    fill_moved(z, a_ref, b_ref, moved_ref)
    contract = (((1,), (1,)), ((), ()))
    for j in range(z.Q):
        rows = slice(j * z.own, (j + 1) * z.own)
        dx_ref[j] = lax.dot_general(moved_ref[rows, :], w_ref[...], contract, preferred_element_type=F32)
    for slot in range(z.Q):

        @pl.when(at[0] == slot)
        def _(slot=slot):
            for j in range(z.Q):
                lanes = slice(slot * z.L, (slot + 1) * z.L)
                dx_ref[j, :, lanes] = dx_ref[j, :, lanes] + d_ref[j * z.own : (j + 1) * z.own, :]

    for m in range(z.Q):
        outs[m][...] = dx_ref[at[0] ^ m].astype(outs[m].dtype)


def kernel_grad(z, at, *refs):
    features, refs = refs[: z.S], refs[z.S :]
    dzs, refs = refs[: z.S + 1], refs[z.S + 1 :]
    value_ref = None
    if len(refs) > z.Q + 2:
        value_ref, refs = refs[0], refs[1:]
    outs, (moved_ref, full_ref) = refs[: z.Q], refs[z.Q :]
    contract = (((0,), (0,)), ((), ()))
    half = z.G // 2
    for t in range(z.S):
        pair = (dzs[0], dzs[1]) if t == 0 else (dzs[1 + t].at[:half], dzs[1 + t].at[half:])
        fill_moved(z, *pair, moved_ref)
        part = lax.dot_general(features[t][...], moved_ref[...], contract, preferred_element_type=F32)
        full_ref[...] = part if t == 0 else full_ref[...] + part
    for r in range(z.Q):
        row = pl.multiple_of((at[0] ^ r) * z.IB, z.IB)
        for k in range(z.K):
            part = full_ref[pl.ds(row, z.IB), k * z.LP : k * z.LP + z.L]
            outs[r][k * z.IB : (k + 1) * z.IB, :] = part.astype(BF16)
        if value_ref is not None:
            outs[r][z.K * z.IB :, :] = value_ref[at[0] ^ r]


def route(z, at, *refs):
    parts, refs = refs[: z.Q], refs[z.Q :]
    outs, refs = refs[: z.Z], refs[z.Z :]
    hold = refs[-1]
    for r in range(z.Q):
        hold[at[2] ^ at[0] ^ r] = parts[r][: z.K * z.IB, :]
    for m in range(z.Z):
        outs[m][...] = hold[m]
    if len(refs) == 3:
        value_ref, slots, _ = refs
        for r in range(z.Q):
            slots[at[0] ^ r] = parts[r][z.K * z.IB :, :]
        for j in range(z.Q):
            value_ref[:, j * z.L : (j + 1) * z.L] = slots[j]


def total_of(z, *refs):
    refs[-1][...] = sum(ref[...].astype(F32) for ref in refs[:-1]).astype(refs[-1].dtype)


def direction_of(grad, first, second, param, decay):
    new_first = BETA * first + (1.0 - BETA) * grad
    new_second = BETA * second + (1.0 - BETA) * grad * grad
    move = new_first / BIAS / (jnp.sqrt(new_second / BIAS) + TINY) + decay * param
    return new_first, new_second, move


def moments(z, j, *refs):
    count = len(refs) - (7 if j else 12)
    parts, refs = refs[:count], refs[count:]
    w_ref, first_ref, second_ref, refs = *refs[:3], refs[3:]
    if j == 0:
        other_ref, g1_ref, g2_ref, refs = refs[0], refs[1], refs[2], refs[5:]
    nf_ref, ns_ref, u_ref, stats_ref = refs
    total_u = jnp.zeros((1, z.L), F32)
    total_w = jnp.zeros((1, z.L), F32)
    for k in range(z.K):
        grad = sum(part[k * z.IB : (k + 1) * z.IB, :].astype(F32) for part in parts)
        w = w_ref[0, k]
        nf, ns, u = direction_of(grad, first_ref[0, k], second_ref[0, k], w, DECAY)
        nf_ref[0, k] = nf
        ns_ref[0, k] = ns
        u_ref[k] = u
        total_u = total_u + jnp.sum(u * u, 0, keepdims=True)
        total_w = total_w + jnp.sum(w * w, 0, keepdims=True)
    if j:
        keep(stats_ref, [total_u, total_w])
    else:
        grads = [g1_ref[0:1, :], g1_ref[1:2, :], g2_ref[0:1, :], g2_ref[1:2, :]]
        spread(stats_ref, [total_u, other_ref[0:1, :], total_w, other_ref[1:2, :]] + grads)


def finish(z, all_ref, w_ref, u0_ref, u1_ref, np_ref, nf_ref, ns_ref, *outs):
    nw_ref, copy_ref, nnp_ref, nnf_ref, nns_ref, trust_ref = outs
    total = all_ref[0]
    for k in range(1, z.R * z.Z):
        total = total + all_ref[k]
    tops, bottoms = [], []
    for j in range(2):
        un = jnp.sqrt(jnp.sum(total[j : j + 1, : z.L], axis=1, keepdims=True))
        wn = jnp.sqrt(jnp.sum(total[2 + j : 3 + j, : z.L], axis=1, keepdims=True))
        tops.append(wn)
        bottoms.append(un)
        scale = RATE * (wn / (un + TINY))
        for k in range(z.K):
            new = w_ref[j, k] - scale * (u0_ref, u1_ref)[j][k]
            nw_ref[j, k] = new
            copy_ref[j, k] = new.astype(BF16)
    for j in range(z.Q):
        nnp_ref[:, j * z.L : (j + 1) * z.L] = all_ref[j * z.Z, 4:8, : z.L]
    param = np_ref[...]
    nf, ns, move = direction_of(nnp_ref[...], nf_ref[...], ns_ref[...], param, 0.0)
    nnf_ref[...] = nf
    nns_ref[...] = ns
    pn = jnp.sqrt(jnp.sum(param * param, axis=1, keepdims=True))
    qn = jnp.sqrt(jnp.sum(move * move, axis=1, keepdims=True))
    nnp_ref[...] = param - RATE * (pn / (qn + TINY)) * move
    for r in range(4):
        tops.append(pn[r : r + 1])
        bottoms.append(qn[r : r + 1])
    at_row = lax.broadcasted_iota(jnp.int32, (2, 6), 0)
    at_col = lax.broadcasted_iota(jnp.int32, (2, 6), 1)
    trust = jnp.zeros((2, 6), F32)
    for c in range(6):
        trust = jnp.where(at_col == c, jnp.where(at_row == 0, tops[c], bottoms[c]), trust)
    trust_ref[...] = trust


def pick(z, more, at, *refs):
    parts, refs = refs[: z.Z], refs[z.Z :]
    map_ref = None
    if more == "map":
        map_ref, valid_ref, refs = refs[0], refs[1], refs[2:]
        rows = []
        for n in range(z.n_own):
            valid = valid_ref[n].astype(F32)
            tall = jnp.sum(valid[:, 0:1], axis=0, keepdims=True)
            wide = jnp.sum(valid[0:1, :], axis=1, keepdims=True)
            rows += [jnp.broadcast_to(tall, (1, z.L)), jnp.broadcast_to(wide, (1, z.L))]
        rows.append(jnp.zeros((z.extra - len(rows), z.L), F32))
        sizes = jnp.concatenate(rows, axis=0).astype(BF16)
    if more == "keep":
        far_ref, outs, (hold, sem) = refs[0], refs[1:-2], refs[-2:]
    else:
        outs, hold = refs[:-1], refs[-1]
    for m in range(z.Z):
        hold[at[2] ^ m] = parts[m][...]
    if more == "keep":
        copy = pltpu.make_async_copy(hold, far_ref, sem)
        copy.start()
    for m in range(z.Q):
        for k in range(z.K):
            outs[m][k * z.IB : (k + 1) * z.IB, :] = hold[at[0] ^ m, k]
        if map_ref is not None:
            for slot in range(z.Q):

                @pl.when((at[0] ^ m) == slot)
                def _(m=m, slot=slot):
                    outs[m][z.K * z.IB : z.K * z.IB + z.own, :] = map_ref[:, slot * z.L : (slot + 1) * z.L]

            outs[m][z.K * z.IB + z.own :, :] = sizes

    if more == "keep":
        copy.wait()


def unpick(z, at, *refs):
    parts, refs = refs[: z.Q], refs[z.Q :]
    for m in range(z.Q):
        q = at[0] ^ m
        for k in range(z.K):
            refs[0][q, k] = parts[m][k * z.IB : (k + 1) * z.IB, :]
        if len(refs) > 1:
            start = z.K * z.IB
            refs[1][pl.ds(pl.multiple_of(q * z.own, z.own), z.own), :] = parts[m][start : start + z.own, :]
            for n in range(z.n_own):
                row = start + z.own + 2 * n
                two = jnp.broadcast_to(parts[m][row : row + 2, 0:1].astype(F32), (2, LANES))
                refs[2][q * z.n_own + n] = jnp.concatenate([two, jnp.zeros((6, LANES), F32)], axis=0)


def shards(z, images, masks, cotangent, weights, first, second, params, p_first, p_second):
    q, s, b = lax.axis_index("q"), lax.axis_index("s"), lax.axis_index("z")
    at = jnp.stack([q, s, b]).astype(jnp.int32)

    def over_z(v, m):
        return lax.ppermute(v, "z", [(i, i ^ m) for i in range(z.Z)]) if m else v

    def over_s(v, m):
        return lax.ppermute(v, "s", [(i, i ^ m) for i in range(z.S)]) if m else v

    def sharers(v):
        return lax.all_to_all(v, ("s", "z"), 0, 0)

    def over_q(v, m):
        return lax.ppermute(v, "q", [(i, i ^ m) for i in range(z.Q)]) if m else v

    def gather_z(w):
        return [over_z(w, m) for m in range(z.Z)]

    def gather(a, b):
        if z.Q != 4:
            return [over_q(v, m) for v in (a, b) for m in range(z.Q)]
        a1, a2, b1, b2 = over_q(a, 1), over_q(a, 2), over_q(b, 1), over_q(b, 2)
        return [a, a1, a2, over_q(a2, 1), b, b1, b2, over_q(b1, 2)]

    def share(packed):
        return [over_s(packed, t) for t in range(z.S)]

    rows = z.own
    GL = (z.G, z.L)
    HL = (z.G // 2, z.L)
    many = z.S * z.Z
    piece = (z.K, z.IB, z.L)
    blocks = near((z.Z, *piece), BF16)
    stat = near((many, 8, LANES))
    conv_scratch = [pltpu.VMEM((z.C, z.K * z.LP), BF16), pltpu.VMEM((rows, z.K * z.LP), F32)]
    grad_scratch = [pltpu.VMEM((z.G, z.K * z.LP), BF16), pltpu.VMEM((z.Q * z.IB, z.K * z.LP), F32)]
    cot_rows = cotangent.reshape(rows, z.C)
    image_rows = images.reshape(rows, z.C)

    low_one, low_two = (weights[j].astype(BF16) for j in range(2))
    one = [over_z(low_one, m) for m in range(z.Z)]
    xs = [over_q(image_rows, m) for m in range(z.Q)]
    one, low_two = together((one, low_two))
    hold = pltpu.VMEM((z.Z, *piece), BF16)
    picked = call(
        functools.partial(pick, z, "map"),
        [near((z.sent, z.L), BF16)] * z.Q,
        (at, *one, cot_rows, masks),
        [hold],
    )
    picked, xs = together((picked, xs))
    two = [over_z(low_two, m) for m in range(z.Z)]
    picked, two = together(([over_q(picked[m], m) for m in range(z.Q)], two))
    front_one, cots, hw = call(
        functools.partial(unpick, z),
        [blocks, near(GL, BF16), near((z.n_group, 8, LANES))],
        (at, *picked),
    )
    keep = away((z.Z, *piece), BF16)
    keep_two, *picked = call(
        functools.partial(pick, z, "keep"),
        [keep] + [near((z.K * z.IB, z.L), BF16)] * z.Q,
        (at, *two),
        [hold, pltpu.SemaphoreType.DMA],
        raw=(keep,),
    )
    w_far = away((z.C, z.K * z.LP), BF16)
    *x_parts, z1, x_slice, slice_params, stats, w_far = call(
        functools.partial(first_conv, z),
        [near((z.G, z.Q * z.IB), BF16)] * z.S
        + [
            near(GL),
            near(GL, BF16),
            near((4, z.L)),
            stat,
            w_far,
        ],
        (at, params, *xs, *share(front_one), hw),
        conv_scratch + [pltpu.SemaphoreType.DMA],
        limit=16,
        raw=(w_far,),
    )
    stats, picked = together((stats, picked))
    stats, picked = together((sharers(stats), [over_q(picked[m], m) for m in range(z.Q)]))
    ha, hb, sum_one, front_two = call(
        functools.partial(hidden, z),
        [near(HL, BF16), near(HL, BF16), near((8, z.L)), blocks],
        (at, z1, stats, hw, slice_params, *picked),
    )
    hs = gather(ha, hb)
    *h_parts, z2, stats = call(
        functools.partial(second_conv, z),
        [near((z.G, z.Q * z.IB), BF16)] * z.S + [near(GL), stat],
        (at, *hs, *share(front_two), hw),
        conv_scratch + [pltpu.VMEM((z.Q, *GL), BF16)],
        limit=16,
    )
    stats, x_parts, h_parts = together((stats, x_parts, h_parts))
    x_parts = [over_s(v, t) for t, v in enumerate(x_parts)]
    h_parts = [over_s(v, t) for t, v in enumerate(h_parts)]
    stats, x_parts, h_parts = together((sharers(stats), x_parts, h_parts))
    out, d, sum_two, stats = call(
        functools.partial(middle, z),
        [near((z.Q, rows, z.L), BF16), near(GL), near((8, z.L)), stat],
        (at, z2, stats, hw, slice_params, x_slice, cots),
    )
    da, db, dz, grad_two = call(
        functools.partial(norm_grad, z, 2),
        [near(HL, BF16), near(HL, BF16), near(GL, BF16), near((8, z.L))],
        (z2, d, sum_two, sharers(stats), hw, slice_params),
    )
    da, db, keep_two = together((da, db, keep_two))
    dz2s = gather(da, db)

    def gradient(features, a, b, whole, *value):
        more = rows if value else 0
        return call(
            functools.partial(kernel_grad, z),
            [near((z.K * z.IB + more, z.L), BF16)] * z.Q,
            (at, *features, a, b, *[over_s(whole, t) for t in range(1, z.S)], *value),
            grad_scratch,
            limit=14,
            cost=COST_GRAD,
        )

    def by_plane(parts):
        return [over_q(parts[r], r) for r in range(z.Q)]

    def along(parts):
        return [over_z(parts[m], m) for m in range(z.Z)]

    def update(j, parts, *more):
        whole = pl.BlockSpec(memory_space=pltpu.VMEM)
        block = pl.BlockSpec((1, *piece), lambda i: (j, 0, 0, 0))
        held = pl.BlockSpec(memory_space=pl.ANY)
        args = [pltpu.with_memory_space_constraint(v, pltpu.VMEM) for v in (*parts,)]
        args += [weights, first, second]
        specs = [whole] * len(parts) + [block] * 3
        if more:
            args += [pltpu.with_memory_space_constraint(v, pltpu.VMEM) for v in more[:3]] + list(more[3:])
            specs += [whole] * 3 + [held] * 2
        n = len(args)
        return pl.pallas_call(
            functools.partial(moments, z, j),
            grid=(1,),
            out_shape=[shape(weights.shape)] * 2
            + [near(piece), near((8, z.L)) if j else near((z.R * z.Z, 8, LANES))],
            in_specs=specs,
            out_specs=[block, block, whole, whole],
            input_output_aliases={} if j else {n - 2: 0, n - 1: 1},
            compiler_params=pltpu.CompilerParams(vmem_limit_bytes=8 * 1024 * 1024),
            cost_estimate=pl.CostEstimate(flops=1 if j else COST_GRAD, bytes_accessed=1, transcendentals=0),
        )(*args)

    parts_two = gradient(h_parts, da, db, dz, out)
    da1, stats = call(
        functools.partial(hidden_grad, z),
        [near(GL), stat],
        (at, *dz2s, *share(keep_two), z1, sum_one, hw, slice_params),
        back_scratch(z),
        limit=16,
    )
    stats, parts_two = together((stats, parts_two))
    stats, parts_two = together((sharers(stats), by_plane(parts_two)))
    da, db, dz, grad_one = call(
        functools.partial(norm_grad, z, 0),
        [near(HL, BF16), near(HL, BF16), near(GL, BF16), near((8, z.L))],
        (z1, da1, sum_one, stats, hw, slice_params),
    )
    flat = near((z.K * z.IB, z.L), BF16)
    hold = pltpu.VMEM((z.Z, z.K * z.IB, z.L), BF16)
    *parts_two, values = call(
        functools.partial(route, z),
        [flat] * z.Z + [near((rows, z.C), BF16)],
        (at, *parts_two),
        [pltpu.VMEM((z.Q, rows, z.L), BF16), hold],
        after=(da,),
    )
    parts_one = gradient(x_parts, da, db, dz)
    parts_one, parts_two = by_plane(parts_one), along(parts_two)
    parts_one, parts_two = together((parts_one, parts_two))
    dxs = call(
        functools.partial(input_part, z),
        [near((rows, z.C))] + [near((rows, z.C), BF16)] * (z.Q - 1),
        (at, da, db, w_far, d),
        [grad_scratch[0], pltpu.VMEM((z.Q, rows, z.C), F32)],
        limit=16,
        cost=COST_GRAD,
        far=(w_far,),
        after=(parts_one[0],),
    )
    parts_one = call(functools.partial(route, z), [flat] * z.Z, (at, *parts_one), [hold])
    parts_one, parts_two = together((parts_one, parts_two))
    parts_one = along(parts_one)
    new_first, new_second, move_two, other = update(1, parts_two)
    dxs = [over_q(dxs[m], m) for m in range(z.Q)]
    new_first, new_second, move_one, stats = update(
        0, parts_one, other, grad_one, grad_two, new_first, new_second
    )
    stats = lax.all_to_all(stats, ("s", "q", "z"), 0, 0)
    dx = call(functools.partial(total_of, z), shape((rows, z.C), BF16), tuple(dxs))
    new_weights, copies, new_params, new_p_first, new_p_second, trust = call(
        functools.partial(finish, z),
        [shape(weights.shape), shape(weights.shape, BF16)] + [shape(params.shape)] * 3 + [shape((2, 6))],
        (stats, weights, move_one, move_two, params, p_first, p_second),
    )
    return (
        values.reshape(images.shape),
        dx.reshape(images.shape),
        new_weights,
        copies,
        new_first,
        new_second,
        new_params,
        new_p_first,
        new_p_second,
        trust,
    )


def solution(mesh):
    def whole(images, masks, cotangent, weights, first, second, params, p_first, p_second):
        z = Sizes(mesh, images.shape, weights.shape)
        inner = Mesh(mesh.devices.reshape(z.Q, z.S, z.Z), ("q", "s", "z"))
        pixels = P(("q", "s", "z"), None, None, None)
        kernels = P(None, None, ("q", "s"), "z")
        return jax.shard_map(
            functools.partial(shards, z),
            mesh=inner,
            in_specs=(pixels, P(("q", "s", "z"), None, None), pixels, kernels, kernels, kernels, P(), P(), P()),
            out_specs=(pixels, pixels, kernels, kernels, kernels, kernels, P(), P(), P(), P()),
            check_vma=False,
        )(images, masks, cotangent, weights, first, second, params, p_first, p_second)

    return whole
```

```python
import functools

import jax
import jax.numpy as jnp
from jax import lax
from jax.experimental import pallas as pl
from jax.experimental.pallas import tpu as pltpu
from jax.sharding import Mesh
from jax.sharding import PartitionSpec as P

STEP = 3
RATE = 0.5
DECAY = 0.01
BETA = 0.5
BIAS = 1.0 - BETA**STEP
EPS = 1e-05
TINY = 1e-06
ROOT = 0.7978845608028654
CUBE = 0.044715
LANES = 128
COST_GRAD = 3 * 10**9
F32 = jnp.float32
BF16 = jnp.bfloat16


def gelu(v):
    return 0.5 * v * (1.0 + jnp.tanh(ROOT * (v + CUBE * (v * v * v))))


def gelu_both(v):
    t = jnp.tanh(ROOT * (v + CUBE * (v * v * v)))
    value = 0.5 * v * (1.0 + t)
    slope = 0.5 * (1.0 + t) + 0.5 * v * (1.0 - t * t) * (ROOT * (1.0 + (3.0 * CUBE) * (v * v)))
    return value, slope


class Sizes:
    def __init__(self, mesh, images, weights):
        self.Z = mesh.shape["ba"]
        self.R = mesh.shape["ha"] * mesh.shape["wa"]
        self.Q = self.Z
        self.S = self.R // self.Q
        n, self.H, self.W, self.C = images
        self.n_own = n // (self.R * self.Z)
        self.own = self.n_own * self.H * self.W
        self.n_group = self.n_own * self.Q
        self.G = self.own * self.Q
        self.L = self.C // self.Q
        self.LP = max(self.L, LANES)
        self.IB = self.C // self.R
        self.K = weights[1]
        self.extra = 16 * ((2 * self.n_own + 15) // 16)
        self.sent = self.K * self.IB + self.own + self.extra


def call(body, out_shape, args, scratch=(), limit=8, far=(), after=(), cost=1, raw=()):
    smem = [a.dtype == jnp.int32 and a.ndim == 1 for a in args]
    away = [any(a is f for f in far) for a in args]
    args = [
        a if m else pltpu.with_memory_space_constraint(a, pltpu.HBM if w else pltpu.VMEM)
        for a, m, w in zip(args, smem, away)
    ]
    n = len(args)

    def run(*refs):
        body(*refs[:n], *refs[n + len(after) :])

    return pl.pallas_call(
        run,
        out_shape=out_shape,
        in_specs=[pl.BlockSpec(memory_space=pltpu.SMEM if m else pltpu.VMEM) for m in smem]
        + [pl.BlockSpec(memory_space=pl.ANY)] * len(after),
        out_specs=jax.tree.map(
            lambda o: pl.BlockSpec(memory_space=pltpu.HBM if any(o is r for r in raw) else pltpu.VMEM),
            out_shape,
        ),
        scratch_shapes=list(scratch),
        compiler_params=pltpu.CompilerParams(vmem_limit_bytes=limit * 1024 * 1024),
        cost_estimate=pl.CostEstimate(flops=cost, bytes_accessed=1, transcendentals=0),
    )(*args, *after)


together = lax.optimization_barrier


def near(dims, dtype=F32):
    return pltpu.VMEM(tuple(dims), dtype)


def away(dims, dtype=F32):
    return pltpu.HBM(tuple(dims), dtype)


def shape(dims, dtype=F32):
    return jax.ShapeDtypeStruct(tuple(dims), dtype)


def image_mask(z, hw):
    dims = (z.H, z.W, z.L)
    rows = lax.broadcasted_iota(jnp.int32, dims, 0).astype(F32)
    cols = lax.broadcasted_iota(jnp.int32, dims, 1).astype(F32)
    tall = hw[0:1, : z.L].reshape(1, 1, z.L)
    wide = hw[1:2, : z.L].reshape(1, 1, z.L)
    return jnp.where((rows < tall) & (cols < wide), 1.0, 0.0).reshape(z.H * z.W, z.L)


def shifted_sum(z, taps, sign):
    dims = (z.n_own, z.H, z.W, z.L)
    cols = lax.broadcasted_iota(jnp.int32, dims, 2)
    total = None
    for c in range(3):
        column = None
        for r in range(3):
            part = taps(3 * r + c).reshape(dims)
            move = (r - 1) * sign
            if move == 1:
                part = jnp.concatenate([part[:, 1:], jnp.zeros_like(part[:, :1])], axis=1)
            elif move == -1:
                part = jnp.concatenate([jnp.zeros_like(part[:, :1]), part[:, :-1]], axis=1)
            column = part if column is None else column + part
        move = (c - 1) * sign
        if move:
            flat = column.reshape(z.n_own * z.H, z.W, z.L)
            flat = pltpu.roll(flat, (-move) % z.W, 1)
            column = flat.reshape(dims)
            edge = z.W - 1 if move == 1 else 0
            column = jnp.where(cols == edge, 0.0, column)
        total = column if total is None else total + column
    return total.reshape(z.own, z.L)


def moved_taps(z, feature):
    dims = (z.n_own, z.H, z.W, z.L)
    cols = lax.broadcasted_iota(jnp.int32, dims, 2)
    out = [None] * 9
    for c in range(3):
        move = 1 - c
        column = feature.reshape(dims)
        if move:
            flat = feature.reshape(z.n_own * z.H, z.W, z.L)
            column = pltpu.roll(flat, (-move) % z.W, 1).reshape(dims)
            edge = z.W - 1 if move == 1 else 0
            column = jnp.where(cols == edge, 0.0, column)
        for r in range(3):
            if r == 0:
                part = jnp.concatenate([column[:, 1:], jnp.zeros_like(column[:, :1])], axis=1)
            elif r == 2:
                part = jnp.concatenate([jnp.zeros_like(column[:, :1]), column[:, :-1]], axis=1)
            else:
                part = column
            out[3 * r + c] = part.reshape(z.own, z.L)
    return out


def fill_moved(z, a_ref, b_ref, moved_ref):
    half = z.Q // 2
    for j in range(z.Q):
        ref, at_row = (a_ref, j) if j < half else (b_ref, j - half)
        block = ref[at_row * z.own : (at_row + 1) * z.own, :].astype(F32)
        for k, part in enumerate(moved_taps(z, block)):
            moved_ref[j * z.own : (j + 1) * z.own, k * z.LP : k * z.LP + z.L] = part.astype(BF16)


def spread(ref, rows):
    used = rows[0].shape[1]
    if len(rows) < 8:
        rows = rows + [jnp.zeros((8 - len(rows), used), F32)]
    stat = jnp.concatenate(rows, axis=0)
    if used < LANES:
        stat = jnp.concatenate([stat, jnp.zeros((8, LANES - used), F32)], axis=1)
    for k in range(ref.shape[0]):
        ref[k] = stat


def local_stats(z, z_ref, hw_ref, stats_ref):
    px = z.H * z.W
    pivot = z_ref[0:1, :]

    def step(n, carry):
        mask = image_mask(z, hw_ref[n])
        centered = mask * (z_ref[pl.ds(pl.multiple_of(n * px, px), px), :] - pivot)
        return (
            carry[0] + jnp.sum(mask, 0, keepdims=True),
            carry[1] + jnp.sum(centered, 0, keepdims=True),
            carry[2] + jnp.sum(centered * centered, 0, keepdims=True),
        )

    zero = jnp.zeros((1, z.L), F32)
    count, total, squares = lax.fori_loop(0, z.n_group, step, (zero, zero, zero), unroll=4)
    offset = total / count
    spread(stats_ref, [count, pivot + offset, jnp.maximum(squares - total * offset, 0.0)])


def conv_into(z, product, y_ref, z_ref, sign=1, at_q=0):
    for j in range(z.Q):
        y_ref[...] = product(j)
        z_ref[pl.ds(pl.multiple_of((at_q ^ j) * z.own, z.own), z.own), :] = shifted_sum(
            z, lambda k: y_ref[:, k * z.LP : k * z.LP + z.L], sign
        )


def fill_kernels(z, at, blocks, wcat):
    for t, block in enumerate(blocks):
        s = at[1] ^ t
        for a in range(z.Z):
            pieces = isinstance(block, (list, tuple))
            row = pl.multiple_of((at[0] ^ a if pieces else a) * z.L + s * z.IB, z.IB)
            for k in range(z.K):
                part = block[a][k * z.IB : (k + 1) * z.IB, :] if pieces else block[a, k]
                wcat[pl.ds(row, z.IB), k * z.LP : k * z.LP + z.L] = part


def split_channels(z, at, slices, outs, rows):
    for s in range(z.S):

        @pl.when(at[1] == s)
        def _(s=s):
            for t in range(z.S):
                low = (s ^ t) * z.IB
                outs[t][rows, :] = jnp.concatenate([v[:, low : low + z.IB] for v in slices], axis=1)


def first_conv(z, at, np_ref, *refs):
    xs, refs = refs[: z.Q], refs[z.Q :]
    blocks = [refs[t * z.Q : (t + 1) * z.Q] for t in range(z.S)]
    refs = refs[z.S * z.Q :]
    outs, refs = refs[: z.S], refs[z.S :]
    z_ref, slice_ref, par_ref, hw_ref, stats_ref, far_w, wcat, y_ref, sem = refs
    for m in range(z.Q):
        for n in range(z.n_own):
            row = z.K * z.IB + 2 * n
            two = jnp.broadcast_to(blocks[0][m][row : row + 2, 0:1].astype(F32), (2, LANES))
            hw_ref[(at[0] ^ m) * z.n_own + n] = jnp.concatenate([two, jnp.zeros((6, LANES), F32)], axis=0)
    fill_kernels(z, at, blocks, wcat)
    copy = pltpu.make_async_copy(wcat, far_w, sem)
    copy.start()
    for m in range(z.Q):
        rows = pl.ds(pl.multiple_of((at[0] ^ m) * z.own, z.own), z.own)
        split_channels(z, at, [xs[m][:, a * z.L : (a + 1) * z.L] for a in range(z.Q)], outs, rows)
    for slot in range(z.Q):

        @pl.when(at[0] == slot)
        def _(slot=slot):
            par_ref[...] = np_ref[:, slot * z.L : (slot + 1) * z.L]
            for m in range(z.Q):
                j = slot ^ m
                slice_ref[j * z.own : (j + 1) * z.own, :] = xs[m][
                    :, slot * z.L : (slot + 1) * z.L
                ]

    def product(m):
        return jnp.dot(xs[m][...], wcat[...], preferred_element_type=F32)

    conv_into(z, product, y_ref, z_ref, 1, at[0])
    local_stats(z, z_ref, hw_ref, stats_ref)
    copy.wait()


def gathered(z, at, parts, hold):
    half = z.G // 2
    for m in range(z.Q):
        hold[at[0] ^ m, :half] = parts[m][...]
        hold[at[0] ^ m, half:] = parts[z.Q + m][...]


def second_conv(z, at, *refs):
    hs, refs = refs[: 2 * z.Q], refs[2 * z.Q :]
    blocks, refs = refs[: z.S], refs[z.S :]
    hw_ref, outs, (z_ref, stats_ref, wcat, y_ref, h_ref) = refs[0], refs[1 : 1 + z.S], refs[1 + z.S :]
    gathered(z, at, hs, h_ref)
    fill_kernels(z, at, blocks, wcat)
    for j in range(z.Q):
        rows = slice(j * z.own, (j + 1) * z.own)
        split_channels(z, at, [h_ref[a, rows, :] for a in range(z.Q)], outs, rows)

    def product(j):
        rows = slice(j * z.own, (j + 1) * z.own)
        if z.L % LANES == 0:
            whole = jnp.concatenate([h_ref[i, rows, :] for i in range(z.Q)], axis=1)
            return jnp.dot(whole, wcat[...], preferred_element_type=F32)
        return sum(
            jnp.dot(h_ref[i, rows, :], wcat[i * z.L : (i + 1) * z.L, :], preferred_element_type=F32)
            for i in range(z.Q)
        )

    conv_into(z, product, y_ref, z_ref)
    local_stats(z, z_ref, hw_ref, stats_ref)


def merged(z, all_ref):
    counts = [all_ref[k, 0:1, : z.L] for k in range(z.S * z.Z)]
    means = [all_ref[k, 1:2, : z.L] for k in range(z.S * z.Z)]
    count = sum(counts)
    mean = sum(c * m for c, m in zip(counts, means)) / count
    squares = sum(
        all_ref[k, 2:3, : z.L] + counts[k] * (means[k] - mean) * (means[k] - mean)
        for k in range(z.S * z.Z)
    )
    return mean, lax.rsqrt(squares / count + EPS), count


def keep(ref, rows):
    used = rows[0].shape[1]
    ref[...] = jnp.concatenate(rows + [jnp.zeros((8 - len(rows), used), F32)], axis=0)


def over_images(z, step, init=0, unroll=2):
    px = z.H * z.W

    def one(n, carry):
        return step(n, pl.ds(pl.multiple_of(n * px, px), px), carry)

    return lax.fori_loop(0, z.n_group, one, init, unroll=unroll)


def over_halves(z, step, refs):
    px, count = z.H * z.W, z.n_group // 2
    for i, ref in enumerate(refs):

        def one(n, carry, i=i, ref=ref):
            rows = pl.ds(pl.multiple_of((i * count + n) * px, px), px)
            ref[pl.ds(pl.multiple_of(n * px, px), px), :] = step(i * count + n, rows)
            return carry

        lax.fori_loop(0, count, one, 0, unroll=2)


def hidden(z, at, z_ref, all_ref, hw_ref, par_ref, *refs):
    parts, (a_ref, b_ref, sum_ref, kernel_ref, map_ref) = refs[: z.Q], refs[z.Q :]
    unpick(z, at, *parts, kernel_ref, map_ref)
    mean, inv, count = merged(z, all_ref)
    keep(sum_ref, [mean, inv, count])
    gain, shift = par_ref[0:1, :], par_ref[1:2, :]

    def step(n, rows):
        mask = image_mask(z, hw_ref[n])
        return gelu(mask * (gain * ((z_ref[rows, :] - mean) * inv) + shift)).astype(BF16)

    over_halves(z, step, (a_ref, b_ref))


def middle(z, at, z_ref, all_ref, hw_ref, par_ref, x_ref, *refs):
    cot_ref, out_ref, d_ref, sum_ref, stats_ref = refs
    mean, inv, count = merged(z, all_ref)
    keep(sum_ref, [mean, inv, count])
    gain, shift = par_ref[2:3, :], par_ref[3:4, :]
    px = z.H * z.W
    carry = (jnp.zeros((1, z.L), F32), jnp.zeros((1, z.L), F32))
    for j in range(z.Q):

        def step(n, carry, j=j):
            local = pl.ds(pl.multiple_of(n * px, px), px)
            rows = pl.ds(pl.multiple_of(j * z.own + n * px, px), px)
            mask = image_mask(z, hw_ref[j * z.n_own + n])
            normed = (z_ref[rows, :] - mean) * inv
            summed = mask * (gain * normed + shift) + x_ref[rows, :].astype(F32)
            value, slope = gelu_both(summed)
            out_ref[j, local, :] = value.astype(BF16)
            d = cot_ref[rows, :].astype(F32) * slope
            d_ref[rows, :] = d
            masked = mask * d
            return (
                carry[0] + jnp.sum(masked, 0, keepdims=True),
                carry[1] + jnp.sum(masked * normed, 0, keepdims=True),
            )

        carry = lax.fori_loop(0, z.n_own, step, carry, unroll=2)
    spread(stats_ref, list(carry))


def norm_grad(z, row, z_ref, up_ref, sum_ref, all_ref, hw_ref, par_ref, a_ref, b_ref, whole_ref, par_grad_ref):
    mean, inv, count = sum_ref[0:1, :], sum_ref[1:2, :], sum_ref[2:3, :]
    shift_grad = sum(all_ref[k, 0:1, : z.L] for k in range(z.S * z.Z))
    gain_grad = sum(all_ref[k, 1:2, : z.L] for k in range(z.S * z.Z))
    keep(par_grad_ref, [gain_grad, shift_grad])
    gain = par_ref[row : row + 1, :]

    def step(n, rows):
        mask = image_mask(z, hw_ref[n])
        normed = (z_ref[rows, :] - mean) * inv
        grad = inv * mask * gain * (up_ref[rows, :] - (shift_grad + normed * gain_grad) / count)
        low = grad.astype(BF16)
        whole_ref[rows, :] = low
        return low

    over_halves(z, step, (a_ref, b_ref))


def back_product(z, at, dz_ref, blocks, wcat):
    for t, block in enumerate(blocks):
        s = at[1] ^ t
        for b in range(z.Z):
            for k in range(z.K):
                rows = pl.ds(pl.multiple_of(k * z.LP + s * z.IB, z.IB), z.IB)
                if z.L % LANES == 0:
                    wcat[0, rows, b * z.L : (b + 1) * z.L] = block[b, k]
                else:
                    wcat[b, rows, :] = block[b, k]
    contract = (((1,), (1,)), ((), ()))

    def product(j):
        rows = slice(j * z.own, (j + 1) * z.own)
        if z.L % LANES == 0:
            whole = jnp.concatenate([dz_ref[i, rows, :] for i in range(z.Q)], axis=1)
            return lax.dot_general(whole, wcat[0], contract, preferred_element_type=F32)
        return sum(
            lax.dot_general(dz_ref[i, rows, :], wcat[i], contract, preferred_element_type=F32)
            for i in range(z.Q)
        )

    return product


def back_scratch(z):
    if z.L % LANES == 0:
        wide = pltpu.VMEM((1, z.K * z.LP, z.C), BF16)
    else:
        wide = pltpu.VMEM((z.Z, z.K * z.LP, z.C // z.Z), BF16)
    return [wide, pltpu.VMEM((z.own, z.K * z.LP), F32), pltpu.VMEM((z.Q, z.G, z.L), BF16)]


def hidden_grad(z, at, *refs):
    dzs, refs = refs[: 2 * z.Q], refs[2 * z.Q :]
    blocks, refs = refs[: z.S], refs[z.S :]
    z_ref, sum_ref, hw_ref, par_ref, da_ref, stats_ref, wcat, y_ref, dz_ref = refs
    gathered(z, at, dzs, dz_ref)
    conv_into(z, back_product(z, at, dz_ref, blocks, wcat), y_ref, da_ref, -1)
    mean, inv = sum_ref[0:1, :], sum_ref[1:2, :]
    gain, shift = par_ref[0:1, :], par_ref[1:2, :]

    def step(n, rows, carry):
        mask = image_mask(z, hw_ref[n])
        normed = (z_ref[rows, :] - mean) * inv
        da = da_ref[rows, :] * gelu_both(mask * (gain * normed + shift))[1]
        da_ref[rows, :] = da
        masked = mask * da
        return (
            carry[0] + jnp.sum(masked, 0, keepdims=True),
            carry[1] + jnp.sum(masked * normed, 0, keepdims=True),
        )

    zero = jnp.zeros((1, z.L), F32)
    spread(stats_ref, list(over_images(z, step, (zero, zero))))


def input_part(z, at, a_ref, b_ref, w_ref, d_ref, *refs):
    outs, (moved_ref, dx_ref) = refs[: z.Q], refs[z.Q :]
    fill_moved(z, a_ref, b_ref, moved_ref)
    contract = (((1,), (1,)), ((), ()))
    for j in range(z.Q):
        rows = slice(j * z.own, (j + 1) * z.own)
        dx_ref[j] = lax.dot_general(moved_ref[rows, :], w_ref[...], contract, preferred_element_type=F32)
    for slot in range(z.Q):

        @pl.when(at[0] == slot)
        def _(slot=slot):
            for j in range(z.Q):
                lanes = slice(slot * z.L, (slot + 1) * z.L)
                dx_ref[j, :, lanes] = dx_ref[j, :, lanes] + d_ref[j * z.own : (j + 1) * z.own, :]

    for m in range(z.Q):
        outs[m][...] = dx_ref[at[0] ^ m].astype(outs[m].dtype)


def kernel_grad(z, at, *refs):
    features, refs = refs[: z.S], refs[z.S :]
    dzs, refs = refs[: z.S + 1], refs[z.S + 1 :]
    value_ref = None
    if len(refs) > z.Q + 2:
        value_ref, refs = refs[0], refs[1:]
    outs, (moved_ref, full_ref) = refs[: z.Q], refs[z.Q :]
    contract = (((0,), (0,)), ((), ()))
    half = z.G // 2
    for t in range(z.S):
        pair = (dzs[0], dzs[1]) if t == 0 else (dzs[1 + t].at[:half], dzs[1 + t].at[half:])
        fill_moved(z, *pair, moved_ref)
        part = lax.dot_general(features[t][...], moved_ref[...], contract, preferred_element_type=F32)
        full_ref[...] = part if t == 0 else full_ref[...] + part
    for r in range(z.Q):
        row = pl.multiple_of((at[0] ^ r) * z.IB, z.IB)
        for k in range(z.K):
            part = full_ref[pl.ds(row, z.IB), k * z.LP : k * z.LP + z.L]
            outs[r][k * z.IB : (k + 1) * z.IB, :] = part.astype(BF16)
        if value_ref is not None:
            outs[r][z.K * z.IB :, :] = value_ref[at[0] ^ r]


def route(z, at, *refs):
    parts, refs = refs[: z.Q], refs[z.Q :]
    outs, refs = refs[: z.Z], refs[z.Z :]
    hold = refs[-1]
    for r in range(z.Q):
        hold[at[2] ^ at[0] ^ r] = parts[r][: z.K * z.IB, :]
    for m in range(z.Z):
        outs[m][...] = hold[m]
    if len(refs) == 3:
        value_ref, slots, _ = refs
        for r in range(z.Q):
            slots[at[0] ^ r] = parts[r][z.K * z.IB :, :]
        for j in range(z.Q):
            value_ref[:, j * z.L : (j + 1) * z.L] = slots[j]


def total_of(z, *refs):
    refs[-1][...] = sum(ref[...].astype(F32) for ref in refs[:-1]).astype(refs[-1].dtype)


def direction_of(grad, first, second, param, decay):
    new_first = BETA * first + (1.0 - BETA) * grad
    new_second = BETA * second + (1.0 - BETA) * grad * grad
    move = new_first / BIAS / (jnp.sqrt(new_second / BIAS) + TINY) + decay * param
    return new_first, new_second, move


def moments(z, j, *refs):
    count = len(refs) - (7 if j else 12)
    parts, refs = refs[:count], refs[count:]
    w_ref, first_ref, second_ref, refs = *refs[:3], refs[3:]
    if j == 0:
        other_ref, g1_ref, g2_ref, refs = refs[0], refs[1], refs[2], refs[5:]
    nf_ref, ns_ref, u_ref, stats_ref = refs
    total_u = jnp.zeros((1, z.L), F32)
    total_w = jnp.zeros((1, z.L), F32)
    for k in range(z.K):
        grad = sum(part[k * z.IB : (k + 1) * z.IB, :].astype(F32) for part in parts)
        w = w_ref[0, k]
        nf, ns, u = direction_of(grad, first_ref[0, k], second_ref[0, k], w, DECAY)
        nf_ref[0, k] = nf
        ns_ref[0, k] = ns
        u_ref[k] = u
        total_u = total_u + jnp.sum(u * u, 0, keepdims=True)
        total_w = total_w + jnp.sum(w * w, 0, keepdims=True)
    if j:
        keep(stats_ref, [total_u, total_w])
    else:
        grads = [g1_ref[0:1, :], g1_ref[1:2, :], g2_ref[0:1, :], g2_ref[1:2, :]]
        spread(stats_ref, [total_u, other_ref[0:1, :], total_w, other_ref[1:2, :]] + grads)


def finish(z, all_ref, w_ref, u0_ref, u1_ref, np_ref, nf_ref, ns_ref, *outs):
    nw_ref, copy_ref, nnp_ref, nnf_ref, nns_ref, trust_ref = outs
    total = all_ref[0]
    for k in range(1, z.R * z.Z):
        total = total + all_ref[k]
    tops, bottoms = [], []
    for j in range(2):
        un = jnp.sqrt(jnp.sum(total[j : j + 1, : z.L], axis=1, keepdims=True))
        wn = jnp.sqrt(jnp.sum(total[2 + j : 3 + j, : z.L], axis=1, keepdims=True))
        tops.append(wn)
        bottoms.append(un)
        scale = RATE * (wn / (un + TINY))
        for k in range(z.K):
            new = w_ref[j, k] - scale * (u0_ref, u1_ref)[j][k]
            nw_ref[j, k] = new
            copy_ref[j, k] = new.astype(BF16)
    for j in range(z.Q):
        nnp_ref[:, j * z.L : (j + 1) * z.L] = all_ref[j * z.Z, 4:8, : z.L]
    param = np_ref[...]
    nf, ns, move = direction_of(nnp_ref[...], nf_ref[...], ns_ref[...], param, 0.0)
    nnf_ref[...] = nf
    nns_ref[...] = ns
    pn = jnp.sqrt(jnp.sum(param * param, axis=1, keepdims=True))
    qn = jnp.sqrt(jnp.sum(move * move, axis=1, keepdims=True))
    nnp_ref[...] = param - RATE * (pn / (qn + TINY)) * move
    for r in range(4):
        tops.append(pn[r : r + 1])
        bottoms.append(qn[r : r + 1])
    at_row = lax.broadcasted_iota(jnp.int32, (2, 6), 0)
    at_col = lax.broadcasted_iota(jnp.int32, (2, 6), 1)
    trust = jnp.zeros((2, 6), F32)
    for c in range(6):
        trust = jnp.where(at_col == c, jnp.where(at_row == 0, tops[c], bottoms[c]), trust)
    trust_ref[...] = trust


def pick(z, first, at, *refs):
    parts, refs = refs[: z.Z], refs[z.Z :]
    if first:
        valid_ref, outs, hold = refs[0], refs[1:-1], refs[-1]
        rows = []
        for n in range(z.n_own):
            valid = valid_ref[n].astype(F32)
            tall = jnp.sum(valid[:, 0:1], axis=0, keepdims=True)
            wide = jnp.sum(valid[0:1, :], axis=1, keepdims=True)
            rows += [jnp.broadcast_to(tall, (1, z.L)), jnp.broadcast_to(wide, (1, z.L))]
        rows.append(jnp.zeros((z.extra - len(rows), z.L), F32))
        sizes = jnp.concatenate(rows, axis=0).astype(BF16)
    else:
        map_ref, far_ref, outs, (hold, sem) = refs[0], refs[1], refs[2:-2], refs[-2:]
    for m in range(z.Z):
        hold[at[2] ^ m] = parts[m][...]
    if not first:
        copy = pltpu.make_async_copy(hold, far_ref, sem)
        copy.start()
    for m in range(z.Q):
        for k in range(z.K):
            outs[m][k * z.IB : (k + 1) * z.IB, :] = hold[at[0] ^ m, k]
        if first:
            outs[m][z.K * z.IB :, :] = sizes
            continue
        for slot in range(z.Q):

            @pl.when((at[0] ^ m) == slot)
            def _(m=m, slot=slot):
                outs[m][z.K * z.IB :, :] = map_ref[:, slot * z.L : (slot + 1) * z.L]

    if not first:
        copy.wait()


def unpick(z, at, *refs):
    parts, (out_ref, map_ref) = refs[: z.Q], refs[z.Q :]
    for m in range(z.Q):
        q = at[0] ^ m
        for k in range(z.K):
            out_ref[q, k] = parts[m][k * z.IB : (k + 1) * z.IB, :]
        map_ref[pl.ds(pl.multiple_of(q * z.own, z.own), z.own), :] = parts[m][z.K * z.IB :, :]


def shards(z, images, masks, cotangent, weights, first, second, params, p_first, p_second):
    q, s, b = lax.axis_index("q"), lax.axis_index("s"), lax.axis_index("z")
    at = jnp.stack([q, s, b]).astype(jnp.int32)

    def over_z(v, m):
        return lax.ppermute(v, "z", [(i, i ^ m) for i in range(z.Z)]) if m else v

    def over_s(v, m):
        return lax.ppermute(v, "s", [(i, i ^ m) for i in range(z.S)]) if m else v

    def sharers(v):
        return lax.all_to_all(v, ("s", "z"), 0, 0)

    def over_q(v, m):
        return lax.ppermute(v, "q", [(i, i ^ m) for i in range(z.Q)]) if m else v

    def gather_z(w):
        return [over_z(w, m) for m in range(z.Z)]

    def gather(a, b):
        if z.Q != 4:
            return [over_q(v, m) for v in (a, b) for m in range(z.Q)]
        a1, a2, b1, b2 = over_q(a, 1), over_q(a, 2), over_q(b, 1), over_q(b, 2)
        return [a, a1, a2, over_q(a2, 1), b, b1, b2, over_q(b1, 2)]

    def share(packed):
        return [over_s(packed, t) for t in range(z.S)]

    rows = z.own
    GL = (z.G, z.L)
    HL = (z.G // 2, z.L)
    many = z.S * z.Z
    piece = (z.K, z.IB, z.L)
    blocks = near((z.Z, *piece), BF16)
    stat = near((many, 8, LANES))
    conv_scratch = [pltpu.VMEM((z.C, z.K * z.LP), BF16), pltpu.VMEM((rows, z.K * z.LP), F32)]
    grad_scratch = [pltpu.VMEM((z.G, z.K * z.LP), BF16), pltpu.VMEM((z.Q * z.IB, z.K * z.LP), F32)]
    cot_rows = cotangent.reshape(rows, z.C)
    image_rows = images.reshape(rows, z.C)

    low_one, low_two = (weights[j].astype(BF16) for j in range(2))
    one = [over_z(low_one, m) for m in range(z.Z)]
    xs = [over_q(image_rows, m) for m in range(z.Q)]
    one, low_two = together((one, low_two))
    hold = pltpu.VMEM((z.Z, *piece), BF16)
    picked = call(
        functools.partial(pick, z, True),
        [near((z.K * z.IB + z.extra, z.L), BF16)] * z.Q,
        (at, *one, masks),
        [hold],
    )
    picked, xs = together((picked, xs))
    two = [over_z(low_two, m) for m in range(z.Z)]
    front_one, two = together(([over_q(picked[m], m) for m in range(z.Q)], two))
    keep = away((z.Z, *piece), BF16)
    keep_two, *picked = call(
        functools.partial(pick, z, False),
        [keep] + [near((z.K * z.IB + rows, z.L), BF16)] * z.Q,
        (at, *two, cot_rows),
        [hold, pltpu.SemaphoreType.DMA],
        raw=(keep,),
    )
    w_far = away((z.C, z.K * z.LP), BF16)
    *x_parts, z1, x_slice, slice_params, hw, stats, w_far = call(
        functools.partial(first_conv, z),
        [near((z.G, z.Q * z.IB), BF16)] * z.S
        + [
            near(GL),
            near(GL, BF16),
            near((4, z.L)),
            near((z.n_group, 8, LANES)),
            stat,
            w_far,
        ],
        (at, params, *xs, *[over_s(v, t) for t in range(z.S) for v in front_one]),
        conv_scratch + [pltpu.SemaphoreType.DMA],
        limit=16,
        raw=(w_far,),
    )
    stats, picked = together((stats, picked))
    stats, picked = together((sharers(stats), [over_q(picked[m], m) for m in range(z.Q)]))
    ha, hb, sum_one, front_two, cots = call(
        functools.partial(hidden, z),
        [near(HL, BF16), near(HL, BF16), near((8, z.L)), blocks, near(GL, BF16)],
        (at, z1, stats, hw, slice_params, *picked),
    )
    hs = gather(ha, hb)
    *h_parts, z2, stats = call(
        functools.partial(second_conv, z),
        [near((z.G, z.Q * z.IB), BF16)] * z.S + [near(GL), stat],
        (at, *hs, *share(front_two), hw),
        conv_scratch + [pltpu.VMEM((z.Q, *GL), BF16)],
        limit=16,
    )
    stats, x_parts, h_parts = together((stats, x_parts, h_parts))
    x_parts = [over_s(v, t) for t, v in enumerate(x_parts)]
    h_parts = [over_s(v, t) for t, v in enumerate(h_parts)]
    stats, x_parts, h_parts = together((sharers(stats), x_parts, h_parts))
    out, d, sum_two, stats = call(
        functools.partial(middle, z),
        [near((z.Q, rows, z.L), BF16), near(GL), near((8, z.L)), stat],
        (at, z2, stats, hw, slice_params, x_slice, cots),
    )
    da, db, dz, grad_two = call(
        functools.partial(norm_grad, z, 2),
        [near(HL, BF16), near(HL, BF16), near(GL, BF16), near((8, z.L))],
        (z2, d, sum_two, sharers(stats), hw, slice_params),
    )
    da, db, keep_two = together((da, db, keep_two))
    dz2s = gather(da, db)

    def gradient(features, a, b, whole, *value):
        more = rows if value else 0
        return call(
            functools.partial(kernel_grad, z),
            [near((z.K * z.IB + more, z.L), BF16)] * z.Q,
            (at, *features, a, b, *[over_s(whole, t) for t in range(1, z.S)], *value),
            grad_scratch,
            limit=14,
            cost=COST_GRAD,
        )

    def by_plane(parts):
        return [over_q(parts[r], r) for r in range(z.Q)]

    def along(parts):
        return [over_z(parts[m], m) for m in range(z.Z)]

    def update(j, parts, *more):
        whole = pl.BlockSpec(memory_space=pltpu.VMEM)
        block = pl.BlockSpec((1, *piece), lambda i: (j, 0, 0, 0))
        held = pl.BlockSpec(memory_space=pl.ANY)
        args = [pltpu.with_memory_space_constraint(v, pltpu.VMEM) for v in (*parts,)]
        args += [weights, first, second]
        specs = [whole] * len(parts) + [block] * 3
        if more:
            args += [pltpu.with_memory_space_constraint(v, pltpu.VMEM) for v in more[:3]] + list(more[3:])
            specs += [whole] * 3 + [held] * 2
        n = len(args)
        return pl.pallas_call(
            functools.partial(moments, z, j),
            grid=(1,),
            out_shape=[shape(weights.shape)] * 2
            + [near(piece), near((8, z.L)) if j else near((z.R * z.Z, 8, LANES))],
            in_specs=specs,
            out_specs=[block, block, whole, whole],
            input_output_aliases={} if j else {n - 2: 0, n - 1: 1},
            compiler_params=pltpu.CompilerParams(vmem_limit_bytes=8 * 1024 * 1024),
            cost_estimate=pl.CostEstimate(flops=1 if j else COST_GRAD, bytes_accessed=1, transcendentals=0),
        )(*args)

    parts_two = gradient(h_parts, da, db, dz, out)
    da1, stats = call(
        functools.partial(hidden_grad, z),
        [near(GL), stat],
        (at, *dz2s, *share(keep_two), z1, sum_one, hw, slice_params),
        back_scratch(z),
        limit=16,
    )
    stats, parts_two = together((stats, parts_two))
    stats, parts_two = together((sharers(stats), by_plane(parts_two)))
    da, db, dz, grad_one = call(
        functools.partial(norm_grad, z, 0),
        [near(HL, BF16), near(HL, BF16), near(GL, BF16), near((8, z.L))],
        (z1, da1, sum_one, stats, hw, slice_params),
    )
    flat = near((z.K * z.IB, z.L), BF16)
    hold = pltpu.VMEM((z.Z, z.K * z.IB, z.L), BF16)
    *parts_two, values = call(
        functools.partial(route, z),
        [flat] * z.Z + [near((rows, z.C), BF16)],
        (at, *parts_two),
        [pltpu.VMEM((z.Q, rows, z.L), BF16), hold],
        after=(da,),
    )
    parts_one = gradient(x_parts, da, db, dz)
    parts_one, parts_two = by_plane(parts_one), along(parts_two)
    parts_one, parts_two = together((parts_one, parts_two))
    dxs = call(
        functools.partial(input_part, z),
        [near((rows, z.C))] + [near((rows, z.C), BF16)] * (z.Q - 1),
        (at, da, db, w_far, d),
        [grad_scratch[0], pltpu.VMEM((z.Q, rows, z.C), F32)],
        limit=16,
        cost=COST_GRAD,
        far=(w_far,),
        after=(parts_one[0],),
    )
    parts_one = call(functools.partial(route, z), [flat] * z.Z, (at, *parts_one), [hold])
    parts_one, parts_two = together((parts_one, parts_two))
    parts_one = along(parts_one)
    new_first, new_second, move_two, other = update(1, parts_two)
    dxs = [over_q(dxs[m], m) for m in range(z.Q)]
    new_first, new_second, move_one, stats = update(
        0, parts_one, other, grad_one, grad_two, new_first, new_second
    )
    stats = lax.all_to_all(stats, ("s", "q", "z"), 0, 0)
    dx = call(functools.partial(total_of, z), shape((rows, z.C), BF16), tuple(dxs))
    new_weights, copies, new_params, new_p_first, new_p_second, trust = call(
        functools.partial(finish, z),
        [shape(weights.shape), shape(weights.shape, BF16)] + [shape(params.shape)] * 3 + [shape((2, 6))],
        (stats, weights, move_one, move_two, params, p_first, p_second),
    )
    return (
        values.reshape(images.shape),
        dx.reshape(images.shape),
        new_weights,
        copies,
        new_first,
        new_second,
        new_params,
        new_p_first,
        new_p_second,
        trust,
    )


def solution(mesh):
    def whole(images, masks, cotangent, weights, first, second, params, p_first, p_second):
        z = Sizes(mesh, images.shape, weights.shape)
        inner = Mesh(mesh.devices.reshape(z.Q, z.S, z.Z), ("q", "s", "z"))
        pixels = P(("q", "s", "z"), None, None, None)
        kernels = P(None, None, ("q", "s"), "z")
        return jax.shard_map(
            functools.partial(shards, z),
            mesh=inner,
            in_specs=(pixels, P(("q", "s", "z"), None, None), pixels, kernels, kernels, kernels, P(), P(), P()),
            out_specs=(pixels, pixels, kernels, kernels, kernels, kernels, P(), P(), P(), P()),
            check_vma=False,
        )(images, masks, cotangent, weights, first, second, params, p_first, p_second)

    return whole
```

```python
import functools

import jax
import jax.numpy as jnp
from jax import lax
from jax.experimental import pallas as pl
from jax.experimental.pallas import tpu as pltpu
from jax.sharding import Mesh
from jax.sharding import PartitionSpec as P

STEP = 3
RATE = 0.5
DECAY = 0.01
BETA = 0.5
BIAS = 1.0 - BETA**STEP
EPS = 1e-05
TINY = 1e-06
ROOT = 0.7978845608028654
CUBE = 0.044715
LANES = 128
COST_GRAD = 3 * 10**9
F32 = jnp.float32
BF16 = jnp.bfloat16


def gelu(v):
    return 0.5 * v * (1.0 + jnp.tanh(ROOT * (v + CUBE * (v * v * v))))


def gelu_both(v):
    t = jnp.tanh(ROOT * (v + CUBE * (v * v * v)))
    value = 0.5 * v * (1.0 + t)
    slope = 0.5 * (1.0 + t) + 0.5 * v * (1.0 - t * t) * (ROOT * (1.0 + (3.0 * CUBE) * (v * v)))
    return value, slope


class Sizes:
    def __init__(self, mesh, images, weights):
        self.Z = mesh.shape["ba"]
        self.R = mesh.shape["ha"] * mesh.shape["wa"]
        self.Q = self.Z
        self.S = self.R // self.Q
        n, self.H, self.W, self.C = images
        self.n_own = n // (self.R * self.Z)
        self.own = self.n_own * self.H * self.W
        self.n_group = self.n_own * self.Q
        self.G = self.own * self.Q
        self.L = self.C // self.Q
        self.LP = max(self.L, LANES)
        self.IB = self.C // self.R
        self.K = weights[1]
        self.extra = 16 * ((2 * self.n_own + 15) // 16)
        self.sent = self.K * self.IB + self.own + self.extra


def call(body, out_shape, args, scratch=(), limit=8, far=(), after=(), cost=1, raw=()):
    smem = [a.dtype == jnp.int32 and a.ndim == 1 for a in args]
    away = [any(a is f for f in far) for a in args]
    args = [
        a if m else pltpu.with_memory_space_constraint(a, pltpu.HBM if w else pltpu.VMEM)
        for a, m, w in zip(args, smem, away)
    ]
    n = len(args)

    def run(*refs):
        body(*refs[:n], *refs[n + len(after) :])

    return pl.pallas_call(
        run,
        out_shape=out_shape,
        in_specs=[pl.BlockSpec(memory_space=pltpu.SMEM if m else pltpu.VMEM) for m in smem]
        + [pl.BlockSpec(memory_space=pl.ANY)] * len(after),
        out_specs=jax.tree.map(
            lambda o: pl.BlockSpec(memory_space=pltpu.HBM if any(o is r for r in raw) else pltpu.VMEM),
            out_shape,
        ),
        scratch_shapes=list(scratch),
        compiler_params=pltpu.CompilerParams(vmem_limit_bytes=limit * 1024 * 1024),
        cost_estimate=pl.CostEstimate(flops=cost, bytes_accessed=1, transcendentals=0),
    )(*args, *after)


together = lax.optimization_barrier


def near(dims, dtype=F32):
    return pltpu.VMEM(tuple(dims), dtype)


def away(dims, dtype=F32):
    return pltpu.HBM(tuple(dims), dtype)


def shape(dims, dtype=F32):
    return jax.ShapeDtypeStruct(tuple(dims), dtype)


def image_mask(z, hw):
    dims = (z.H, z.W, z.L)
    rows = lax.broadcasted_iota(jnp.int32, dims, 0).astype(F32)
    cols = lax.broadcasted_iota(jnp.int32, dims, 1).astype(F32)
    tall = hw[0:1, : z.L].reshape(1, 1, z.L)
    wide = hw[1:2, : z.L].reshape(1, 1, z.L)
    return jnp.where((rows < tall) & (cols < wide), 1.0, 0.0).reshape(z.H * z.W, z.L)


def shifted_sum(z, taps, sign):
    dims = (z.n_own, z.H, z.W, z.L)
    cols = lax.broadcasted_iota(jnp.int32, dims, 2)
    total = None
    for c in range(3):
        column = None
        for r in range(3):
            part = taps(3 * r + c).reshape(dims)
            move = (r - 1) * sign
            if move == 1:
                part = jnp.concatenate([part[:, 1:], jnp.zeros_like(part[:, :1])], axis=1)
            elif move == -1:
                part = jnp.concatenate([jnp.zeros_like(part[:, :1]), part[:, :-1]], axis=1)
            column = part if column is None else column + part
        move = (c - 1) * sign
        if move:
            flat = column.reshape(z.n_own * z.H, z.W, z.L)
            flat = pltpu.roll(flat, (-move) % z.W, 1)
            column = flat.reshape(dims)
            edge = z.W - 1 if move == 1 else 0
            column = jnp.where(cols == edge, 0.0, column)
        total = column if total is None else total + column
    return total.reshape(z.own, z.L)


def moved_taps(z, feature):
    dims = (z.n_own, z.H, z.W, z.L)
    cols = lax.broadcasted_iota(jnp.int32, dims, 2)
    out = [None] * 9
    for c in range(3):
        move = 1 - c
        column = feature.reshape(dims)
        if move:
            flat = feature.reshape(z.n_own * z.H, z.W, z.L)
            column = pltpu.roll(flat, (-move) % z.W, 1).reshape(dims)
            edge = z.W - 1 if move == 1 else 0
            column = jnp.where(cols == edge, 0.0, column)
        for r in range(3):
            if r == 0:
                part = jnp.concatenate([column[:, 1:], jnp.zeros_like(column[:, :1])], axis=1)
            elif r == 2:
                part = jnp.concatenate([jnp.zeros_like(column[:, :1]), column[:, :-1]], axis=1)
            else:
                part = column
            out[3 * r + c] = part.reshape(z.own, z.L)
    return out


def fill_moved(z, a_ref, b_ref, moved_ref):
    half = z.Q // 2
    for j in range(z.Q):
        ref, at_row = (a_ref, j) if j < half else (b_ref, j - half)
        block = ref[at_row * z.own : (at_row + 1) * z.own, :].astype(F32)
        for k, part in enumerate(moved_taps(z, block)):
            moved_ref[j * z.own : (j + 1) * z.own, k * z.LP : k * z.LP + z.L] = part.astype(BF16)


def spread(ref, rows):
    used, many = rows[0].shape[1], ref.shape[1]
    if len(rows) < many:
        rows = rows + [jnp.zeros((many - len(rows), used), F32)]
    stat = jnp.concatenate(rows, axis=0)
    if used < LANES:
        stat = jnp.concatenate([stat, jnp.zeros((many, LANES - used), F32)], axis=1)
    for k in range(ref.shape[0]):
        ref[k] = stat


def local_stats(z, z_ref, hw_ref, stats_ref):
    px = z.H * z.W
    pivot = z_ref[0:1, :]

    def step(n, carry):
        mask = image_mask(z, hw_ref[n])
        centered = mask * (z_ref[pl.ds(pl.multiple_of(n * px, px), px), :] - pivot)
        return (
            carry[0] + jnp.sum(mask, 0, keepdims=True),
            carry[1] + jnp.sum(centered, 0, keepdims=True),
            carry[2] + jnp.sum(centered * centered, 0, keepdims=True),
        )

    zero = jnp.zeros((1, z.L), F32)
    count, total, squares = lax.fori_loop(0, z.n_group, step, (zero, zero, zero), unroll=4)
    offset = total / count
    spread(stats_ref, [count, pivot + offset, jnp.maximum(squares - total * offset, 0.0)])


def conv_into(z, product, y_ref, z_ref, sign=1, at_q=0):
    for j in range(z.Q):
        y_ref[...] = product(j)
        z_ref[pl.ds(pl.multiple_of((at_q ^ j) * z.own, z.own), z.own), :] = shifted_sum(
            z, lambda k: y_ref[:, k * z.LP : k * z.LP + z.L], sign
        )


def fill_kernels(z, at, blocks, wcat):
    for t, block in enumerate(blocks):
        s = at[1] ^ t
        for a in range(z.Z):
            pieces = isinstance(block, (list, tuple))
            row = pl.multiple_of((at[0] ^ a if pieces else a) * z.L + s * z.IB, z.IB)
            for k in range(z.K):
                part = block[a][k * z.IB : (k + 1) * z.IB, :] if pieces else block[a, k]
                wcat[pl.ds(row, z.IB), k * z.LP : k * z.LP + z.L] = part


def split_channels(z, at, slices, outs, rows):
    for s in range(z.S):

        @pl.when(at[1] == s)
        def _(s=s):
            for t in range(z.S):
                low = (s ^ t) * z.IB
                outs[t][rows, :] = jnp.concatenate([v[:, low : low + z.IB] for v in slices], axis=1)


def split_images(z, at, np_ref, *refs):
    xs, outs, (slice_ref, par_ref) = refs[: z.Q], refs[z.Q : -2], refs[-2:]
    for m in range(z.Q):
        rows = pl.ds(pl.multiple_of((at[0] ^ m) * z.own, z.own), z.own)
        split_channels(z, at, [xs[m][:, a * z.L : (a + 1) * z.L] for a in range(z.Q)], outs, rows)
    for slot in range(z.Q):

        @pl.when(at[0] == slot)
        def _(slot=slot):
            par_ref[...] = np_ref[:, slot * z.L : (slot + 1) * z.L]
            for m in range(z.Q):
                j = slot ^ m
                slice_ref[j * z.own : (j + 1) * z.own, :] = xs[m][
                    :, slot * z.L : (slot + 1) * z.L
                ]


def first_conv(z, at, *refs):
    xs, refs = refs[: z.Q], refs[z.Q :]
    blocks = [refs[t * z.Q : (t + 1) * z.Q] for t in range(z.S)]
    refs = refs[z.S * z.Q :]
    z_ref, hw_ref, stats_ref, far_w, wcat, y_ref, sem = refs
    for m in range(z.Q):
        for n in range(z.n_own):
            row = z.K * z.IB + 2 * n
            two = jnp.broadcast_to(blocks[0][m][row : row + 2, 0:1].astype(F32), (2, LANES))
            hw_ref[(at[0] ^ m) * z.n_own + n] = jnp.concatenate([two, jnp.zeros((6, LANES), F32)], axis=0)
    fill_kernels(z, at, blocks, wcat)
    copy = pltpu.make_async_copy(wcat, far_w, sem)
    copy.start()

    def product(m):
        return jnp.dot(xs[m][...], wcat[...], preferred_element_type=F32)

    conv_into(z, product, y_ref, z_ref, 1, at[0])
    local_stats(z, z_ref, hw_ref, stats_ref)
    copy.wait()


def gathered(z, at, parts, hold):
    half = z.G // 2
    for m in range(z.Q):
        hold[at[0] ^ m, :half] = parts[m][...]
        hold[at[0] ^ m, half:] = parts[z.Q + m][...]


def second_conv(z, at, *refs):
    hs, refs = refs[: 2 * z.Q], refs[2 * z.Q :]
    blocks, refs = refs[: z.S], refs[z.S :]
    hw_ref, outs, (z_ref, stats_ref, wcat, y_ref, h_ref) = refs[0], refs[1 : 1 + z.S], refs[1 + z.S :]
    gathered(z, at, hs, h_ref)
    fill_kernels(z, at, blocks, wcat)
    for j in range(z.Q):
        rows = slice(j * z.own, (j + 1) * z.own)
        split_channels(z, at, [h_ref[a, rows, :] for a in range(z.Q)], outs, rows)

    def product(j):
        rows = slice(j * z.own, (j + 1) * z.own)
        if z.L % LANES == 0:
            whole = jnp.concatenate([h_ref[i, rows, :] for i in range(z.Q)], axis=1)
            return jnp.dot(whole, wcat[...], preferred_element_type=F32)
        return sum(
            jnp.dot(h_ref[i, rows, :], wcat[i * z.L : (i + 1) * z.L, :], preferred_element_type=F32)
            for i in range(z.Q)
        )

    conv_into(z, product, y_ref, z_ref)
    local_stats(z, z_ref, hw_ref, stats_ref)


def merged(z, all_ref):
    counts = [all_ref[k, 0:1, : z.L] for k in range(z.S * z.Z)]
    means = [all_ref[k, 1:2, : z.L] for k in range(z.S * z.Z)]
    count = sum(counts)
    mean = sum(c * m for c, m in zip(counts, means)) / count
    squares = sum(
        all_ref[k, 2:3, : z.L] + counts[k] * (means[k] - mean) * (means[k] - mean)
        for k in range(z.S * z.Z)
    )
    return mean, lax.rsqrt(squares / count + EPS), count


def keep(ref, rows):
    used = rows[0].shape[1]
    ref[...] = jnp.concatenate(rows + [jnp.zeros((8 - len(rows), used), F32)], axis=0)


def over_images(z, step, init=0, unroll=2):
    px = z.H * z.W

    def one(n, carry):
        return step(n, pl.ds(pl.multiple_of(n * px, px), px), carry)

    return lax.fori_loop(0, z.n_group, one, init, unroll=unroll)


def over_halves(z, step, refs):
    px, count = z.H * z.W, z.n_group // 2
    for i, ref in enumerate(refs):

        def one(n, carry, i=i, ref=ref):
            rows = pl.ds(pl.multiple_of((i * count + n) * px, px), px)
            ref[pl.ds(pl.multiple_of(n * px, px), px), :] = step(i * count + n, rows)
            return carry

        lax.fori_loop(0, count, one, 0, unroll=2)


def hidden(z, at, z_ref, all_ref, hw_ref, par_ref, *refs):
    parts, (a_ref, b_ref, sum_ref, kernel_ref, map_ref) = refs[: z.Q], refs[z.Q :]
    unpick(z, at, *parts, kernel_ref, map_ref)
    mean, inv, count = merged(z, all_ref)
    keep(sum_ref, [mean, inv, count])
    gain, shift = par_ref[0:1, :], par_ref[1:2, :]

    def step(n, rows):
        mask = image_mask(z, hw_ref[n])
        return gelu(mask * (gain * ((z_ref[rows, :] - mean) * inv) + shift)).astype(BF16)

    over_halves(z, step, (a_ref, b_ref))


def middle(z, at, z_ref, all_ref, hw_ref, par_ref, x_ref, *refs):
    cot_ref, out_ref, d_ref, sum_ref, stats_ref = refs
    mean, inv, count = merged(z, all_ref)
    keep(sum_ref, [mean, inv, count])
    gain, shift = par_ref[2:3, :], par_ref[3:4, :]
    px = z.H * z.W
    carry = (jnp.zeros((1, z.L), F32), jnp.zeros((1, z.L), F32))
    for j in range(z.Q):

        def step(n, carry, j=j):
            local = pl.ds(pl.multiple_of(n * px, px), px)
            rows = pl.ds(pl.multiple_of(j * z.own + n * px, px), px)
            mask = image_mask(z, hw_ref[j * z.n_own + n])
            normed = (z_ref[rows, :] - mean) * inv
            summed = mask * (gain * normed + shift) + x_ref[rows, :].astype(F32)
            value, slope = gelu_both(summed)
            out_ref[j, local, :] = value.astype(BF16)
            d = cot_ref[rows, :].astype(F32) * slope
            d_ref[rows, :] = d
            masked = mask * d
            return (
                carry[0] + jnp.sum(masked, 0, keepdims=True),
                carry[1] + jnp.sum(masked * normed, 0, keepdims=True),
            )

        carry = lax.fori_loop(0, z.n_own, step, carry, unroll=2)
    spread(stats_ref, list(carry))


def norm_grad(z, row, z_ref, up_ref, sum_ref, all_ref, hw_ref, par_ref, a_ref, b_ref, whole_ref, par_grad_ref):
    mean, inv, count = sum_ref[0:1, :], sum_ref[1:2, :], sum_ref[2:3, :]
    shift_grad = sum(all_ref[k, 0:1, : z.L] for k in range(z.S * z.Z))
    gain_grad = sum(all_ref[k, 1:2, : z.L] for k in range(z.S * z.Z))
    keep(par_grad_ref, [gain_grad, shift_grad])
    gain = par_ref[row : row + 1, :]

    def step(n, rows):
        mask = image_mask(z, hw_ref[n])
        normed = (z_ref[rows, :] - mean) * inv
        grad = inv * mask * gain * (up_ref[rows, :] - (shift_grad + normed * gain_grad) / count)
        low = grad.astype(BF16)
        whole_ref[rows, :] = low
        return low

    over_halves(z, step, (a_ref, b_ref))


def hidden_slope(z, at, *refs):
    blocks, (z_ref, sum_ref, hw_ref, par_ref, wcat, slope_ref) = refs[: z.S], refs[z.S :]
    for t, block in enumerate(blocks):
        s = at[1] ^ t
        for b in range(z.Z):
            for k in range(z.K):
                rows = pl.ds(pl.multiple_of(k * z.LP + s * z.IB, z.IB), z.IB)
                if z.L % LANES == 0:
                    wcat[0, rows, b * z.L : (b + 1) * z.L] = block[b, k]
                else:
                    wcat[b, rows, :] = block[b, k]
    mean, inv = sum_ref[0:1, :], sum_ref[1:2, :]
    gain, shift = par_ref[0:1, :], par_ref[1:2, :]

    def step(n, rows, carry):
        normed = (z_ref[rows, :] - mean) * inv
        slope_ref[rows, :] = gelu_both(image_mask(z, hw_ref[n]) * (gain * normed + shift))[1]
        return carry

    over_images(z, step)


def back_product(z, dz_ref, wcat):
    contract = (((1,), (1,)), ((), ()))

    def product(j):
        rows = slice(j * z.own, (j + 1) * z.own)
        if z.L % LANES == 0:
            whole = jnp.concatenate([dz_ref[i, rows, :] for i in range(z.Q)], axis=1)
            return lax.dot_general(whole, wcat[0], contract, preferred_element_type=F32)
        return sum(
            lax.dot_general(dz_ref[i, rows, :], wcat[i], contract, preferred_element_type=F32)
            for i in range(z.Q)
        )

    return product


def back_wide(z):
    if z.L % LANES == 0:
        return near((1, z.K * z.LP, z.C), BF16)
    return near((z.Z, z.K * z.LP, z.C // z.Z), BF16)


def hidden_grad(z, at, *refs):
    dzs, refs = refs[: 2 * z.Q], refs[2 * z.Q :]
    wcat, slope_ref, z_ref, sum_ref, hw_ref, da_ref, stats_ref, y_ref, dz_ref = refs
    gathered(z, at, dzs, dz_ref)
    conv_into(z, back_product(z, dz_ref, wcat), y_ref, da_ref, -1)
    mean, inv = sum_ref[0:1, :], sum_ref[1:2, :]

    def step(n, rows, carry):
        mask = image_mask(z, hw_ref[n])
        normed = (z_ref[rows, :] - mean) * inv
        da = da_ref[rows, :] * slope_ref[rows, :]
        da_ref[rows, :] = da
        masked = mask * da
        return (
            carry[0] + jnp.sum(masked, 0, keepdims=True),
            carry[1] + jnp.sum(masked * normed, 0, keepdims=True),
        )

    zero = jnp.zeros((1, z.L), F32)
    spread(stats_ref, list(over_images(z, step, (zero, zero))))


def input_part(z, at, a_ref, b_ref, w_ref, d_ref, *refs):
    outs, (moved_ref, dx_ref) = refs[: z.Q], refs[z.Q :]
    fill_moved(z, a_ref, b_ref, moved_ref)
    contract = (((1,), (1,)), ((), ()))
    for j in range(z.Q):
        rows = slice(j * z.own, (j + 1) * z.own)
        dx_ref[j] = lax.dot_general(moved_ref[rows, :], w_ref[...], contract, preferred_element_type=F32)
    for slot in range(z.Q):

        @pl.when(at[0] == slot)
        def _(slot=slot):
            for j in range(z.Q):
                lanes = slice(slot * z.L, (slot + 1) * z.L)
                dx_ref[j, :, lanes] = dx_ref[j, :, lanes] + d_ref[j * z.own : (j + 1) * z.own, :]

    for m in range(z.Q):
        outs[m][...] = dx_ref[at[0] ^ m].astype(outs[m].dtype)


def kernel_grad(z, at, *refs):
    features, refs = refs[: z.S], refs[z.S :]
    dzs, refs = refs[: z.S + 1], refs[z.S + 1 :]
    value_ref = None
    if len(refs) > z.Q + 2:
        value_ref, refs = refs[0], refs[1:]
    outs, (moved_ref, full_ref) = refs[: z.Q], refs[z.Q :]
    contract = (((0,), (0,)), ((), ()))
    half = z.G // 2
    for t in range(z.S):
        pair = (dzs[0], dzs[1]) if t == 0 else (dzs[1 + t].at[:half], dzs[1 + t].at[half:])
        fill_moved(z, *pair, moved_ref)
        part = lax.dot_general(features[t][...], moved_ref[...], contract, preferred_element_type=F32)
        full_ref[...] = part if t == 0 else full_ref[...] + part
    for r in range(z.Q):
        row = pl.multiple_of((at[0] ^ r) * z.IB, z.IB)
        for k in range(z.K):
            part = full_ref[pl.ds(row, z.IB), k * z.LP : k * z.LP + z.L]
            outs[r][k * z.IB : (k + 1) * z.IB, :] = part.astype(BF16)
        if value_ref is not None:
            outs[r][z.K * z.IB :, :] = value_ref[at[0] ^ r]


def route(z, at, *refs):
    parts, refs = refs[: z.Q], refs[z.Q :]
    outs, refs = refs[: z.Z], refs[z.Z :]
    hold = refs[-1]
    for r in range(z.Q):
        hold[at[2] ^ at[0] ^ r] = parts[r][: z.K * z.IB, :]
    for m in range(z.Z):
        outs[m][...] = hold[m]
    if len(refs) == 3:
        value_ref, slots, _ = refs
        for r in range(z.Q):
            slots[at[0] ^ r] = parts[r][z.K * z.IB :, :]
        for j in range(z.Q):
            value_ref[:, j * z.L : (j + 1) * z.L] = slots[j]


def total_of(z, *refs):
    refs[-1][...] = sum(ref[...].astype(F32) for ref in refs[:-1]).astype(refs[-1].dtype)


def direction_of(grad, first, second, param, decay):
    new_first = BETA * first + (1.0 - BETA) * grad
    new_second = BETA * second + (1.0 - BETA) * grad * grad
    move = new_first / BIAS / (jnp.sqrt(new_second / BIAS) + TINY) + decay * param
    return new_first, new_second, move


def moments(z, j, *refs):
    count = len(refs) - 10
    parts, refs = refs[:count], refs[count:]
    w_ref, first_ref, second_ref, refs = *refs[:3], refs[3:]
    if j:
        g1_ref, g2_ref, at, refs = *refs[:3], refs[3:]
    else:
        other_ref, refs = refs[0], refs[3:]
    nf_ref, ns_ref, u_ref, stats_ref = refs
    total_u = jnp.zeros((1, z.L), F32)
    total_w = jnp.zeros((1, z.L), F32)
    for k in range(z.K):
        grad = sum(part[k * z.IB : (k + 1) * z.IB, :].astype(F32) for part in parts)
        w = w_ref[0, k]
        nf, ns, u = direction_of(grad, first_ref[0, k], second_ref[0, k], w, DECAY)
        nf_ref[0, k] = nf
        ns_ref[0, k] = ns
        u_ref[k] = u
        total_u = total_u + jnp.sum(u * u, 0, keepdims=True)
        total_w = total_w + jnp.sum(w * w, 0, keepdims=True)
    lane = lax.broadcasted_iota(jnp.int32, (1, z.L), 1)
    sums = jnp.zeros((1, z.L), F32) if j else other_ref[0:1, :]
    for c, v in enumerate([total_u, total_w]):
        sums = jnp.where(lane == 2 * c + j, jnp.sum(v, axis=1, keepdims=True), sums)
    if j:
        own = jnp.zeros((1, z.L), F32)
        for r, v in enumerate([g1_ref[0:1, :], g1_ref[1:2, :], g2_ref[0:1, :], g2_ref[1:2, :]]):
            own = jnp.where(at[2] == r, v, own)
        keep(stats_ref, [sums, own])
    else:
        spread(stats_ref, [sums, other_ref[1:2, :]])


def finish(z, all_ref, w_ref, u0_ref, u1_ref, np_ref, nf_ref, ns_ref, *outs):
    nw_ref, copy_ref, nnp_ref, nnf_ref, nns_ref, trust_ref = outs
    total = all_ref[0, 0:1, :]
    for k in range(1, z.R * z.Z):
        total = total + all_ref[k, 0:1, :]
    tops, bottoms = [], []
    for j in range(2):
        un = jnp.sqrt(total[:, j : j + 1])
        wn = jnp.sqrt(total[:, 2 + j : 3 + j])
        tops.append(wn)
        bottoms.append(un)
        scale = RATE * (wn / (un + TINY))
        for k in range(z.K):
            new = w_ref[j, k] - scale * (u0_ref, u1_ref)[j][k]
            nw_ref[j, k] = new
            copy_ref[j, k] = new.astype(BF16)
    for j in range(z.Q):
        for r in range(4):
            nnp_ref[r : r + 1, j * z.L : (j + 1) * z.L] = all_ref[j * z.Z + r, 1:2, : z.L]
    param = np_ref[...]
    nf, ns, move = direction_of(nnp_ref[...], nf_ref[...], ns_ref[...], param, 0.0)
    nnf_ref[...] = nf
    nns_ref[...] = ns
    pn = jnp.sqrt(jnp.sum(param * param, axis=1, keepdims=True))
    qn = jnp.sqrt(jnp.sum(move * move, axis=1, keepdims=True))
    nnp_ref[...] = param - RATE * (pn / (qn + TINY)) * move
    for r in range(4):
        tops.append(pn[r : r + 1])
        bottoms.append(qn[r : r + 1])
    at_row = lax.broadcasted_iota(jnp.int32, (2, 6), 0)
    at_col = lax.broadcasted_iota(jnp.int32, (2, 6), 1)
    trust = jnp.zeros((2, 6), F32)
    for c in range(6):
        trust = jnp.where(at_col == c, jnp.where(at_row == 0, tops[c], bottoms[c]), trust)
    trust_ref[...] = trust


def pick(z, first, at, *refs):
    parts, refs = refs[: z.Z], refs[z.Z :]
    if first:
        valid_ref, outs, hold = refs[0], refs[1:-1], refs[-1]
        rows = []
        for n in range(z.n_own):
            valid = valid_ref[n].astype(F32)
            tall = jnp.sum(valid[:, 0:1], axis=0, keepdims=True)
            wide = jnp.sum(valid[0:1, :], axis=1, keepdims=True)
            rows += [jnp.broadcast_to(tall, (1, z.L)), jnp.broadcast_to(wide, (1, z.L))]
        rows.append(jnp.zeros((z.extra - len(rows), z.L), F32))
        sizes = jnp.concatenate(rows, axis=0).astype(BF16)
    else:
        map_ref, far_ref, outs, (hold, sem) = refs[0], refs[1], refs[2:-2], refs[-2:]
    for m in range(z.Z):
        hold[at[2] ^ m] = parts[m][...]
    if not first:
        copy = pltpu.make_async_copy(hold, far_ref, sem)
        copy.start()
    for m in range(z.Q):
        for k in range(z.K):
            outs[m][k * z.IB : (k + 1) * z.IB, :] = hold[at[0] ^ m, k]
        if first:
            outs[m][z.K * z.IB :, :] = sizes
            continue
        for slot in range(z.Q):

            @pl.when((at[0] ^ m) == slot)
            def _(m=m, slot=slot):
                outs[m][z.K * z.IB :, :] = map_ref[:, slot * z.L : (slot + 1) * z.L]

    if not first:
        copy.wait()


def unpick(z, at, *refs):
    parts, (out_ref, map_ref) = refs[: z.Q], refs[z.Q :]
    for m in range(z.Q):
        q = at[0] ^ m
        for k in range(z.K):
            out_ref[q, k] = parts[m][k * z.IB : (k + 1) * z.IB, :]
        map_ref[pl.ds(pl.multiple_of(q * z.own, z.own), z.own), :] = parts[m][z.K * z.IB :, :]


def shards(z, images, masks, cotangent, weights, first, second, params, p_first, p_second):
    q, s, b = lax.axis_index("q"), lax.axis_index("s"), lax.axis_index("z")
    at = jnp.stack([q, s, b]).astype(jnp.int32)

    def over_z(v, m):
        return lax.ppermute(v, "z", [(i, i ^ m) for i in range(z.Z)]) if m else v

    def over_s(v, m):
        return lax.ppermute(v, "s", [(i, i ^ m) for i in range(z.S)]) if m else v

    def sharers(v):
        return lax.all_to_all(v, ("s", "z"), 0, 0)

    def over_q(v, m):
        return lax.ppermute(v, "q", [(i, i ^ m) for i in range(z.Q)]) if m else v

    def gather_z(w):
        return [over_z(w, m) for m in range(z.Z)]

    def gather(a, b):
        if z.Q != 4:
            return [over_q(v, m) for v in (a, b) for m in range(z.Q)]
        a1, a2, b1, b2 = over_q(a, 1), over_q(a, 2), over_q(b, 1), over_q(b, 2)
        return [a, a1, a2, over_q(a2, 1), b, b1, b2, over_q(b1, 2)]

    def share(packed):
        return [over_s(packed, t) for t in range(z.S)]

    rows = z.own
    GL = (z.G, z.L)
    HL = (z.G // 2, z.L)
    many = z.S * z.Z
    piece = (z.K, z.IB, z.L)
    blocks = near((z.Z, *piece), BF16)
    stat, pair = near((many, 4, LANES)), near((many, 2, LANES))
    conv_scratch = [pltpu.VMEM((z.C, z.K * z.LP), BF16), pltpu.VMEM((rows, z.K * z.LP), F32)]
    grad_scratch = [pltpu.VMEM((z.G, z.K * z.LP), BF16), pltpu.VMEM((z.Q * z.IB, z.K * z.LP), F32)]
    cot_rows = cotangent.reshape(rows, z.C)
    image_rows = images.reshape(rows, z.C)

    low_one, low_two = (weights[j].astype(BF16) for j in range(2))
    one = [over_z(low_one, m) for m in range(z.Z)]
    xs = [over_q(image_rows, m) for m in range(z.Q)]
    one, low_two = together((one, low_two))
    hold = pltpu.VMEM((z.Z, *piece), BF16)
    picked = call(
        functools.partial(pick, z, True),
        [near((z.K * z.IB + z.extra, z.L), BF16)] * z.Q,
        (at, *one, masks),
        [hold],
    )
    picked, xs = together((picked, xs))
    two = [over_z(low_two, m) for m in range(z.Z)]
    *x_parts, x_slice, slice_params = call(
        functools.partial(split_images, z),
        [near((z.G, z.Q * z.IB), BF16)] * z.S + [near(GL, BF16), near((4, z.L))],
        (at, params, *xs),
    )
    front_one = [over_q(picked[m], m) for m in range(z.Q)]
    front_one, x_parts, two = together((front_one, x_parts, two))
    keep = away((z.Z, *piece), BF16)
    keep_two, *picked = call(
        functools.partial(pick, z, False),
        [keep] + [near((z.K * z.IB + rows, z.L), BF16)] * z.Q,
        (at, *two, cot_rows),
        [hold, pltpu.SemaphoreType.DMA],
        raw=(keep,),
    )
    w_far = away((z.C, z.K * z.LP), BF16)
    z1, hw, stats, w_far = call(
        functools.partial(first_conv, z),
        [near(GL), near((z.n_group, 8, LANES)), stat, w_far],
        (at, *xs, *[over_s(v, t) for t in range(z.S) for v in front_one]),
        conv_scratch + [pltpu.SemaphoreType.DMA],
        limit=16,
        raw=(w_far,),
    )
    stats, picked = together((stats, picked))
    stats, picked = together((sharers(stats), [over_q(picked[m], m) for m in range(z.Q)]))
    ha, hb, sum_one, front_two, cots = call(
        functools.partial(hidden, z),
        [near(HL, BF16), near(HL, BF16), near((8, z.L)), blocks, near(GL, BF16)],
        (at, z1, stats, hw, slice_params, *picked),
    )
    hs = gather(ha, hb)
    *h_parts, z2, stats = call(
        functools.partial(second_conv, z),
        [near((z.G, z.Q * z.IB), BF16)] * z.S + [near(GL), stat],
        (at, *hs, *share(front_two), hw),
        conv_scratch + [pltpu.VMEM((z.Q, *GL), BF16)],
        limit=16,
    )
    stats, x_parts, h_parts = together((stats, x_parts, h_parts))
    x_parts = [over_s(v, t) for t, v in enumerate(x_parts)]
    h_parts = [over_s(v, t) for t, v in enumerate(h_parts)]
    stats, x_parts, h_parts = together((sharers(stats), x_parts, h_parts))
    out, d, sum_two, stats = call(
        functools.partial(middle, z),
        [near((z.Q, rows, z.L), BF16), near(GL), near((8, z.L)), pair],
        (at, z2, stats, hw, slice_params, x_slice, cots),
    )
    da, db, dz, grad_two = call(
        functools.partial(norm_grad, z, 2),
        [near(HL, BF16), near(HL, BF16), near(GL, BF16), near((8, z.L))],
        (z2, d, sum_two, sharers(stats), hw, slice_params),
    )
    da, db, keep_two = together((da, db, keep_two))
    dz2s = gather(da, db)

    def gradient(features, a, b, whole, *value):
        more = rows if value else 0
        return call(
            functools.partial(kernel_grad, z),
            [near((z.K * z.IB + more, z.L), BF16)] * z.Q,
            (at, *features, a, b, *[over_s(whole, t) for t in range(1, z.S)], *value),
            grad_scratch,
            limit=14,
            cost=COST_GRAD,
        )

    def by_plane(parts):
        return [over_q(parts[r], r) for r in range(z.Q)]

    def along(parts):
        return [over_z(parts[m], m) for m in range(z.Z)]

    def update(j, parts, *more):
        whole = pl.BlockSpec(memory_space=pltpu.VMEM)
        block = pl.BlockSpec((1, *piece), lambda i: (j, 0, 0, 0))
        held = pl.BlockSpec(memory_space=pl.ANY)
        args = [pltpu.with_memory_space_constraint(v, pltpu.VMEM) for v in parts] + [weights, first, second]
        specs = [whole] * len(parts) + [block] * 3
        if j:
            args += [pltpu.with_memory_space_constraint(v, pltpu.VMEM) for v in more] + [at]
            specs += [whole] * 2 + [pl.BlockSpec(memory_space=pltpu.SMEM)]
        else:
            args += [pltpu.with_memory_space_constraint(more[0], pltpu.VMEM), *more[1:]]
            specs += [whole] + [held] * 2
        n = len(args)
        return pl.pallas_call(
            functools.partial(moments, z, j),
            grid=(1,),
            out_shape=[shape(weights.shape)] * 2
            + [near(piece), near((8, z.L)) if j else near((z.R * z.Z, 2, LANES))],
            in_specs=specs,
            out_specs=[block, block, whole, whole],
            input_output_aliases={} if j else {n - 2: 0, n - 1: 1},
            compiler_params=pltpu.CompilerParams(vmem_limit_bytes=8 * 1024 * 1024),
            cost_estimate=pl.CostEstimate(flops=1 if j else COST_GRAD, bytes_accessed=1, transcendentals=0),
        )(*args)

    parts_two = gradient(h_parts, da, db, dz, out)
    wide, slope = call(
        functools.partial(hidden_slope, z),
        [back_wide(z), near(GL)],
        (at, *share(keep_two), z1, sum_one, hw, slice_params),
    )
    da1, stats = call(
        functools.partial(hidden_grad, z),
        [near(GL), pair],
        (at, *dz2s, wide, slope, z1, sum_one, hw),
        [pltpu.VMEM((rows, z.K * z.LP), F32), pltpu.VMEM((z.Q, *GL), BF16)],
        limit=16,
    )
    stats, parts_two = together((stats, parts_two))
    stats, parts_two = together((sharers(stats), by_plane(parts_two)))
    da, db, dz, grad_one = call(
        functools.partial(norm_grad, z, 0),
        [near(HL, BF16), near(HL, BF16), near(GL, BF16), near((8, z.L))],
        (z1, da1, sum_one, stats, hw, slice_params),
    )
    flat = near((z.K * z.IB, z.L), BF16)
    hold = pltpu.VMEM((z.Z, z.K * z.IB, z.L), BF16)
    *parts_two, values = call(
        functools.partial(route, z),
        [flat] * z.Z + [near((rows, z.C), BF16)],
        (at, *parts_two),
        [pltpu.VMEM((z.Q, rows, z.L), BF16), hold],
        after=(da,),
    )
    parts_one = gradient(x_parts, da, db, dz)
    parts_one, parts_two = by_plane(parts_one), along(parts_two)
    parts_one, parts_two = together((parts_one, parts_two))
    dxs = call(
        functools.partial(input_part, z),
        [near((rows, z.C))] + [near((rows, z.C), BF16)] * (z.Q - 1),
        (at, da, db, w_far, d),
        [grad_scratch[0], pltpu.VMEM((z.Q, rows, z.C), F32)],
        limit=16,
        cost=COST_GRAD,
        far=(w_far,),
        after=(parts_one[0],),
    )
    parts_one = call(functools.partial(route, z), [flat] * z.Z, (at, *parts_one), [hold])
    parts_one, parts_two = together((parts_one, parts_two))
    parts_one = along(parts_one)
    new_first, new_second, move_two, other = update(1, parts_two, grad_one, grad_two)
    dxs = [over_q(dxs[m], m) for m in range(z.Q)]
    new_first, new_second, move_one, stats = update(0, parts_one, other, new_first, new_second)
    stats = lax.all_to_all(stats, ("s", "q", "z"), 0, 0)
    dx = call(functools.partial(total_of, z), shape((rows, z.C), BF16), tuple(dxs))
    stats, dx = together((stats, dx))
    new_weights, copies, new_params, new_p_first, new_p_second, trust = call(
        functools.partial(finish, z),
        [shape(weights.shape), shape(weights.shape, BF16)] + [shape(params.shape)] * 3 + [shape((2, 6))],
        (stats, weights, move_one, move_two, params, p_first, p_second),
    )
    return (
        values.reshape(images.shape),
        dx.reshape(images.shape),
        new_weights,
        copies,
        new_first,
        new_second,
        new_params,
        new_p_first,
        new_p_second,
        trust,
    )


def solution(mesh):
    def whole(images, masks, cotangent, weights, first, second, params, p_first, p_second):
        z = Sizes(mesh, images.shape, weights.shape)
        inner = Mesh(mesh.devices.reshape(z.Q, z.S, z.Z), ("q", "s", "z"))
        pixels = P(("q", "s", "z"), None, None, None)
        kernels = P(None, None, ("q", "s"), "z")
        return jax.shard_map(
            functools.partial(shards, z),
            mesh=inner,
            in_specs=(pixels, P(("q", "s", "z"), None, None), pixels, kernels, kernels, kernels, P(), P(), P()),
            out_specs=(pixels, pixels, kernels, kernels, kernels, kernels, P(), P(), P(), P()),
            check_vma=False,
        )(images, masks, cotangent, weights, first, second, params, p_first, p_second)

    return whole
```

```python
import functools

import jax
import jax.numpy as jnp
from jax import lax
from jax.experimental import pallas as pl
from jax.experimental.pallas import tpu as pltpu
from jax.sharding import Mesh
from jax.sharding import PartitionSpec as P

STEP = 3
RATE = 0.5
DECAY = 0.01
BETA = 0.5
BIAS = 1.0 - BETA**STEP
EPS = 1e-05
TINY = 1e-06
ROOT = 0.7978845608028654
CUBE = 0.044715
LANES = 128
COST_GRAD = 3 * 10**9
F32 = jnp.float32
BF16 = jnp.bfloat16


def gelu(v):
    return 0.5 * v * (1.0 + jnp.tanh(ROOT * (v + CUBE * (v * v * v))))


def gelu_both(v):
    t = jnp.tanh(ROOT * (v + CUBE * (v * v * v)))
    value = 0.5 * v * (1.0 + t)
    slope = 0.5 * (1.0 + t) + 0.5 * v * (1.0 - t * t) * (ROOT * (1.0 + (3.0 * CUBE) * (v * v)))
    return value, slope


class Sizes:
    def __init__(self, mesh, images, weights):
        self.Z = mesh.shape["ba"]
        self.R = mesh.shape["ha"] * mesh.shape["wa"]
        self.Q = self.Z
        self.S = self.R // self.Q
        n, self.H, self.W, self.C = images
        self.n_own = n // (self.R * self.Z)
        self.own = self.n_own * self.H * self.W
        self.n_group = self.n_own * self.Q
        self.G = self.own * self.Q
        self.L = self.C // self.Q
        self.LP = max(self.L, LANES)
        self.IB = self.C // self.R
        self.K = weights[1]
        self.extra = 16 * ((2 * self.n_own + 15) // 16)
        self.sent = self.K * self.IB + self.own + self.extra


def call(body, out_shape, args, scratch=(), limit=8, far=(), after=(), cost=1, raw=()):
    smem = [a.dtype == jnp.int32 and a.ndim == 1 for a in args]
    away = [any(a is f for f in far) for a in args]
    args = [
        a if m else pltpu.with_memory_space_constraint(a, pltpu.HBM if w else pltpu.VMEM)
        for a, m, w in zip(args, smem, away)
    ]
    n = len(args)

    def run(*refs):
        body(*refs[:n], *refs[n + len(after) :])

    return pl.pallas_call(
        run,
        out_shape=out_shape,
        in_specs=[pl.BlockSpec(memory_space=pltpu.SMEM if m else pltpu.VMEM) for m in smem]
        + [pl.BlockSpec(memory_space=pl.ANY)] * len(after),
        out_specs=jax.tree.map(
            lambda o: pl.BlockSpec(memory_space=pltpu.HBM if any(o is r for r in raw) else pltpu.VMEM),
            out_shape,
        ),
        scratch_shapes=list(scratch),
        compiler_params=pltpu.CompilerParams(vmem_limit_bytes=limit * 1024 * 1024),
        cost_estimate=pl.CostEstimate(flops=cost, bytes_accessed=1, transcendentals=0),
    )(*args, *after)


together = lax.optimization_barrier


def near(dims, dtype=F32):
    return pltpu.VMEM(tuple(dims), dtype)


def away(dims, dtype=F32):
    return pltpu.HBM(tuple(dims), dtype)


def shape(dims, dtype=F32):
    return jax.ShapeDtypeStruct(tuple(dims), dtype)


def image_mask(z, hw):
    dims = (z.H, z.W, z.L)
    rows = lax.broadcasted_iota(jnp.int32, dims, 0).astype(F32)
    cols = lax.broadcasted_iota(jnp.int32, dims, 1).astype(F32)
    tall = hw[0:1, : z.L].reshape(1, 1, z.L)
    wide = hw[1:2, : z.L].reshape(1, 1, z.L)
    return jnp.where((rows < tall) & (cols < wide), 1.0, 0.0).reshape(z.H * z.W, z.L)


def shifted_sum(z, taps, sign):
    dims = (z.n_own, z.H, z.W, z.L)
    cols = lax.broadcasted_iota(jnp.int32, dims, 2)
    total = None
    for c in range(3):
        column = None
        for r in range(3):
            part = taps(3 * r + c).reshape(dims)
            move = (r - 1) * sign
            if move == 1:
                part = jnp.concatenate([part[:, 1:], jnp.zeros_like(part[:, :1])], axis=1)
            elif move == -1:
                part = jnp.concatenate([jnp.zeros_like(part[:, :1]), part[:, :-1]], axis=1)
            column = part if column is None else column + part
        move = (c - 1) * sign
        if move:
            flat = column.reshape(z.n_own * z.H, z.W, z.L)
            flat = pltpu.roll(flat, (-move) % z.W, 1)
            column = flat.reshape(dims)
            edge = z.W - 1 if move == 1 else 0
            column = jnp.where(cols == edge, 0.0, column)
        total = column if total is None else total + column
    return total.reshape(z.own, z.L)


def moved_taps(z, feature):
    dims = (z.n_own, z.H, z.W, z.L)
    cols = lax.broadcasted_iota(jnp.int32, dims, 2)
    out = [None] * 9
    for c in range(3):
        move = 1 - c
        column = feature.reshape(dims)
        if move:
            flat = feature.reshape(z.n_own * z.H, z.W, z.L)
            column = pltpu.roll(flat, (-move) % z.W, 1).reshape(dims)
            edge = z.W - 1 if move == 1 else 0
            column = jnp.where(cols == edge, 0.0, column)
        for r in range(3):
            if r == 0:
                part = jnp.concatenate([column[:, 1:], jnp.zeros_like(column[:, :1])], axis=1)
            elif r == 2:
                part = jnp.concatenate([jnp.zeros_like(column[:, :1]), column[:, :-1]], axis=1)
            else:
                part = column
            out[3 * r + c] = part.reshape(z.own, z.L)
    return out


def fill_moved(z, a_ref, b_ref, moved_ref):
    half = z.Q // 2
    for j in range(z.Q):
        ref, at_row = (a_ref, j) if j < half else (b_ref, j - half)
        block = ref[at_row * z.own : (at_row + 1) * z.own, :].astype(F32)
        for k, part in enumerate(moved_taps(z, block)):
            moved_ref[j * z.own : (j + 1) * z.own, k * z.LP : k * z.LP + z.L] = part.astype(BF16)


def spread(ref, rows):
    used, many = rows[0].shape[1], ref.shape[1]
    if len(rows) < many:
        rows = rows + [jnp.zeros((many - len(rows), used), F32)]
    stat = jnp.concatenate(rows, axis=0)
    if used < LANES:
        stat = jnp.concatenate([stat, jnp.zeros((many, LANES - used), F32)], axis=1)
    for k in range(ref.shape[0]):
        ref[k] = stat


def local_stats(z, z_ref, hw_ref, stats_ref):
    px = z.H * z.W
    pivot = z_ref[0:1, :]

    def step(n, carry):
        mask = image_mask(z, hw_ref[n])
        centered = mask * (z_ref[pl.ds(pl.multiple_of(n * px, px), px), :] - pivot)
        return (
            carry[0] + jnp.sum(mask, 0, keepdims=True),
            carry[1] + jnp.sum(centered, 0, keepdims=True),
            carry[2] + jnp.sum(centered * centered, 0, keepdims=True),
        )

    zero = jnp.zeros((1, z.L), F32)
    count, total, squares = lax.fori_loop(0, z.n_group, step, (zero, zero, zero), unroll=4)
    offset = total / count
    spread(stats_ref, [count, pivot + offset, jnp.maximum(squares - total * offset, 0.0)])


def conv_into(z, product, y_ref, z_ref, sign=1, at_q=0):
    for j in range(z.Q):
        y_ref[...] = product(j)
        z_ref[pl.ds(pl.multiple_of((at_q ^ j) * z.own, z.own), z.own), :] = shifted_sum(
            z, lambda k: y_ref[:, k * z.LP : k * z.LP + z.L], sign
        )


def fill_kernels(z, at, blocks, wcat):
    for t, block in enumerate(blocks):
        s = at[1] ^ t
        for m in range(z.Z):
            pieces = isinstance(block, (list, tuple))
            row = pl.multiple_of((at[0] ^ m if pieces else m) * z.L + s * z.IB, z.IB)
            for k in range(z.K):
                part = block[m][k * z.IB : (k + 1) * z.IB, :] if pieces else block[at[0] ^ m, k]
                wcat[pl.ds(row, z.IB), k * z.LP : k * z.LP + z.L] = part


def split_channels(z, at, slices, outs, rows):
    parts = [jnp.concatenate([v[:, s * z.IB : (s + 1) * z.IB] for v in slices], axis=1) for s in range(z.S)]
    for t in range(z.S):
        part = parts[t]
        for s in range(1, z.S):
            part = jnp.where(at[1] == s, parts[s ^ t], part)
        outs[t][rows, :] = part


def split_images(z, at, np_ref, *refs):
    xs, outs, (slice_ref, par_ref) = refs[: z.Q], refs[z.Q : -2], refs[-2:]
    for m in range(z.Q):
        rows = pl.ds(pl.multiple_of((at[0] ^ m) * z.own, z.own), z.own)
        split_channels(z, at, [xs[m][:, a * z.L : (a + 1) * z.L] for a in range(z.Q)], outs, rows)
    for slot in range(z.Q):

        @pl.when(at[0] == slot)
        def _(slot=slot):
            par_ref[...] = np_ref[:, slot * z.L : (slot + 1) * z.L]
            for m in range(z.Q):
                j = slot ^ m
                slice_ref[j * z.own : (j + 1) * z.own, :] = xs[m][
                    :, slot * z.L : (slot + 1) * z.L
                ]


def first_conv(z, at, *refs):
    xs, refs = refs[: z.Q], refs[z.Q :]
    blocks = [refs[t * z.Q : (t + 1) * z.Q] for t in range(z.S)]
    refs = refs[z.S * z.Q :]
    z_ref, hw_ref, stats_ref, far_w, wcat, y_ref, sem = refs
    for m in range(z.Q):
        for n in range(z.n_own):
            row = z.K * z.IB + 2 * n
            two = jnp.broadcast_to(blocks[0][m][row : row + 2, 0:1].astype(F32), (2, LANES))
            hw_ref[(at[0] ^ m) * z.n_own + n] = jnp.concatenate([two, jnp.zeros((6, LANES), F32)], axis=0)
    fill_kernels(z, at, blocks, wcat)
    copy = pltpu.make_async_copy(wcat, far_w, sem)
    copy.start()

    def product(m):
        return jnp.dot(xs[m][...], wcat[...], preferred_element_type=F32)

    conv_into(z, product, y_ref, z_ref, 1, at[0])
    local_stats(z, z_ref, hw_ref, stats_ref)
    copy.wait()


def gathered(z, parts, j):
    half = z.Q // 2
    at_part, row = (0, j) if j < half else (z.Q, j - half)
    return [parts[at_part + m][row * z.own : (row + 1) * z.own, :] for m in range(z.Q)]


def second_conv(z, at, *refs):
    hs, refs = refs[: 2 * z.Q], refs[2 * z.Q :]
    blocks, refs = refs[: z.S], refs[z.S :]
    hw_ref, outs, (z_ref, stats_ref, wcat, y_ref) = refs[0], refs[1 : 1 + z.S], refs[1 + z.S :]
    fill_kernels(z, at, blocks, wcat)

    def product(j):
        slices = gathered(z, hs, j)
        split_channels(z, at, slices, outs, slice(j * z.own, (j + 1) * z.own))
        if z.L % LANES == 0:
            return jnp.dot(jnp.concatenate(slices, axis=1), wcat[...], preferred_element_type=F32)
        return sum(
            jnp.dot(v, wcat[m * z.L : (m + 1) * z.L, :], preferred_element_type=F32)
            for m, v in enumerate(slices)
        )

    conv_into(z, product, y_ref, z_ref)
    local_stats(z, z_ref, hw_ref, stats_ref)


def merged(z, all_ref):
    counts = [all_ref[k, 0:1, : z.L] for k in range(z.S * z.Z)]
    means = [all_ref[k, 1:2, : z.L] for k in range(z.S * z.Z)]
    count = sum(counts)
    mean = sum(c * m for c, m in zip(counts, means)) / count
    squares = sum(
        all_ref[k, 2:3, : z.L] + counts[k] * (means[k] - mean) * (means[k] - mean)
        for k in range(z.S * z.Z)
    )
    return mean, lax.rsqrt(squares / count + EPS), count


def keep(ref, rows):
    used = rows[0].shape[1]
    ref[...] = jnp.concatenate(rows + [jnp.zeros((8 - len(rows), used), F32)], axis=0)


def over_images(z, step, init=0, unroll=2):
    px = z.H * z.W

    def one(n, carry):
        return step(n, pl.ds(pl.multiple_of(n * px, px), px), carry)

    return lax.fori_loop(0, z.n_group, one, init, unroll=unroll)


def over_halves(z, step, refs):
    px, count = z.H * z.W, z.n_group // 2
    for i, ref in enumerate(refs):

        def one(n, carry, i=i, ref=ref):
            rows = pl.ds(pl.multiple_of((i * count + n) * px, px), px)
            ref[pl.ds(pl.multiple_of(n * px, px), px), :] = step(i * count + n, rows)
            return carry

        lax.fori_loop(0, count, one, 0, unroll=2)


def hidden(z, at, z_ref, all_ref, hw_ref, par_ref, *refs):
    parts, (a_ref, b_ref, sum_ref, kernel_ref, map_ref) = refs[: z.Q], refs[z.Q :]
    unpick(z, at, *parts, kernel_ref, map_ref)
    mean, inv, count = merged(z, all_ref)
    keep(sum_ref, [mean, inv, count])
    gain, shift = par_ref[0:1, :], par_ref[1:2, :]

    def step(n, rows):
        mask = image_mask(z, hw_ref[n])
        return gelu(mask * (gain * ((z_ref[rows, :] - mean) * inv) + shift)).astype(BF16)

    over_halves(z, step, (a_ref, b_ref))


def middle(z, at, z_ref, all_ref, hw_ref, par_ref, x_ref, *refs):
    cot_ref, out_ref, d_ref, sum_ref, stats_ref = refs
    mean, inv, count = merged(z, all_ref)
    keep(sum_ref, [mean, inv, count])
    gain, shift = par_ref[2:3, :], par_ref[3:4, :]
    px = z.H * z.W
    carry = (jnp.zeros((1, z.L), F32), jnp.zeros((1, z.L), F32))
    for j in range(z.Q):

        def step(n, carry, j=j):
            local = pl.ds(pl.multiple_of(n * px, px), px)
            rows = pl.ds(pl.multiple_of(j * z.own + n * px, px), px)
            mask = image_mask(z, hw_ref[j * z.n_own + n])
            normed = (z_ref[rows, :] - mean) * inv
            summed = mask * (gain * normed + shift) + x_ref[rows, :].astype(F32)
            value, slope = gelu_both(summed)
            out_ref[j, local, :] = value.astype(BF16)
            d = cot_ref[rows, :].astype(F32) * slope
            d_ref[rows, :] = d
            masked = mask * d
            return (
                carry[0] + jnp.sum(masked, 0, keepdims=True),
                carry[1] + jnp.sum(masked * normed, 0, keepdims=True),
            )

        carry = lax.fori_loop(0, z.n_own, step, carry, unroll=2)
    spread(stats_ref, list(carry))


def norm_grad(z, row, z_ref, up_ref, sum_ref, all_ref, hw_ref, par_ref, a_ref, b_ref, whole_ref, par_grad_ref):
    mean, inv, count = sum_ref[0:1, :], sum_ref[1:2, :], sum_ref[2:3, :]
    shift_grad = sum(all_ref[k, 0:1, : z.L] for k in range(z.S * z.Z))
    gain_grad = sum(all_ref[k, 1:2, : z.L] for k in range(z.S * z.Z))
    keep(par_grad_ref, [gain_grad, shift_grad])
    gain = par_ref[row : row + 1, :]

    def step(n, rows):
        mask = image_mask(z, hw_ref[n])
        normed = (z_ref[rows, :] - mean) * inv
        grad = inv * mask * gain * (up_ref[rows, :] - (shift_grad + normed * gain_grad) / count)
        low = grad.astype(BF16)
        whole_ref[rows, :] = low
        return low

    over_halves(z, step, (a_ref, b_ref))


def hidden_slope(z, at, *refs):
    blocks, (z_ref, sum_ref, hw_ref, par_ref, wcat, slope_ref) = refs[: z.S], refs[z.S :]
    for t, block in enumerate(blocks):
        s = at[1] ^ t
        for m in range(z.Z):
            for k in range(z.K):
                rows = pl.ds(pl.multiple_of(k * z.LP + s * z.IB, z.IB), z.IB)
                if z.L % LANES == 0:
                    wcat[0, rows, m * z.L : (m + 1) * z.L] = block[at[0] ^ m, k]
                else:
                    wcat[m, rows, :] = block[at[0] ^ m, k]
    mean, inv = sum_ref[0:1, :], sum_ref[1:2, :]
    gain, shift = par_ref[0:1, :], par_ref[1:2, :]

    def step(n, rows, carry):
        normed = (z_ref[rows, :] - mean) * inv
        slope_ref[rows, :] = gelu_both(image_mask(z, hw_ref[n]) * (gain * normed + shift))[1]
        return carry

    over_images(z, step)


def back_product(z, dzs, wcat):
    contract = (((1,), (1,)), ((), ()))

    def product(j):
        slices = gathered(z, dzs, j)
        if z.L % LANES == 0:
            whole = jnp.concatenate(slices, axis=1)
            return lax.dot_general(whole, wcat[0], contract, preferred_element_type=F32)
        return sum(
            lax.dot_general(v, wcat[m], contract, preferred_element_type=F32) for m, v in enumerate(slices)
        )

    return product


def back_wide(z):
    if z.L % LANES == 0:
        return near((1, z.K * z.LP, z.C), BF16)
    return near((z.Z, z.K * z.LP, z.C // z.Z), BF16)


def hidden_grad(z, at, *refs):
    dzs, refs = refs[: 2 * z.Q], refs[2 * z.Q :]
    wcat, slope_ref, z_ref, sum_ref, hw_ref, da_ref, stats_ref, y_ref = refs
    conv_into(z, back_product(z, dzs, wcat), y_ref, da_ref, -1)
    mean, inv = sum_ref[0:1, :], sum_ref[1:2, :]

    def step(n, rows, carry):
        mask = image_mask(z, hw_ref[n])
        normed = (z_ref[rows, :] - mean) * inv
        da = da_ref[rows, :] * slope_ref[rows, :]
        da_ref[rows, :] = da
        masked = mask * da
        return (
            carry[0] + jnp.sum(masked, 0, keepdims=True),
            carry[1] + jnp.sum(masked * normed, 0, keepdims=True),
        )

    zero = jnp.zeros((1, z.L), F32)
    spread(stats_ref, list(over_images(z, step, (zero, zero))))


def input_part(z, at, a_ref, b_ref, w_ref, d_ref, *refs):
    outs, moved_ref = refs[: z.Q], refs[z.Q]
    fill_moved(z, a_ref, b_ref, moved_ref)
    contract = (((1,), (1,)), ((), ()))
    for m in range(z.Q):
        rows = pl.ds(pl.multiple_of((at[0] ^ m) * z.own, z.own), z.own)
        part = lax.dot_general(moved_ref[rows, :], w_ref[...], contract, preferred_element_type=F32)
        d = d_ref[rows, :]
        own = jnp.concatenate([jnp.where(at[0] == slot, d, 0.0) for slot in range(z.Q)], axis=1)
        outs[m][...] = (part + own).astype(outs[m].dtype)


def kernel_grad(z, ordered, at, *refs):
    features, refs = refs[: z.S], refs[z.S :]
    dzs, refs = refs[: z.S + 1], refs[z.S + 1 :]
    value_ref = None
    if len(refs) > z.Q + 2:
        value_ref, refs = refs[0], refs[1:]
    outs, (moved_ref, full_ref) = refs[: z.Q], refs[z.Q :]
    contract = (((0,), (0,)), ((), ()))
    half = z.G // 2
    for t in range(z.S):
        pair = (dzs[0], dzs[1]) if t == 0 else (dzs[1 + t].at[:half], dzs[1 + t].at[half:])
        moved = moved_ref.at[t % 2]
        fill_moved(z, *pair, moved)
        part = lax.dot_general(features[t][...], moved[...], contract, preferred_element_type=F32)
        full_ref[...] = part if t == 0 else full_ref[...] + part
    for r in range(z.Q):
        row = pl.multiple_of((at[0] ^ r if ordered else r) * z.IB, z.IB)
        for k in range(z.K):
            part = full_ref[pl.ds(row, z.IB), k * z.LP : k * z.LP + z.L]
            outs[r][k * z.IB : (k + 1) * z.IB, :] = part.astype(BF16)
        if value_ref is not None:
            outs[r][z.K * z.IB :, :] = value_ref[at[0] ^ r]


def route(z, at, *refs):
    parts, refs = refs[: z.Q], refs[z.Q :]
    outs, refs = refs[: z.Z], refs[z.Z :]
    hold = refs[-1]
    for r in range(z.Q):
        hold[at[2] ^ at[0] ^ r] = parts[r][: z.K * z.IB, :]
    for m in range(z.Z):
        outs[m][...] = hold[m]
    if len(refs) == 3:
        value_ref, slots, _ = refs
        for r in range(z.Q):
            slots[at[0] ^ r] = parts[r][z.K * z.IB :, :]
        for j in range(z.Q):
            value_ref[:, j * z.L : (j + 1) * z.L] = slots[j]


def total_of(z, *refs):
    refs[-1][...] = sum(ref[...].astype(F32) for ref in refs[:-1]).astype(refs[-1].dtype)


def direction_of(grad, first, second, param, decay):
    new_first = BETA * first + (1.0 - BETA) * grad
    new_second = BETA * second + (1.0 - BETA) * grad * grad
    move = new_first / BIAS / (jnp.sqrt(new_second / BIAS) + TINY) + decay * param
    return new_first, new_second, move


def moments(z, j, *refs):
    count = len(refs) - 10
    parts, refs = refs[:count], refs[count:]
    w_ref, first_ref, second_ref, refs = *refs[:3], refs[3:]
    if j:
        g1_ref, g2_ref, at, refs = *refs[:3], refs[3:]
    else:
        other_ref, refs = refs[0], refs[3:]
    nf_ref, ns_ref, u_ref, stats_ref = refs
    total_u = jnp.zeros((1, z.L), F32)
    total_w = jnp.zeros((1, z.L), F32)
    for k in range(z.K):
        grad = sum(part[k * z.IB : (k + 1) * z.IB, :].astype(F32) for part in parts)
        w = w_ref[0, k]
        nf, ns, u = direction_of(grad, first_ref[0, k], second_ref[0, k], w, DECAY)
        nf_ref[0, k] = nf
        ns_ref[0, k] = ns
        u_ref[k] = u
        total_u = total_u + jnp.sum(u * u, 0, keepdims=True)
        total_w = total_w + jnp.sum(w * w, 0, keepdims=True)
    lane = lax.broadcasted_iota(jnp.int32, (1, z.L), 1)
    sums = jnp.zeros((1, z.L), F32) if j else other_ref[0:1, :]
    for c, v in enumerate([total_u, total_w]):
        sums = jnp.where(lane == 2 * c + j, jnp.sum(v, axis=1, keepdims=True), sums)
    if j:
        own = jnp.zeros((1, z.L), F32)
        for r, v in enumerate([g1_ref[0:1, :], g1_ref[1:2, :], g2_ref[0:1, :], g2_ref[1:2, :]]):
            own = jnp.where(at[2] == r, v, own)
        keep(stats_ref, [sums, own])
    else:
        spread(stats_ref, [sums, other_ref[1:2, :]])


def finish(z, all_ref, w_ref, u0_ref, u1_ref, np_ref, nf_ref, ns_ref, *outs):
    nw_ref, copy_ref, nnp_ref, nnf_ref, nns_ref, trust_ref = outs
    total = all_ref[0, 0:1, :]
    for k in range(1, z.R * z.Z):
        total = total + all_ref[k, 0:1, :]
    tops, bottoms = [], []
    for j in range(2):
        un = jnp.sqrt(total[:, j : j + 1])
        wn = jnp.sqrt(total[:, 2 + j : 3 + j])
        tops.append(wn)
        bottoms.append(un)
        scale = RATE * (wn / (un + TINY))
        for k in range(z.K):
            new = w_ref[j, k] - scale * (u0_ref, u1_ref)[j][k]
            nw_ref[j, k] = new
            copy_ref[j, k] = new.astype(BF16)
    for j in range(z.Q):
        for r in range(4):
            nnp_ref[r : r + 1, j * z.L : (j + 1) * z.L] = all_ref[j * z.Z + r, 1:2, : z.L]
    param = np_ref[...]
    nf, ns, move = direction_of(nnp_ref[...], nf_ref[...], ns_ref[...], param, 0.0)
    nnf_ref[...] = nf
    nns_ref[...] = ns
    pn = jnp.sqrt(jnp.sum(param * param, axis=1, keepdims=True))
    qn = jnp.sqrt(jnp.sum(move * move, axis=1, keepdims=True))
    nnp_ref[...] = param - RATE * (pn / (qn + TINY)) * move
    for r in range(4):
        tops.append(pn[r : r + 1])
        bottoms.append(qn[r : r + 1])
    at_row = lax.broadcasted_iota(jnp.int32, (2, 6), 0)
    at_col = lax.broadcasted_iota(jnp.int32, (2, 6), 1)
    trust = jnp.zeros((2, 6), F32)
    for c in range(6):
        trust = jnp.where(at_col == c, jnp.where(at_row == 0, tops[c], bottoms[c]), trust)
    trust_ref[...] = trust


def pick(z, first, at, *refs):
    parts, refs = refs[: z.Z], refs[z.Z :]
    if first:
        valid_ref, outs, hold = refs[0], refs[1:-1], refs[-1]
        rows = []
        for n in range(z.n_own):
            valid = valid_ref[n].astype(F32)
            tall = jnp.sum(valid[:, 0:1], axis=0, keepdims=True)
            wide = jnp.sum(valid[0:1, :], axis=1, keepdims=True)
            rows += [jnp.broadcast_to(tall, (1, z.L)), jnp.broadcast_to(wide, (1, z.L))]
        rows.append(jnp.zeros((z.extra - len(rows), z.L), F32))
        sizes = jnp.concatenate(rows, axis=0).astype(BF16)
    else:
        map_ref, far_ref, outs, (hold, sem) = refs[0], refs[1], refs[2:-2], refs[-2:]
    for m in range(z.Z):
        hold[at[2] ^ m] = parts[m][...]
    if not first:
        copy = pltpu.make_async_copy(hold, far_ref, sem)
        copy.start()
    for m in range(z.Q):
        for k in range(z.K):
            outs[m][k * z.IB : (k + 1) * z.IB, :] = hold[at[0] ^ m, k]
        if first:
            outs[m][z.K * z.IB :, :] = sizes
            continue
        for slot in range(z.Q):

            @pl.when((at[0] ^ m) == slot)
            def _(m=m, slot=slot):
                outs[m][z.K * z.IB :, :] = map_ref[:, slot * z.L : (slot + 1) * z.L]

    if not first:
        copy.wait()


def unpick(z, at, *refs):
    parts, (out_ref, map_ref) = refs[: z.Q], refs[z.Q :]
    for m in range(z.Q):
        q = at[0] ^ m
        for k in range(z.K):
            out_ref[q, k] = parts[m][k * z.IB : (k + 1) * z.IB, :]
        map_ref[pl.ds(pl.multiple_of(q * z.own, z.own), z.own), :] = parts[m][z.K * z.IB :, :]


def shards(z, images, masks, cotangent, weights, first, second, params, p_first, p_second):
    q, s, b = lax.axis_index("q"), lax.axis_index("s"), lax.axis_index("z")
    at = jnp.stack([q, s, b]).astype(jnp.int32)

    def over_z(v, m):
        return lax.ppermute(v, "z", [(i, i ^ m) for i in range(z.Z)]) if m else v

    def over_s(v, m):
        return lax.ppermute(v, "s", [(i, i ^ m) for i in range(z.S)]) if m else v

    def sharers(v):
        return lax.all_to_all(v, ("s", "z"), 0, 0)

    def over_q(v, m):
        return lax.ppermute(v, "q", [(i, i ^ m) for i in range(z.Q)]) if m else v

    def gather_z(w):
        return [over_z(w, m) for m in range(z.Z)]

    def gather(a, b):
        if z.Q != 4:
            return [over_q(v, m) for v in (a, b) for m in range(z.Q)]
        a1, a2, b1, b2 = over_q(a, 1), over_q(a, 2), over_q(b, 1), over_q(b, 2)
        return [a, a1, a2, over_q(a2, 1), b, b1, b2, over_q(b1, 2)]

    def share(packed):
        return [over_s(packed, t) for t in range(z.S)]

    rows = z.own
    GL = (z.G, z.L)
    HL = (z.G // 2, z.L)
    many = z.S * z.Z
    piece = (z.K, z.IB, z.L)
    blocks = near((z.Z, *piece), BF16)
    stat, pair = near((many, 4, LANES)), near((many, 2, LANES))
    conv_scratch = [pltpu.VMEM((z.C, z.K * z.LP), BF16), pltpu.VMEM((rows, z.K * z.LP), F32)]
    moved = (z.G, z.K * z.LP)
    grad_scratch = [pltpu.VMEM((2, *moved), BF16), pltpu.VMEM((z.Q * z.IB, z.K * z.LP), F32)]
    cot_rows = cotangent.reshape(rows, z.C)
    image_rows = images.reshape(rows, z.C)

    low_one, low_two = (weights[j].astype(BF16) for j in range(2))
    one = [over_z(low_one, m) for m in range(z.Z)]
    xs = [over_q(image_rows, m) for m in range(z.Q)]
    one, low_two = together((one, low_two))
    hold = pltpu.VMEM((z.Z, *piece), BF16)
    picked = call(
        functools.partial(pick, z, True),
        [near((z.K * z.IB + z.extra, z.L), BF16)] * z.Q,
        (at, *one, masks),
        [hold],
    )
    picked, xs = together((picked, xs))
    two = [over_z(low_two, m) for m in range(z.Z)]
    *x_parts, x_slice, slice_params = call(
        functools.partial(split_images, z),
        [near((z.G, z.Q * z.IB), BF16)] * z.S + [near(GL, BF16), near((4, z.L))],
        (at, params, *xs),
    )
    front_one = [over_q(picked[m], m) for m in range(z.Q)]
    front_one, x_parts, two = together((front_one, x_parts, two))
    keep = away((z.Z, *piece), BF16)
    keep_two, *picked = call(
        functools.partial(pick, z, False),
        [keep] + [near((z.K * z.IB + rows, z.L), BF16)] * z.Q,
        (at, *two, cot_rows),
        [hold, pltpu.SemaphoreType.DMA],
        raw=(keep,),
    )
    w_far = away((z.C, z.K * z.LP), BF16)
    z1, hw, stats, w_far = call(
        functools.partial(first_conv, z),
        [near(GL), near((z.n_group, 8, LANES)), stat, w_far],
        (at, *xs, *[over_s(v, t) for t in range(z.S) for v in front_one]),
        conv_scratch + [pltpu.SemaphoreType.DMA],
        limit=16,
        raw=(w_far,),
    )
    stats, picked = together((stats, picked))
    stats, picked = together((sharers(stats), [over_q(picked[m], m) for m in range(z.Q)]))
    ha, hb, sum_one, front_two, cots = call(
        functools.partial(hidden, z),
        [near(HL, BF16), near(HL, BF16), near((8, z.L)), blocks, near(GL, BF16)],
        (at, z1, stats, hw, slice_params, *picked),
    )
    hs = gather(ha, hb)
    *h_parts, z2, stats = call(
        functools.partial(second_conv, z),
        [near((z.G, z.Q * z.IB), BF16)] * z.S + [near(GL), stat],
        (at, *hs, *share(front_two), hw),
        conv_scratch,
        limit=16,
    )
    stats, x_parts, h_parts = together((stats, x_parts, h_parts))
    x_parts = [over_s(v, t) for t, v in enumerate(x_parts)]
    h_parts = [over_s(v, t) for t, v in enumerate(h_parts)]
    stats, x_parts, h_parts = together((sharers(stats), x_parts, h_parts))
    out, d, sum_two, stats = call(
        functools.partial(middle, z),
        [near((z.Q, rows, z.L), BF16), near(GL), near((8, z.L)), pair],
        (at, z2, stats, hw, slice_params, x_slice, cots),
    )
    da, db, dz, grad_two = call(
        functools.partial(norm_grad, z, 2),
        [near(HL, BF16), near(HL, BF16), near(GL, BF16), near((8, z.L))],
        (z2, d, sum_two, sharers(stats), hw, slice_params),
    )
    da, db, keep_two = together((da, db, keep_two))
    dz2s = gather(da, db)

    def gradient(features, a, b, whole, *value):
        more = rows if value else 0
        return call(
            functools.partial(kernel_grad, z, not value),
            [near((z.K * z.IB + more, z.L), BF16)] * z.Q,
            (at, *features, a, b, *[over_s(whole, t) for t in range(1, z.S)], *value),
            grad_scratch,
            limit=18,
            cost=COST_GRAD,
        )

    def by_plane(parts):
        return [over_q(parts[r], r) for r in range(z.Q)]

    def along(parts):
        return [over_z(parts[m], m) for m in range(z.Z)]

    def update(j, parts, *more):
        whole = pl.BlockSpec(memory_space=pltpu.VMEM)
        block = pl.BlockSpec((1, *piece), lambda i: (j, 0, 0, 0))
        held = pl.BlockSpec(memory_space=pl.ANY)
        args = [pltpu.with_memory_space_constraint(v, pltpu.VMEM) for v in parts] + [weights, first, second]
        specs = [whole] * len(parts) + [block] * 3
        if j:
            args += [pltpu.with_memory_space_constraint(v, pltpu.VMEM) for v in more] + [at]
            specs += [whole] * 2 + [pl.BlockSpec(memory_space=pltpu.SMEM)]
        else:
            args += [pltpu.with_memory_space_constraint(more[0], pltpu.VMEM), *more[1:]]
            specs += [whole] + [held] * 2
        n = len(args)
        return pl.pallas_call(
            functools.partial(moments, z, j),
            grid=(1,),
            out_shape=[shape(weights.shape)] * 2
            + [near(piece), near((8, z.L)) if j else near((z.R * z.Z, 2, LANES))],
            in_specs=specs,
            out_specs=[block, block, whole, whole],
            input_output_aliases={} if j else {n - 2: 0, n - 1: 1},
            compiler_params=pltpu.CompilerParams(vmem_limit_bytes=8 * 1024 * 1024),
            cost_estimate=pl.CostEstimate(flops=1 if j else COST_GRAD, bytes_accessed=1, transcendentals=0),
        )(*args)

    parts_two = gradient(h_parts, da, db, dz, out)
    wide, slope = call(
        functools.partial(hidden_slope, z),
        [back_wide(z), near(GL)],
        (at, *share(keep_two), z1, sum_one, hw, slice_params),
    )
    da1, stats = call(
        functools.partial(hidden_grad, z),
        [near(GL), pair],
        (at, *dz2s, wide, slope, z1, sum_one, hw),
        [pltpu.VMEM((rows, z.K * z.LP), F32)],
        limit=16,
    )
    stats, parts_two = together((stats, parts_two))
    stats, parts_two = together((sharers(stats), by_plane(parts_two)))
    da, db, dz, grad_one = call(
        functools.partial(norm_grad, z, 0),
        [near(HL, BF16), near(HL, BF16), near(GL, BF16), near((8, z.L))],
        (z1, da1, sum_one, stats, hw, slice_params),
    )
    flat = near((z.K * z.IB, z.L), BF16)
    hold = pltpu.VMEM((z.Z, z.K * z.IB, z.L), BF16)
    *parts_two, values = call(
        functools.partial(route, z),
        [flat] * z.Z + [near((rows, z.C), BF16)],
        (at, *parts_two),
        [pltpu.VMEM((z.Q, rows, z.L), BF16), hold],
        after=(da,),
    )
    parts_one = gradient(x_parts, da, db, dz)
    parts_one, parts_two[3] = together((parts_one, parts_two[3]))
    parts_one, parts_two = by_plane(parts_one), along(parts_two)
    parts_one, parts_two = together((parts_one, parts_two))
    dxs = call(
        functools.partial(input_part, z),
        [near((rows, z.C))] + [near((rows, z.C), BF16)] * (z.Q - 1),
        (at, da, db, w_far, d),
        [pltpu.VMEM(moved, BF16)],
        limit=16,
        cost=COST_GRAD,
        far=(w_far,),
        after=(parts_one[0],),
    )
    parts_one = call(functools.partial(route, z), [flat] * z.Z, (at, *parts_one), [hold])
    parts_one, parts_two = together((parts_one, parts_two))
    parts_one = along(parts_one)
    new_first, new_second, move_two, other = update(1, parts_two, grad_one, grad_two)
    dxs = [over_q(dxs[m], m) for m in range(z.Q)]
    new_first, new_second, move_one, stats = update(0, parts_one, other, new_first, new_second)
    stats = lax.all_to_all(stats, ("s", "q", "z"), 0, 0)
    dx = call(functools.partial(total_of, z), shape((rows, z.C), BF16), tuple(dxs))
    stats, dx = together((stats, dx))
    new_weights, copies, new_params, new_p_first, new_p_second, trust = call(
        functools.partial(finish, z),
        [shape(weights.shape), shape(weights.shape, BF16)] + [shape(params.shape)] * 3 + [shape((2, 6))],
        (stats, weights, move_one, move_two, params, p_first, p_second),
    )
    return (
        values.reshape(images.shape),
        dx.reshape(images.shape),
        new_weights,
        copies,
        new_first,
        new_second,
        new_params,
        new_p_first,
        new_p_second,
        trust,
    )


def solution(mesh):
    def whole(images, masks, cotangent, weights, first, second, params, p_first, p_second):
        z = Sizes(mesh, images.shape, weights.shape)
        inner = Mesh(mesh.devices.reshape(z.Q, z.S, z.Z), ("q", "s", "z"))
        pixels = P(("q", "s", "z"), None, None, None)
        kernels = P(None, None, ("q", "s"), "z")
        return jax.shard_map(
            functools.partial(shards, z),
            mesh=inner,
            in_specs=(pixels, P(("q", "s", "z"), None, None), pixels, kernels, kernels, kernels, P(), P(), P()),
            out_specs=(pixels, pixels, kernels, kernels, kernels, kernels, P(), P(), P(), P()),
            check_vma=False,
        )(images, masks, cotangent, weights, first, second, params, p_first, p_second)

    return whole
```

```python
import functools

import jax
import jax.numpy as jnp
from jax import lax
from jax.experimental import pallas as pl
from jax.experimental.pallas import tpu as pltpu
from jax.sharding import Mesh
from jax.sharding import PartitionSpec as P

STEP = 3
RATE = 0.5
DECAY = 0.01
BETA = 0.5
BIAS = 1.0 - BETA**STEP
EPS = 1e-05
TINY = 1e-06
ROOT = 0.7978845608028654
CUBE = 0.044715
LANES = 128
COST_GRAD = 3 * 10**9
F32 = jnp.float32
BF16 = jnp.bfloat16


def gelu(v):
    return 0.5 * v * (1.0 + jnp.tanh(ROOT * (v + CUBE * (v * v * v))))


def gelu_both(v):
    t = jnp.tanh(ROOT * (v + CUBE * (v * v * v)))
    value = 0.5 * v * (1.0 + t)
    slope = 0.5 * (1.0 + t) + 0.5 * v * (1.0 - t * t) * (ROOT * (1.0 + (3.0 * CUBE) * (v * v)))
    return value, slope


class Sizes:
    def __init__(self, mesh, images, weights):
        self.Z = mesh.shape["ba"]
        self.R = mesh.shape["ha"] * mesh.shape["wa"]
        self.Q = self.Z
        self.S = self.R // self.Q
        n, self.H, self.W, self.C = images
        self.n_own = n // (self.R * self.Z)
        self.own = self.n_own * self.H * self.W
        self.n_group = self.n_own * self.Q
        self.G = self.own * self.Q
        self.L = self.C // self.Q
        self.LP = max(self.L, LANES)
        self.IB = self.C // self.R
        self.K = weights[1]
        self.extra = 16 * ((2 * self.n_own + 15) // 16)
        self.sent = self.K * self.IB + self.own + self.extra


def call(body, out_shape, args, scratch=(), limit=8, far=(), after=(), cost=1, raw=()):
    smem = [a.dtype == jnp.int32 and a.ndim == 1 for a in args]
    away = [any(a is f for f in far) for a in args]
    args = [
        a if m else pltpu.with_memory_space_constraint(a, pltpu.HBM if w else pltpu.VMEM)
        for a, m, w in zip(args, smem, away)
    ]
    n = len(args)

    def run(*refs):
        body(*refs[:n], *refs[n + len(after) :])

    return pl.pallas_call(
        run,
        out_shape=out_shape,
        in_specs=[pl.BlockSpec(memory_space=pltpu.SMEM if m else pltpu.VMEM) for m in smem]
        + [pl.BlockSpec(memory_space=pl.ANY)] * len(after),
        out_specs=jax.tree.map(
            lambda o: pl.BlockSpec(memory_space=pltpu.HBM if any(o is r for r in raw) else pltpu.VMEM),
            out_shape,
        ),
        scratch_shapes=list(scratch),
        compiler_params=pltpu.CompilerParams(vmem_limit_bytes=limit * 1024 * 1024),
        cost_estimate=pl.CostEstimate(flops=cost, bytes_accessed=1, transcendentals=0),
    )(*args, *after)


together = lax.optimization_barrier


def near(dims, dtype=F32):
    return pltpu.VMEM(tuple(dims), dtype)


def away(dims, dtype=F32):
    return pltpu.HBM(tuple(dims), dtype)


def shape(dims, dtype=F32):
    return jax.ShapeDtypeStruct(tuple(dims), dtype)


def image_mask(z, hw):
    dims = (z.H, z.W, z.L)
    rows = lax.broadcasted_iota(jnp.int32, dims, 0).astype(F32)
    cols = lax.broadcasted_iota(jnp.int32, dims, 1).astype(F32)
    tall = hw[0:1, : z.L].reshape(1, 1, z.L)
    wide = hw[1:2, : z.L].reshape(1, 1, z.L)
    return jnp.where((rows < tall) & (cols < wide), 1.0, 0.0).reshape(z.H * z.W, z.L)


def shifted_sum(z, taps, sign):
    dims = (z.n_own, z.H, z.W, z.L)
    cols = lax.broadcasted_iota(jnp.int32, dims, 2)
    total = None
    for c in range(3):
        column = None
        for r in range(3):
            part = taps(3 * r + c).reshape(dims)
            move = (r - 1) * sign
            if move == 1:
                part = jnp.concatenate([part[:, 1:], jnp.zeros_like(part[:, :1])], axis=1)
            elif move == -1:
                part = jnp.concatenate([jnp.zeros_like(part[:, :1]), part[:, :-1]], axis=1)
            column = part if column is None else column + part
        move = (c - 1) * sign
        if move:
            flat = column.reshape(z.n_own * z.H, z.W, z.L)
            flat = pltpu.roll(flat, (-move) % z.W, 1)
            column = flat.reshape(dims)
            edge = z.W - 1 if move == 1 else 0
            column = jnp.where(cols == edge, 0.0, column)
        total = column if total is None else total + column
    return total.reshape(z.own, z.L)


def moved_taps(z, feature):
    dims = (z.n_own, z.H, z.W, z.L)
    cols = lax.broadcasted_iota(jnp.int32, dims, 2)
    out = [None] * 9
    for c in range(3):
        move = 1 - c
        column = feature.reshape(dims)
        if move:
            flat = feature.reshape(z.n_own * z.H, z.W, z.L)
            column = pltpu.roll(flat, (-move) % z.W, 1).reshape(dims)
            edge = z.W - 1 if move == 1 else 0
            column = jnp.where(cols == edge, 0.0, column)
        for r in range(3):
            if r == 0:
                part = jnp.concatenate([column[:, 1:], jnp.zeros_like(column[:, :1])], axis=1)
            elif r == 2:
                part = jnp.concatenate([jnp.zeros_like(column[:, :1]), column[:, :-1]], axis=1)
            else:
                part = column
            out[3 * r + c] = part.reshape(z.own, z.L)
    return out


def fill_moved(z, a_ref, b_ref, moved_ref):
    half = z.Q // 2
    for j in range(z.Q):
        ref, at_row = (a_ref, j) if j < half else (b_ref, j - half)
        block = ref[at_row * z.own : (at_row + 1) * z.own, :].astype(F32)
        for k, part in enumerate(moved_taps(z, block)):
            moved_ref[j * z.own : (j + 1) * z.own, k * z.LP : k * z.LP + z.L] = part.astype(BF16)


def spread(ref, rows):
    used, many = rows[0].shape[1], ref.shape[1]
    if len(rows) < many:
        rows = rows + [jnp.zeros((many - len(rows), used), F32)]
    stat = jnp.concatenate(rows, axis=0)
    if used < LANES:
        stat = jnp.concatenate([stat, jnp.zeros((many, LANES - used), F32)], axis=1)
    for k in range(ref.shape[0]):
        ref[k] = stat


def local_stats(z, z_ref, hw_ref, stats_ref):
    px = z.H * z.W
    pivot = z_ref[0:1, :]

    def step(n, carry):
        mask = image_mask(z, hw_ref[n])
        centered = mask * (z_ref[pl.ds(pl.multiple_of(n * px, px), px), :] - pivot)
        return (
            carry[0] + jnp.sum(mask, 0, keepdims=True),
            carry[1] + jnp.sum(centered, 0, keepdims=True),
            carry[2] + jnp.sum(centered * centered, 0, keepdims=True),
        )

    zero = jnp.zeros((1, z.L), F32)
    count, total, squares = lax.fori_loop(0, z.n_group, step, (zero, zero, zero), unroll=4)
    offset = total / count
    spread(stats_ref, [count, pivot + offset, jnp.maximum(squares - total * offset, 0.0)])


def conv_into(z, product, y_ref, z_ref, sign=1, at_q=0):
    for j in range(z.Q):
        y_ref[...] = product(j)
        z_ref[pl.ds(pl.multiple_of((at_q ^ j) * z.own, z.own), z.own), :] = shifted_sum(
            z, lambda k: y_ref[:, k * z.LP : k * z.LP + z.L], sign
        )


def fill_kernels(z, at, blocks, wcat):
    for t, block in enumerate(blocks):
        s = at[1] ^ t
        for m in range(z.Z):
            pieces = isinstance(block, (list, tuple))
            row = pl.multiple_of((at[0] ^ m if pieces else m) * z.L + s * z.IB, z.IB)
            for k in range(z.K):
                part = block[m][k * z.IB : (k + 1) * z.IB, :] if pieces else block[at[0] ^ m, k]
                wcat[pl.ds(row, z.IB), k * z.LP : k * z.LP + z.L] = part


def split_channels(z, at, slices, outs, rows):
    parts = [jnp.concatenate([v[:, s * z.IB : (s + 1) * z.IB] for v in slices], axis=1) for s in range(z.S)]
    for t in range(z.S):
        part = parts[t]
        for s in range(1, z.S):
            part = jnp.where(at[1] == s, parts[s ^ t], part)
        outs[t][rows, :] = part


def split_images(z, at, np_ref, *refs):
    xs, outs, (slice_ref, par_ref) = refs[: z.Q], refs[z.Q : -2], refs[-2:]
    for m in range(z.Q):
        rows = pl.ds(pl.multiple_of((at[0] ^ m) * z.own, z.own), z.own)
        split_channels(z, at, [xs[m][:, a * z.L : (a + 1) * z.L] for a in range(z.Q)], outs, rows)
    for slot in range(z.Q):

        @pl.when(at[0] == slot)
        def _(slot=slot):
            par_ref[...] = np_ref[:, slot * z.L : (slot + 1) * z.L]
            for m in range(z.Q):
                j = slot ^ m
                slice_ref[j * z.own : (j + 1) * z.own, :] = xs[m][
                    :, slot * z.L : (slot + 1) * z.L
                ]


def first_conv(z, at, *refs):
    xs, refs = refs[: z.Q], refs[z.Q :]
    blocks = [refs[t * z.Q : (t + 1) * z.Q] for t in range(z.S)]
    refs = refs[z.S * z.Q :]
    z_ref, hw_ref, stats_ref, far_w, wcat, y_ref, sem = refs
    for m in range(z.Q):
        for n in range(z.n_own):
            row = z.K * z.IB + 2 * n
            two = jnp.broadcast_to(blocks[0][m][row : row + 2, 0:1].astype(F32), (2, LANES))
            hw_ref[(at[0] ^ m) * z.n_own + n] = jnp.concatenate([two, jnp.zeros((6, LANES), F32)], axis=0)
    fill_kernels(z, at, blocks, wcat)
    copy = pltpu.make_async_copy(wcat, far_w, sem)
    copy.start()

    def product(m):
        return jnp.dot(xs[m][...], wcat[...], preferred_element_type=F32)

    conv_into(z, product, y_ref, z_ref, 1, at[0])
    local_stats(z, z_ref, hw_ref, stats_ref)
    copy.wait()


def gathered(z, parts, j):
    half = z.Q // 2
    at_part, row = (0, j) if j < half else (z.Q, j - half)
    return [parts[at_part + m][row * z.own : (row + 1) * z.own, :] for m in range(z.Q)]


def second_conv(z, at, *refs):
    hs, refs = refs[: 2 * z.Q], refs[2 * z.Q :]
    blocks, refs = refs[: z.S], refs[z.S :]
    hw_ref, outs, (z_ref, stats_ref, wcat, y_ref) = refs[0], refs[1 : 1 + z.S], refs[1 + z.S :]
    fill_kernels(z, at, blocks, wcat)

    def product(j):
        slices = gathered(z, hs, j)
        split_channels(z, at, slices, outs, slice(j * z.own, (j + 1) * z.own))
        if z.L % LANES == 0:
            return jnp.dot(jnp.concatenate(slices, axis=1), wcat[...], preferred_element_type=F32)
        return sum(
            jnp.dot(v, wcat[m * z.L : (m + 1) * z.L, :], preferred_element_type=F32)
            for m, v in enumerate(slices)
        )

    conv_into(z, product, y_ref, z_ref)
    local_stats(z, z_ref, hw_ref, stats_ref)


def merged(z, all_ref):
    counts = [all_ref[k, 0:1, : z.L] for k in range(z.S * z.Z)]
    means = [all_ref[k, 1:2, : z.L] for k in range(z.S * z.Z)]
    count = sum(counts)
    mean = sum(c * m for c, m in zip(counts, means)) / count
    squares = sum(
        all_ref[k, 2:3, : z.L] + counts[k] * (means[k] - mean) * (means[k] - mean)
        for k in range(z.S * z.Z)
    )
    return mean, lax.rsqrt(squares / count + EPS), count


def keep(ref, rows):
    used = rows[0].shape[1]
    ref[...] = jnp.concatenate(rows + [jnp.zeros((8 - len(rows), used), F32)], axis=0)


def over_images(z, step, init=0, unroll=2):
    px = z.H * z.W

    def one(n, carry):
        return step(n, pl.ds(pl.multiple_of(n * px, px), px), carry)

    return lax.fori_loop(0, z.n_group, one, init, unroll=unroll)


def over_halves(z, step, refs):
    px, count = z.H * z.W, z.n_group // 2
    for i, ref in enumerate(refs):

        def one(n, carry, i=i, ref=ref):
            rows = pl.ds(pl.multiple_of((i * count + n) * px, px), px)
            ref[pl.ds(pl.multiple_of(n * px, px), px), :] = step(i * count + n, rows)
            return carry

        lax.fori_loop(0, count, one, 0, unroll=2)


def hidden(z, at, z_ref, all_ref, hw_ref, par_ref, *refs):
    parts, (a_ref, b_ref, sum_ref, kernel_ref, map_ref) = refs[: z.Q], refs[z.Q :]
    unpick(z, at, *parts, kernel_ref, map_ref)
    mean, inv, count = merged(z, all_ref)
    keep(sum_ref, [mean, inv, count])
    gain, shift = par_ref[0:1, :], par_ref[1:2, :]

    def step(n, rows):
        mask = image_mask(z, hw_ref[n])
        return gelu(mask * (gain * ((z_ref[rows, :] - mean) * inv) + shift)).astype(BF16)

    over_halves(z, step, (a_ref, b_ref))


def middle(z, at, z_ref, all_ref, hw_ref, par_ref, x_ref, *refs):
    cot_ref, out_ref, d_ref, sum_ref, stats_ref = refs
    mean, inv, count = merged(z, all_ref)
    keep(sum_ref, [mean, inv, count])
    gain, shift = par_ref[2:3, :], par_ref[3:4, :]
    px = z.H * z.W
    carry = (jnp.zeros((1, z.L), F32), jnp.zeros((1, z.L), F32))
    for j in range(z.Q):

        def step(n, carry, j=j):
            local = pl.ds(pl.multiple_of(n * px, px), px)
            rows = pl.ds(pl.multiple_of(j * z.own + n * px, px), px)
            mask = image_mask(z, hw_ref[j * z.n_own + n])
            normed = (z_ref[rows, :] - mean) * inv
            summed = mask * (gain * normed + shift) + x_ref[rows, :].astype(F32)
            value, slope = gelu_both(summed)
            out_ref[j, local, :] = value.astype(BF16)
            d = cot_ref[rows, :].astype(F32) * slope
            d_ref[rows, :] = d
            masked = mask * d
            return (
                carry[0] + jnp.sum(masked, 0, keepdims=True),
                carry[1] + jnp.sum(masked * normed, 0, keepdims=True),
            )

        carry = lax.fori_loop(0, z.n_own, step, carry, unroll=2)
    spread(stats_ref, list(carry))


def norm_grad(z, row, z_ref, up_ref, sum_ref, all_ref, hw_ref, par_ref, a_ref, b_ref, whole_ref, par_grad_ref):
    mean, inv, count = sum_ref[0:1, :], sum_ref[1:2, :], sum_ref[2:3, :]
    shift_grad = sum(all_ref[k, 0:1, : z.L] for k in range(z.S * z.Z))
    gain_grad = sum(all_ref[k, 1:2, : z.L] for k in range(z.S * z.Z))
    keep(par_grad_ref, [gain_grad, shift_grad])
    gain = par_ref[row : row + 1, :]

    def step(n, rows):
        mask = image_mask(z, hw_ref[n])
        normed = (z_ref[rows, :] - mean) * inv
        grad = inv * mask * gain * (up_ref[rows, :] - (shift_grad + normed * gain_grad) / count)
        low = grad.astype(BF16)
        whole_ref[rows, :] = low
        return low

    over_halves(z, step, (a_ref, b_ref))


def hidden_slope(z, at, *refs):
    blocks, (z_ref, sum_ref, hw_ref, par_ref, wcat, slope_ref) = refs[: z.S], refs[z.S :]
    for t, block in enumerate(blocks):
        s = at[1] ^ t
        for m in range(z.Z):
            for k in range(z.K):
                rows = pl.ds(pl.multiple_of(k * z.LP + s * z.IB, z.IB), z.IB)
                if z.L % LANES == 0:
                    wcat[0, rows, m * z.L : (m + 1) * z.L] = block[at[0] ^ m, k]
                else:
                    wcat[m, rows, :] = block[at[0] ^ m, k]
    mean, inv = sum_ref[0:1, :], sum_ref[1:2, :]
    gain, shift = par_ref[0:1, :], par_ref[1:2, :]

    def step(n, rows, carry):
        normed = (z_ref[rows, :] - mean) * inv
        slope_ref[rows, :] = gelu_both(image_mask(z, hw_ref[n]) * (gain * normed + shift))[1]
        return carry

    over_images(z, step)


def back_product(z, dzs, wcat):
    contract = (((1,), (1,)), ((), ()))

    def product(j):
        slices = gathered(z, dzs, j)
        if z.L % LANES == 0:
            whole = jnp.concatenate(slices, axis=1)
            return lax.dot_general(whole, wcat[0], contract, preferred_element_type=F32)
        return sum(
            lax.dot_general(v, wcat[m], contract, preferred_element_type=F32) for m, v in enumerate(slices)
        )

    return product


def back_wide(z):
    if z.L % LANES == 0:
        return near((1, z.K * z.LP, z.C), BF16)
    return near((z.Z, z.K * z.LP, z.C // z.Z), BF16)


def hidden_grad(z, at, *refs):
    dzs, refs = refs[: 2 * z.Q], refs[2 * z.Q :]
    wcat, slope_ref, z_ref, sum_ref, hw_ref, da_ref, stats_ref, y_ref = refs
    conv_into(z, back_product(z, dzs, wcat), y_ref, da_ref, -1)
    mean, inv = sum_ref[0:1, :], sum_ref[1:2, :]

    def step(n, rows, carry):
        mask = image_mask(z, hw_ref[n])
        normed = (z_ref[rows, :] - mean) * inv
        da = da_ref[rows, :] * slope_ref[rows, :]
        da_ref[rows, :] = da
        masked = mask * da
        return (
            carry[0] + jnp.sum(masked, 0, keepdims=True),
            carry[1] + jnp.sum(masked * normed, 0, keepdims=True),
        )

    zero = jnp.zeros((1, z.L), F32)
    spread(stats_ref, list(over_images(z, step, (zero, zero))))


def input_part(z, at, a_ref, b_ref, w_ref, d_ref, *refs):
    outs, moved_ref = refs[: z.Q], refs[z.Q]
    fill_moved(z, a_ref, b_ref, moved_ref)
    contract = (((1,), (1,)), ((), ()))
    for m in range(z.Q):
        rows = pl.ds(pl.multiple_of((at[0] ^ m) * z.own, z.own), z.own)
        part = lax.dot_general(moved_ref[rows, :], w_ref[...], contract, preferred_element_type=F32)
        d = d_ref[rows, :]
        own = jnp.concatenate([jnp.where(at[0] == slot, d, 0.0) for slot in range(z.Q)], axis=1)
        outs[m][...] = (part + own).astype(outs[m].dtype)


def kernel_grad(z, ordered, at, *refs):
    features, refs = refs[: z.S], refs[z.S :]
    dzs, refs = refs[: z.S + 1], refs[z.S + 1 :]
    value_ref = None
    if len(refs) > z.Q + 2:
        value_ref, refs = refs[0], refs[1:]
    outs, (moved_ref, full_ref) = refs[: z.Q], refs[z.Q :]
    contract = (((0,), (0,)), ((), ()))
    half = z.G // 2
    for t in range(z.S):
        pair = (dzs[0], dzs[1]) if t == 0 else (dzs[1 + t].at[:half], dzs[1 + t].at[half:])
        moved = moved_ref.at[t % 2]
        fill_moved(z, *pair, moved)
        part = lax.dot_general(features[t][...], moved[...], contract, preferred_element_type=F32)
        full_ref[...] = part if t == 0 else full_ref[...] + part
    for r in range(z.Q):
        row = pl.multiple_of((at[0] ^ r if ordered else r) * z.IB, z.IB)
        for k in range(z.K):
            part = full_ref[pl.ds(row, z.IB), k * z.LP : k * z.LP + z.L]
            outs[r][k * z.IB : (k + 1) * z.IB, :] = part.astype(BF16)
        if value_ref is not None:
            outs[r][z.K * z.IB :, :] = value_ref[at[0] ^ r]


def route(z, at, *refs):
    parts, refs = refs[: z.Q], refs[z.Q :]
    outs, refs = refs[: z.Z], refs[z.Z :]
    hold = refs[-1]
    for r in range(z.Q):
        hold[at[2] ^ at[0] ^ r] = parts[r][: z.K * z.IB, :]
    for m in range(z.Z):
        outs[m][...] = hold[m]
    if len(refs) == 3:
        value_ref, slots, _ = refs
        for r in range(z.Q):
            slots[at[0] ^ r] = parts[r][z.K * z.IB :, :]
        for j in range(z.Q):
            value_ref[:, j * z.L : (j + 1) * z.L] = slots[j]


def total_of(z, *refs):
    refs[-1][...] = sum(ref[...].astype(F32) for ref in refs[:-1]).astype(refs[-1].dtype)


def direction_of(grad, first, second, param, decay):
    new_first = BETA * first + (1.0 - BETA) * grad
    new_second = BETA * second + (1.0 - BETA) * grad * grad
    move = new_first / BIAS / (jnp.sqrt(new_second / BIAS) + TINY) + decay * param
    return new_first, new_second, move


def moments(z, j, *refs):
    count = len(refs) - 10
    parts, refs = refs[:count], refs[count:]
    w_ref, first_ref, second_ref, refs = *refs[:3], refs[3:]
    if j:
        g1_ref, g2_ref, at, refs = *refs[:3], refs[3:]
    else:
        other_ref, refs = refs[0], refs[3:]
    nf_ref, ns_ref, u_ref, stats_ref = refs
    total_u = jnp.zeros((1, z.L), F32)
    total_w = jnp.zeros((1, z.L), F32)
    for k in range(z.K):
        grad = sum(part[k * z.IB : (k + 1) * z.IB, :].astype(F32) for part in parts)
        w = w_ref[0, k]
        nf, ns, u = direction_of(grad, first_ref[0, k], second_ref[0, k], w, DECAY)
        nf_ref[0, k] = nf
        ns_ref[0, k] = ns
        u_ref[k] = u
        total_u = total_u + jnp.sum(u * u, 0, keepdims=True)
        total_w = total_w + jnp.sum(w * w, 0, keepdims=True)
    lane = lax.broadcasted_iota(jnp.int32, (1, z.L), 1)
    sums = jnp.zeros((1, z.L), F32) if j else other_ref[0:1, :]
    for c, v in enumerate([total_u, total_w]):
        sums = jnp.where(lane == 2 * c + j, jnp.sum(v, axis=1, keepdims=True), sums)
    if j:
        own = jnp.zeros((1, z.L), F32)
        for r, v in enumerate([g1_ref[0:1, :], g1_ref[1:2, :], g2_ref[0:1, :], g2_ref[1:2, :]]):
            own = jnp.where(at[2] == r, v, own)
        keep(stats_ref, [sums, own])
    else:
        spread(stats_ref, [sums, other_ref[1:2, :]])


def finish(z, all_ref, w_ref, u0_ref, u1_ref, np_ref, nf_ref, ns_ref, *outs):
    nw_ref, copy_ref, nnp_ref, nnf_ref, nns_ref, trust_ref = outs
    total = all_ref[0, 0:1, :]
    for k in range(1, z.R * z.Z):
        total = total + all_ref[k, 0:1, :]
    tops, bottoms = [], []
    for j in range(2):
        un = jnp.sqrt(total[:, j : j + 1])
        wn = jnp.sqrt(total[:, 2 + j : 3 + j])
        tops.append(wn)
        bottoms.append(un)
        scale = RATE * (wn / (un + TINY))
        for k in range(z.K):
            new = w_ref[j, k] - scale * (u0_ref, u1_ref)[j][k]
            nw_ref[j, k] = new
            copy_ref[j, k] = new.astype(BF16)
    for j in range(z.Q):
        for r in range(4):
            nnp_ref[r : r + 1, j * z.L : (j + 1) * z.L] = all_ref[j * z.Z + r, 1:2, : z.L]
    param = np_ref[...]
    nf, ns, move = direction_of(nnp_ref[...], nf_ref[...], ns_ref[...], param, 0.0)
    nnf_ref[...] = nf
    nns_ref[...] = ns
    pn = jnp.sqrt(jnp.sum(param * param, axis=1, keepdims=True))
    qn = jnp.sqrt(jnp.sum(move * move, axis=1, keepdims=True))
    nnp_ref[...] = param - RATE * (pn / (qn + TINY)) * move
    for r in range(4):
        tops.append(pn[r : r + 1])
        bottoms.append(qn[r : r + 1])
    at_row = lax.broadcasted_iota(jnp.int32, (2, 6), 0)
    at_col = lax.broadcasted_iota(jnp.int32, (2, 6), 1)
    trust = jnp.zeros((2, 6), F32)
    for c in range(6):
        trust = jnp.where(at_col == c, jnp.where(at_row == 0, tops[c], bottoms[c]), trust)
    trust_ref[...] = trust


def pick(z, first, at, *refs):
    parts, refs = refs[: z.Z], refs[z.Z :]
    if first:
        valid_ref, outs, hold = refs[0], refs[1:-1], refs[-1]
        rows = []
        for n in range(z.n_own):
            valid = valid_ref[n].astype(F32)
            tall = jnp.sum(valid[:, 0:1], axis=0, keepdims=True)
            wide = jnp.sum(valid[0:1, :], axis=1, keepdims=True)
            rows += [jnp.broadcast_to(tall, (1, z.L)), jnp.broadcast_to(wide, (1, z.L))]
        rows.append(jnp.zeros((z.extra - len(rows), z.L), F32))
        sizes = jnp.concatenate(rows, axis=0).astype(BF16)
    else:
        map_ref, far_ref, outs, (hold, sem) = refs[0], refs[1], refs[2:-2], refs[-2:]
    for m in range(z.Z):
        hold[at[2] ^ m] = parts[m][...]
    if not first:
        copy = pltpu.make_async_copy(hold, far_ref, sem)
        copy.start()
    for m in range(z.Q):
        for k in range(z.K):
            outs[m][k * z.IB : (k + 1) * z.IB, :] = hold[at[0] ^ m, k]
        if first:
            outs[m][z.K * z.IB :, :] = sizes
            continue
        part = map_ref[:, : z.L]
        for slot in range(1, z.Q):
            part = jnp.where((at[0] ^ m) == slot, map_ref[:, slot * z.L : (slot + 1) * z.L], part)
        outs[m][z.K * z.IB :, :] = part

    if not first:
        copy.wait()


def unpick(z, at, *refs):
    parts, (out_ref, map_ref) = refs[: z.Q], refs[z.Q :]
    for m in range(z.Q):
        q = at[0] ^ m
        for k in range(z.K):
            out_ref[q, k] = parts[m][k * z.IB : (k + 1) * z.IB, :]
        map_ref[pl.ds(pl.multiple_of(q * z.own, z.own), z.own), :] = parts[m][z.K * z.IB :, :]


def shards(z, images, masks, cotangent, weights, first, second, params, p_first, p_second):
    q, s, b = lax.axis_index("q"), lax.axis_index("s"), lax.axis_index("z")
    at = jnp.stack([q, s, b]).astype(jnp.int32)

    def over_z(v, m):
        return lax.ppermute(v, "z", [(i, i ^ m) for i in range(z.Z)]) if m else v

    def over_s(v, m):
        return lax.ppermute(v, "s", [(i, i ^ m) for i in range(z.S)]) if m else v

    def sharers(v):
        return lax.all_to_all(v, ("s", "z"), 0, 0)

    def over_q(v, m):
        return lax.ppermute(v, "q", [(i, i ^ m) for i in range(z.Q)]) if m else v

    def gather_z(w):
        return [over_z(w, m) for m in range(z.Z)]

    def gather(a, b):
        if z.Q != 4:
            return [over_q(v, m) for v in (a, b) for m in range(z.Q)]
        a1, a2, b1, b2 = over_q(a, 1), over_q(a, 2), over_q(b, 1), over_q(b, 2)
        return [a, a1, a2, over_q(a2, 1), b, b1, b2, over_q(b1, 2)]

    def share(packed):
        return [over_s(packed, t) for t in range(z.S)]

    rows = z.own
    GL = (z.G, z.L)
    HL = (z.G // 2, z.L)
    many = z.S * z.Z
    piece = (z.K, z.IB, z.L)
    blocks = near((z.Z, *piece), BF16)
    stat, pair = near((many, 4, LANES)), near((many, 2, LANES))
    conv_scratch = [pltpu.VMEM((z.C, z.K * z.LP), BF16), pltpu.VMEM((rows, z.K * z.LP), F32)]
    moved = (z.G, z.K * z.LP)
    grad_scratch = [pltpu.VMEM((2, *moved), BF16), pltpu.VMEM((z.Q * z.IB, z.K * z.LP), F32)]
    cot_rows = cotangent.reshape(rows, z.C)
    image_rows = images.reshape(rows, z.C)

    low_one, low_two = (weights[j].astype(BF16) for j in range(2))
    one = [over_z(low_one, m) for m in range(z.Z)]
    xs = [over_q(image_rows, m) for m in range(z.Q)]
    one, low_two = together((one, low_two))
    hold = pltpu.VMEM((z.Z, *piece), BF16)
    picked = call(
        functools.partial(pick, z, True),
        [near((z.K * z.IB + z.extra, z.L), BF16)] * z.Q,
        (at, *one, masks),
        [hold],
    )
    picked, xs = together((picked, xs))
    two = [over_z(low_two, m) for m in range(z.Z)]
    *x_parts, x_slice, slice_params = call(
        functools.partial(split_images, z),
        [near((z.G, z.Q * z.IB), BF16)] * z.S + [near(GL, BF16), near((4, z.L))],
        (at, params, *xs),
    )
    front_one = [over_q(picked[m], m) for m in range(z.Q)]
    front_one, x_parts, two = together((front_one, x_parts, two))
    keep = away((z.Z, *piece), BF16)
    keep_two, *picked = call(
        functools.partial(pick, z, False),
        [keep] + [near((z.K * z.IB + rows, z.L), BF16)] * z.Q,
        (at, *two, cot_rows),
        [hold, pltpu.SemaphoreType.DMA],
        raw=(keep,),
    )
    w_far = away((z.C, z.K * z.LP), BF16)
    z1, hw, stats, w_far = call(
        functools.partial(first_conv, z),
        [near(GL), near((z.n_group, 8, LANES)), stat, w_far],
        (at, *xs, *[over_s(v, t) for t in range(z.S) for v in front_one]),
        conv_scratch + [pltpu.SemaphoreType.DMA],
        limit=16,
        raw=(w_far,),
    )
    stats, picked = together((stats, picked))
    stats, picked = together((sharers(stats), [over_q(picked[m], m) for m in range(z.Q)]))
    ha, hb, sum_one, front_two, cots = call(
        functools.partial(hidden, z),
        [near(HL, BF16), near(HL, BF16), near((8, z.L)), blocks, near(GL, BF16)],
        (at, z1, stats, hw, slice_params, *picked),
    )
    hs = gather(ha, hb)
    *h_parts, z2, stats = call(
        functools.partial(second_conv, z),
        [near((z.G, z.Q * z.IB), BF16)] * z.S + [near(GL), stat],
        (at, *hs, *share(front_two), hw),
        conv_scratch,
        limit=16,
    )
    stats, x_parts, h_parts = together((stats, x_parts, h_parts))
    x_parts = [over_s(v, t) for t, v in enumerate(x_parts)]
    h_parts = [over_s(v, t) for t, v in enumerate(h_parts)]
    stats, x_parts, h_parts = together((sharers(stats), x_parts, h_parts))
    out, d, sum_two, stats = call(
        functools.partial(middle, z),
        [near((z.Q, rows, z.L), BF16), near(GL), near((8, z.L)), pair],
        (at, z2, stats, hw, slice_params, x_slice, cots),
    )
    da, db, dz, grad_two = call(
        functools.partial(norm_grad, z, 2),
        [near(HL, BF16), near(HL, BF16), near(GL, BF16), near((8, z.L))],
        (z2, d, sum_two, sharers(stats), hw, slice_params),
    )
    da, db, keep_two = together((da, db, keep_two))
    dz2s = gather(da, db)

    def gradient(features, a, b, whole, *value):
        more = rows if value else 0
        return call(
            functools.partial(kernel_grad, z, not value),
            [near((z.K * z.IB + more, z.L), BF16)] * z.Q,
            (at, *features, a, b, *[over_s(whole, t) for t in range(1, z.S)], *value),
            grad_scratch,
            limit=18,
            cost=COST_GRAD,
        )

    def by_plane(parts):
        return [over_q(parts[r], r) for r in range(z.Q)]

    def along(parts):
        return [over_z(parts[m], m) for m in range(z.Z)]

    def update(j, parts, *more):
        whole = pl.BlockSpec(memory_space=pltpu.VMEM)
        block = pl.BlockSpec((1, *piece), lambda i: (j, 0, 0, 0))
        held = pl.BlockSpec(memory_space=pl.ANY)
        args = [pltpu.with_memory_space_constraint(v, pltpu.VMEM) for v in parts] + [weights, first, second]
        specs = [whole] * len(parts) + [block] * 3
        if j:
            args += [pltpu.with_memory_space_constraint(v, pltpu.VMEM) for v in more] + [at]
            specs += [whole] * 2 + [pl.BlockSpec(memory_space=pltpu.SMEM)]
        else:
            args += [pltpu.with_memory_space_constraint(more[0], pltpu.VMEM), *more[1:]]
            specs += [whole] + [held] * 2
        n = len(args)
        return pl.pallas_call(
            functools.partial(moments, z, j),
            grid=(1,),
            out_shape=[shape(weights.shape)] * 2
            + [near(piece), near((8, z.L)) if j else near((z.R * z.Z, 2, LANES))],
            in_specs=specs,
            out_specs=[block, block, whole, whole],
            input_output_aliases={} if j else {n - 2: 0, n - 1: 1},
            compiler_params=pltpu.CompilerParams(vmem_limit_bytes=8 * 1024 * 1024),
            cost_estimate=pl.CostEstimate(flops=1 if j else COST_GRAD, bytes_accessed=1, transcendentals=0),
        )(*args)

    parts_two = gradient(h_parts, da, db, dz, out)
    wide, slope = call(
        functools.partial(hidden_slope, z),
        [back_wide(z), near(GL)],
        (at, *share(keep_two), z1, sum_one, hw, slice_params),
    )
    da1, stats = call(
        functools.partial(hidden_grad, z),
        [near(GL), pair],
        (at, *dz2s, wide, slope, z1, sum_one, hw),
        [pltpu.VMEM((rows, z.K * z.LP), F32)],
        limit=16,
    )
    stats, parts_two = together((stats, parts_two))
    stats, parts_two = together((sharers(stats), by_plane(parts_two)))
    da, db, dz, grad_one = call(
        functools.partial(norm_grad, z, 0),
        [near(HL, BF16), near(HL, BF16), near(GL, BF16), near((8, z.L))],
        (z1, da1, sum_one, stats, hw, slice_params),
    )
    flat = near((z.K * z.IB, z.L), BF16)
    hold = pltpu.VMEM((z.Z, z.K * z.IB, z.L), BF16)
    *parts_two, values = call(
        functools.partial(route, z),
        [flat] * z.Z + [near((rows, z.C), BF16)],
        (at, *parts_two),
        [pltpu.VMEM((z.Q, rows, z.L), BF16), hold],
        after=(da,),
    )
    parts_one = gradient(x_parts, da, db, dz)
    parts_one, parts_two[3] = together((parts_one, parts_two[3]))
    parts_one, parts_two = by_plane(parts_one), along(parts_two)
    parts_one, parts_two = together((parts_one, parts_two))
    dxs = call(
        functools.partial(input_part, z),
        [near((rows, z.C))] + [near((rows, z.C), BF16)] * (z.Q - 1),
        (at, da, db, w_far, d),
        [pltpu.VMEM(moved, BF16)],
        limit=16,
        cost=COST_GRAD,
        far=(w_far,),
        after=(parts_one[0],),
    )
    parts_one = call(functools.partial(route, z), [flat] * z.Z, (at, *parts_one), [hold])
    parts_one, parts_two = together((parts_one, parts_two))
    parts_one = along(parts_one)
    new_first, new_second, move_two, other = update(1, parts_two, grad_one, grad_two)
    dxs = [over_q(dxs[m], m) for m in range(z.Q)]
    new_first, new_second, move_one, stats = update(0, parts_one, other, new_first, new_second)
    stats = lax.all_to_all(stats, ("s", "q", "z"), 0, 0)
    dx = call(functools.partial(total_of, z), shape((rows, z.C), BF16), tuple(dxs))
    stats, dx = together((stats, dx))
    new_weights, copies, new_params, new_p_first, new_p_second, trust = call(
        functools.partial(finish, z),
        [shape(weights.shape), shape(weights.shape, BF16)] + [shape(params.shape)] * 3 + [shape((2, 6))],
        (stats, weights, move_one, move_two, params, p_first, p_second),
    )
    return (
        values.reshape(images.shape),
        dx.reshape(images.shape),
        new_weights,
        copies,
        new_first,
        new_second,
        new_params,
        new_p_first,
        new_p_second,
        trust,
    )


def solution(mesh):
    def whole(images, masks, cotangent, weights, first, second, params, p_first, p_second):
        z = Sizes(mesh, images.shape, weights.shape)
        inner = Mesh(mesh.devices.reshape(z.Q, z.S, z.Z), ("q", "s", "z"))
        pixels = P(("q", "s", "z"), None, None, None)
        kernels = P(None, None, ("q", "s"), "z")
        return jax.shard_map(
            functools.partial(shards, z),
            mesh=inner,
            in_specs=(pixels, P(("q", "s", "z"), None, None), pixels, kernels, kernels, kernels, P(), P(), P()),
            out_specs=(pixels, pixels, kernels, kernels, kernels, kernels, P(), P(), P(), P()),
            check_vma=False,
        )(images, masks, cotangent, weights, first, second, params, p_first, p_second)

    return whole
```
